256 devices in a mesh: dp: 8 (over x, core), point: 32 (over z, y).
Axes of the slice: x: 4, y: 4, z: 8, core: 2. Of those that a mesh axis runs over, the one named last changes fastest.
Arguments:
- material_points: bfloat16 [8, 16384, 256], P('dp', 'point'), may hold values from -16 to 16
- loss_sensitivity: bfloat16 [8, 16384, 256], P('dp', 'point'), may hold values from -6 to 6
- averaged_quantity_linear: bfloat16 [256, 256], replicated, may hold values from -0.375 to 0.375
- partition_choosing_linear: bfloat16 [256, 256], replicated, may hold values from -0.375 to 0.375
- partition_assigning_linear: bfloat16 [32, 64], replicated, may hold values from -2 to 2
- summary_point_linears: bfloat16 [32, 96], replicated, may hold values from -2 to 2
- closing_linear_map: bfloat16 [256, 256], replicated, may hold values from -0.375 to 0.375
- expanding_linear_map: bfloat16 [256, 1024], replicated, may hold values from -0.375 to 0.375
- contracting_linear_map: bfloat16 [1024, 256], replicated, may hold values from -0.1875 to 0.1875
- softmax_sharpness: float32 [8], replicated, may hold values from 0.5 to 2
Outputs:
- updated: bfloat16 [8, 16384, 256], P('dp', 'point')
- particle_grad: bfloat16 [8, 16384, 256], P('dp', 'point')
- feature_grad: float32 [256, 256], replicated
- project_grad: float32 [256, 256], replicated
- slice_grad: float32 [32, 64], replicated
- token_grad: float32 [32, 96], replicated
- output_grad: float32 [256, 256], replicated
- up_grad: float32 [256, 1024], replicated
- down_grad: float32 [1024, 256], replicated
The draws below stay inside these ranges and needn't reach their ends.
All inputs are finite; a program needn't handle non-finite values.
Results may differ from the reference program's by a relative error of at most 0.03.
Values sent between devices are 32-bit elements; how exact they have to be, the bound alone decides.
A program may use at most 64 MiB of HBM per device.

```python
import math
import jax
import jax.numpy as jnp
from jax import lax

C = 256
CHANNEL_GROUPS = 8
SLICES = 64
FF = 1024
HEAD_DIM = 32
POINTS_DEV = 512
TOKENS = 16384
SNAPS = 8


def draw_material_points(key, part):
    key = jax.random.fold_in(key, 7)
    direction_key, noise_key = jax.random.split(key)
    blocks = TOKENS // POINTS_DEV
    position_ramp = jnp.arange(blocks, dtype=jnp.float32) / max(blocks - 1, 1)
    directions = jax.random.normal(direction_key, (SNAPS, blocks, 1, C), jnp.float32)
    amplitude = 1.0 + 2.0 * position_ramp
    noise_rows = jax.random.normal(noise_key, (SNAPS, blocks, POINTS_DEV, C), jnp.float32)
    values = amplitude[None, :, None, None] * directions + noise_rows
    return jnp.clip(values, -16.0, 16.0).reshape(SNAPS, TOKENS, C).astype(jnp.bfloat16)


def block_scale(own_key, shape, cuts, least, high):
    loudness = 1.0
    for axis_at, parts in cuts:
        steps = jax.random.uniform(jax.random.fold_in(jax.random.fold_in(own_key, 6), axis_at), (parts,), jnp.float32, least / len(cuts), high / len(cuts))
        loudness = loudness * jnp.repeat(jnp.exp(steps), shape[axis_at] // parts).reshape((-1,) + (1,) * (len(shape) - 1 - axis_at))
    return loudness


def centred(rng, shape, scale, bound, shards=(), held_as=jnp.bfloat16):
    loudness = block_scale(rng, shape, shards, -0.22, 0.18) if shards else 1.0
    drawn = jax.random.normal(rng, shape, jnp.float32) * scale * loudness
    return jnp.minimum(jnp.maximum(drawn, -bound), bound).astype(held_as)


def setup_inputs(seed: int = 0) -> dict:
    seeds = jax.random.split(jax.random.key(seed), 11)
    return {
        "material_points": draw_material_points(jax.random.fold_in(seeds[10], 71), 0),
        "loss_sensitivity": centred(seeds[1], (SNAPS, TOKENS, C), 1.0, 6.0, ((0, 8), (1, 32))),
        "averaged_quantity_linear": centred(seeds[2], (C, C), C ** -0.5, 0.375),
        "partition_choosing_linear": centred(seeds[3], (C, C), C ** -0.5, 0.375),
        "partition_assigning_linear": centred(seeds[4], (HEAD_DIM, SLICES), 8 ** -0.5, 2.0),
        "summary_point_linears": centred(seeds[5], (HEAD_DIM, 3 * HEAD_DIM), 8 ** -0.5, 2.0),
        "closing_linear_map": centred(seeds[6], (C, C), C ** -0.5, 0.375),
        "expanding_linear_map": centred(seeds[7], (C, FF), C ** -0.5, 0.375),
        "contracting_linear_map": centred(seeds[8], (FF, C), FF ** -0.5, 0.1875),
        "softmax_sharpness": jnp.clip(jnp.exp(jax.random.uniform(seeds[9], (CHANNEL_GROUPS,), jnp.float32, math.log(0.5), math.log(2.0))), 0.5, 2.0),
    }


eps_norm = 1e-05
eps_mass = 1e-05
gelu_coef = 0.7978845608028654

def normalize(values):
    values = values.astype(jnp.float32)
    center = values - lax.optimization_barrier(jnp.mean(values, axis=-1, keepdims=True))
    inverse = lax.rsqrt(lax.optimization_barrier(jnp.mean(center * center, axis=-1, keepdims=True)) + eps_norm)
    return (center * inverse, inverse)

def normalize_back(normed, inverse, incoming):
    mean_grad = lax.optimization_barrier(jnp.mean(incoming, axis=-1, keepdims=True))
    mean_proj = lax.optimization_barrier(jnp.mean(incoming * normed, axis=-1, keepdims=True))
    return inverse * (incoming - mean_grad - normed * mean_proj)

def gelu_pair(hidden):
    inner = gelu_coef * (hidden + 0.044715 * hidden * hidden * hidden)
    tangent = jnp.tanh(inner)
    activated = 0.5 * hidden * (1.0 + tangent)
    gelu_slope = 0.5 * (1.0 + tangent) + 0.5 * hidden * (1.0 - tangent * tangent) * gelu_coef * (1.0 + 3.0 * 0.044715 * hidden * hidden)
    return (activated, gelu_slope)

def token_mix(slice_feature_totals, slice_mass, token_single_float):
    per_head_width = slice_feature_totals.shape[2]
    slice_tokens = slice_feature_totals / (slice_mass + eps_mass)[:, :, None]
    projection_rows = jnp.einsum('wzg,gl->wzl', slice_tokens, token_single_float, precision=lax.Precision.HIGHEST)
    slice_query_rows = projection_rows[:, :, :per_head_width]
    slice_key_rows = projection_rows[:, :, per_head_width:2 * per_head_width]
    slice_value_rows = projection_rows[:, :, 2 * per_head_width:]
    attention_scores = jnp.einsum('vts,vzs->vtz', slice_query_rows, slice_key_rows, precision=lax.Precision.HIGHEST) * per_head_width ** (-0.5)
    exponent = jnp.exp(attention_scores)
    attention_result = exponent / lax.optimization_barrier(jnp.sum(exponent, axis=-1, keepdims=True))
    return jnp.einsum('yew,ywa->yea', attention_result, slice_value_rows, precision=lax.Precision.HIGHEST)

def material_snapshot_layout(entering_material_entries, sensitivity_entering_entries, averaged_quantity_linear, partition_choosing_linear, partition_assigning_linear, summary_point_linears, closing_linear_map, expanding_linear_map, contracting_linear_map, softmax_sharpness):
    particle_row_count = entering_material_entries.shape[0]
    hidden_model_width = entering_material_entries.shape[1]
    per_head_width = partition_assigning_linear.shape[0]
    head_count = hidden_model_width // per_head_width
    thirty_two_bit_kind = jnp.float32
    bfloat_sixteen_kind = jnp.bfloat16
    normed, inverse = normalize(entering_material_entries)
    normed_half = normed.astype(bfloat_sixteen_kind)
    features = jnp.dot(normed_half, averaged_quantity_linear, preferred_element_type=thirty_two_bit_kind).astype(bfloat_sixteen_kind)
    projection_rows = jnp.dot(normed_half, partition_choosing_linear, preferred_element_type=thirty_two_bit_kind).astype(bfloat_sixteen_kind)
    feature_per_head = features.reshape(particle_row_count, head_count, per_head_width)
    linear_image_each_group = projection_rows.reshape(particle_row_count, head_count, per_head_width)
    partition_energy_entries = jnp.einsum('gnj,jv->gnv', linear_image_each_group.astype(thirty_two_bit_kind), partition_assigning_linear.astype(thirty_two_bit_kind)) / softmax_sharpness[None, :, None]
    exponent = jnp.exp(partition_energy_entries)
    partition_membership_share = exponent / lax.optimization_barrier(jnp.sum(exponent, axis=-1, keepdims=True))
    slice_probability_low = partition_membership_share.astype(bfloat_sixteen_kind)
    slice_feature_totals = jnp.einsum('cts,ctl->tsl', slice_probability_low.astype(thirty_two_bit_kind), feature_per_head.astype(thirty_two_bit_kind))
    slice_mass = lax.optimization_barrier(jnp.sum(partition_membership_share, axis=0))
    mixed, pullback = jax.vjp(token_mix, slice_feature_totals, slice_mass, summary_point_linears.astype(thirty_two_bit_kind))
    token_blend_low = mixed.astype(bfloat_sixteen_kind)
    broadcast_rows = jnp.einsum('wov,ovc->woc', slice_probability_low.astype(thirty_two_bit_kind), token_blend_low.astype(thirty_two_bit_kind)).astype(bfloat_sixteen_kind).reshape(particle_row_count, hidden_model_width)
    residual = (entering_material_entries.astype(thirty_two_bit_kind) + jnp.dot(broadcast_rows, closing_linear_map, preferred_element_type=thirty_two_bit_kind)).astype(bfloat_sixteen_kind)
    normed2, inverse2 = normalize(residual)
    normed2_half = normed2.astype(bfloat_sixteen_kind)
    hidden = jnp.dot(normed2_half, expanding_linear_map, preferred_element_type=thirty_two_bit_kind)
    activated, gelu_slope = gelu_pair(hidden)
    activated_half = activated.astype(bfloat_sixteen_kind)
    updated = (residual.astype(thirty_two_bit_kind) + jnp.dot(activated_half, contracting_linear_map, preferred_element_type=thirty_two_bit_kind)).astype(bfloat_sixteen_kind)
    grad_hidden = (jnp.dot(sensitivity_entering_entries, contracting_linear_map.T, preferred_element_type=thirty_two_bit_kind) * gelu_slope).astype(bfloat_sixteen_kind)
    grad_normed2 = jnp.dot(grad_hidden, expanding_linear_map.T, preferred_element_type=thirty_two_bit_kind)
    grad_residual = sensitivity_entering_entries.astype(thirty_two_bit_kind) + normalize_back(normed2, inverse2, grad_normed2)
    grad_residual_half = grad_residual.astype(bfloat_sixteen_kind)
    grad_spread = jnp.dot(grad_residual_half, closing_linear_map.T, preferred_element_type=thirty_two_bit_kind).astype(bfloat_sixteen_kind)
    broadcast_per_head = grad_spread.reshape(particle_row_count, head_count, per_head_width)
    gradient_token_blend = jnp.einsum('cts,ctl->tsl', slice_probability_low.astype(thirty_two_bit_kind), broadcast_per_head.astype(thirty_two_bit_kind))
    grad_sums, gradient_slice_weight_total, grad_tokenmap = pullback(gradient_token_blend)
    gradient_totals_low = grad_sums.astype(bfloat_sixteen_kind)
    sensitivity_assignment_share = jnp.einsum('wgv,gzv->wgz', broadcast_per_head.astype(thirty_two_bit_kind), token_blend_low.astype(thirty_two_bit_kind))
    sensitivity_assignment_share = sensitivity_assignment_share + jnp.einsum('wgv,gzv->wgz', feature_per_head.astype(thirty_two_bit_kind), gradient_totals_low.astype(thirty_two_bit_kind)) + gradient_slice_weight_total[None]
    gradient_feature_rows = jnp.einsum('wov,ovc->woc', slice_probability_low.astype(thirty_two_bit_kind), gradient_totals_low.astype(thirty_two_bit_kind)).astype(bfloat_sixteen_kind).reshape(particle_row_count, hidden_model_width)
    sensitivity_partition_energies = (partition_membership_share * (sensitivity_assignment_share - lax.optimization_barrier(jnp.sum(partition_membership_share * sensitivity_assignment_share, axis=-1, keepdims=True))) / softmax_sharpness[None, :, None]).astype(bfloat_sixteen_kind)
    grad_projected = jnp.einsum('rhm,dm->rhd', sensitivity_partition_energies.astype(thirty_two_bit_kind), partition_assigning_linear.astype(thirty_two_bit_kind)).astype(bfloat_sixteen_kind).reshape(particle_row_count, hidden_model_width)
    grad_normed = jnp.dot(gradient_feature_rows, averaged_quantity_linear.T, preferred_element_type=thirty_two_bit_kind) + jnp.dot(grad_projected, partition_choosing_linear.T, preferred_element_type=thirty_two_bit_kind)
    particle_grad = (grad_residual + normalize_back(normed, inverse, grad_normed)).astype(bfloat_sixteen_kind)
    feature_grad = jnp.dot(normed_half.T, gradient_feature_rows, preferred_element_type=thirty_two_bit_kind)
    project_grad = jnp.dot(normed_half.T, grad_projected, preferred_element_type=thirty_two_bit_kind)
    slice_grad = jnp.einsum('rhd,rhm->dm', linear_image_each_group.astype(thirty_two_bit_kind), sensitivity_partition_energies.astype(thirty_two_bit_kind))
    output_grad = jnp.dot(broadcast_rows.T, grad_residual_half, preferred_element_type=thirty_two_bit_kind)
    up_grad = jnp.dot(normed2_half.T, grad_hidden, preferred_element_type=thirty_two_bit_kind)
    down_grad = jnp.dot(activated_half.T, sensitivity_entering_entries, preferred_element_type=thirty_two_bit_kind)
    return (updated, particle_grad, (feature_grad, project_grad, slice_grad, grad_tokenmap, output_grad, up_grad, down_grad))

def reference(material_points, loss_sensitivity, averaged_quantity_linear, partition_choosing_linear, partition_assigning_linear, summary_point_linears, closing_linear_map, expanding_linear_map, contracting_linear_map, softmax_sharpness):

    def one_snapshot(loss_and_sensitivity_pair):
        return material_snapshot_layout(loss_and_sensitivity_pair[0], loss_and_sensitivity_pair[1], averaged_quantity_linear, partition_choosing_linear, partition_assigning_linear, summary_point_linears, closing_linear_map, expanding_linear_map, contracting_linear_map, softmax_sharpness)
    updated, particle_grad, grads_all = lax.map(one_snapshot, (material_points, loss_sensitivity))
    grad_scale = (SNAPS * TOKENS) ** (-0.5)
    totals = [lax.optimization_barrier(jnp.sum(item, axis=0)) * grad_scale for item in grads_all]
    return (updated, particle_grad, totals[0], totals[1], totals[2], totals[3], totals[4], totals[5], totals[6])
```

```python
import functools

import jax
import jax.numpy as jnp
from jax import lax
from jax.experimental import pallas as pl
from jax.experimental.pallas import tpu as pltpu
from jax.sharding import PartitionSpec as P

F32 = jnp.float32
BF16 = jnp.bfloat16
MESH = pl.DeviceIdType.MESH
EPS = 1e-05
GELU = 0.7978845608028654
HIGH = lax.Precision.HIGHEST

NX, NC, NZ, NY = 4, 2, 8, 4
ROWS = 512
C, FF, HEADS, HD, SL = 256, 1024, 8, 32, 64
PAIRS = 4
KXY = NX * NY
EROWS = 72
LROWS = 17
CH = 128


def dot(a, b):
    return jnp.dot(a, b, preferred_element_type=F32)


def dot_t(a, b):
    return lax.dot_general(a, b, (((1,), (1,)), ((), ())), preferred_element_type=F32)


def tdot(a, b):
    return lax.dot_general(a, b, (((0,), (0,)), ((), ())), preferred_element_type=F32)


def hdot(a, b, dims):
    return lax.dot_general(
        a, b, ((dims[:1], dims[1:]), ((), ())), precision=HIGH, preferred_element_type=F32
    )


def norm_rows(v):
    center = v - jnp.mean(v, axis=-1, keepdims=True)
    inv = lax.rsqrt(jnp.mean(center * center, axis=-1, keepdims=True) + EPS)
    return center * inv, inv


def norm_back(normed, inv, g):
    return inv * (
        g - jnp.mean(g, axis=-1, keepdims=True) - normed * jnp.mean(g * normed, axis=-1, keepdims=True)
    )


def seg_sum(v, ones):
    hi = v.astype(BF16)
    lo = (v - hi.astype(F32)).astype(BF16)
    return jnp.concatenate(
        [
            dot(hi[:, 256 * g : 256 * g + 256], ones) + dot(lo[:, 256 * g : 256 * g + 256], ones)
            for g in range(2)
        ],
        axis=1,
    )


def each(n, f):
    def step(i, carry):
        f(i)
        return carry

    lax.fori_loop(0, n, step, 0)


def remote(src, dst, ss, rs, dev):
    return pltpu.make_async_remote_copy(
        src_ref=src, dst_ref=dst, send_sem=ss, recv_sem=rs, device_id=dev, device_id_type=MESH
    )


SCRATCH = dict(
    mp=pltpu.VMEM((ROWS, C), BF16),
    ls=pltpu.VMEM((ROWS, C), BF16),
    wa=pltpu.VMEM((C, C), BF16),
    wp=pltpu.VMEM((C, C), BF16),
    ws=pltpu.VMEM((HD, SL), BF16),
    wt=pltpu.VMEM((HD, 3 * HD), BF16),
    wc=pltpu.VMEM((C, C), BF16),
    we=pltpu.VMEM((C, FF), BF16),
    wd=pltpu.VMEM((FF, C), BF16),
    in_sem=pltpu.SemaphoreType.DMA((9,)),
    nh=pltpu.VMEM((ROWS, C), BF16),
    feat=pltpu.VMEM((ROWS, C), BF16),
    proj=pltpu.VMEM((ROWS, C), BF16),
    asg=pltpu.VMEM((ROWS, 512), F32),
    ah=pltpu.VMEM((ROWS, 512), BF16),
    bdw=pltpu.VMEM((C, 512), BF16),
    bdm=pltpu.VMEM((C, 512), BF16),
    bdg=pltpu.VMEM((C, 512), BF16),
    ones=pltpu.VMEM((256, 256), BF16),
    spread=pltpu.VMEM((ROWS, C), BF16),
    n2h=pltpu.VMEM((ROWS, C), BF16),
    act=pltpu.VMEM((ROWS, FF), BF16),
    gh=pltpu.VMEM((ROWS, FF), BF16),
    gres=pltpu.VMEM((ROWS, C), F32),
    grh=pltpu.VMEM((ROWS, C), BF16),
    gspr=pltpu.VMEM((ROWS, C), BF16),
    ga=pltpu.VMEM((ROWS, 512), F32),
    gl=pltpu.VMEM((ROWS, 512), BF16),
    gf=pltpu.VMEM((ROWS, C), BF16),
    gp=pltpu.VMEM((ROWS, C), BF16),
    upd=pltpu.VMEM((ROWS, C), BF16),
    pgr=pltpu.VMEM((ROWS, C), BF16),
    a_p=pltpu.VMEM((PAIRS, 40, 128), F32),
    a_y=pltpu.VMEM((3, 40, 128), F32),
    a_z=pltpu.VMEM((NZ, 40, 128), F32),
    a_m=pltpu.VMEM((PAIRS, HD, 128), F32),
    a_ys=pltpu.SemaphoreType.DMA((2, 3)),
    a_zs=pltpu.SemaphoreType.DMA((2, 7)),
    a_ms=pltpu.SemaphoreType.DMA((2, 3)),
    b_p=pltpu.VMEM((PAIRS, HD, 128), F32),
    b_y=pltpu.VMEM((3, HD, 128), F32),
    b_z=pltpu.VMEM((NZ, HD, 128), F32),
    b_m=pltpu.VMEM((PAIRS, 40, 128), F32),
    b_ys=pltpu.SemaphoreType.DMA((2, 3)),
    b_zs=pltpu.SemaphoreType.DMA((2, 7)),
    b_ms=pltpu.SemaphoreType.DMA((2, 3)),
    e_all=pltpu.VMEM((2 * KXY, EROWS, C), F32),
    e_core=pltpu.VMEM((KXY, EROWS, C), F32),
    e_xy=pltpu.VMEM((KXY - 1, EROWS, C), F32),
    e_part=pltpu.VMEM((EROWS, C), F32),
    e_z=pltpu.VMEM((NZ, 8, C), F32),
    e_zo=pltpu.VMEM((NZ, 8, C), F32),
    e_fin=pltpu.VMEM((2 * KXY, EROWS, C), F32),
    e_cs=pltpu.SemaphoreType.DMA((2,)),
    e_xys=pltpu.SemaphoreType.DMA((2, KXY - 1)),
    e_zs=pltpu.SemaphoreType.DMA((2, 7)),
    e_zos=pltpu.SemaphoreType.DMA((2, 7)),
    e_zgs=pltpu.SemaphoreType.DMA((2, 7)),
    e_xygs=pltpu.SemaphoreType.DMA((2, KXY - 1)),
    e_cgs=pltpu.SemaphoreType.DMA((2,)),
    l_all=pltpu.VMEM((2 * KXY, LROWS, C), F32),
    l_core=pltpu.VMEM((KXY, LROWS, C), F32),
    l_xy=pltpu.VMEM((KXY - 1, LROWS, C), F32),
    l_z=pltpu.VMEM((NZ, LROWS, C), F32),
    l_fin=pltpu.VMEM((2 * KXY, LROWS, C), F32),
    l_cs=pltpu.SemaphoreType.DMA((2,)),
    l_xys=pltpu.SemaphoreType.DMA((2, KXY - 1)),
    l_zs=pltpu.SemaphoreType.DMA((2, 7)),
    l_xygs=pltpu.SemaphoreType.DMA((2, KXY - 1)),
    l_cgs=pltpu.SemaphoreType.DMA((2,)),
    out_sem=pltpu.SemaphoreType.DMA((10,)),
)


class Names:
    pass


def kernel(scale, *refs):
    ins, rest = refs[:10], refs[10:]
    (o_upd, o_pg, o_feat, o_proj, o_slice, o_tok, o_out, o_up, o_down) = rest[:9]
    s = Names()
    for name, ref in zip(SCRATCH, rest[9:]):
        setattr(s, name, ref)

    dp, pt = lax.axis_index("dp"), lax.axis_index("point")
    x, c = dp // NC, dp % NC
    z, y = pt // NY, pt % NY
    k = x * NY + y
    own = c * KXY + k
    other = (x * NC + (1 - c), pt)

    def at_y(i):
        return lax.rem(y + i + 1, NY)

    def from_y(i):
        return lax.rem(y + NY - 1 - i, NY)

    def at_z(i):
        return lax.rem(z + i + 1, NZ)

    def from_z(i):
        return lax.rem(z + NZ - 1 - i, NZ)

    def at_xy(i):
        j = i + 1
        return lax.rem(x + j // NY, NX), lax.rem(y + j % NY, NY)

    def from_xy(i):
        j = i + 1
        return lax.rem(x + NX - j // NY, NX), lax.rem(y + NY - j % NY, NY)

    def dev_y(yy):
        return (dp, z * NY + yy)

    def dev_z(zz):
        return (dp, zz * NY + y)

    def dev_xy(xx, yy):
        return (xx * NC + c, z * NY + yy)

    barrier = pltpu.get_barrier_semaphore()
    pl.semaphore_signal(barrier, inc=1, device_id=other, device_id_type=MESH)
    each(
        KXY - 1,
        lambda i: pl.semaphore_signal(
            barrier, inc=1, device_id=dev_xy(*at_xy(i)), device_id_type=MESH
        ),
    )
    each(
        NZ - 1,
        lambda i: pl.semaphore_signal(barrier, inc=1, device_id=dev_z(at_z(i)), device_id_type=MESH),
    )

    in_dst = (s.mp, s.ls, s.wa, s.wp, s.ws, s.wt, s.wc, s.we, s.wd)
    loads = [pltpu.make_async_copy(a, b, s.in_sem.at[i]) for i, (a, b) in enumerate(zip(ins, in_dst))]
    order = (0, 2, 3, 4, 5, 1, 6, 7, 8)
    for i in order:
        loads[i].start()
    sharp_ref = ins[9]

    lane = lax.broadcasted_iota(jnp.int32, (1, 512), 1)
    sharp = jnp.full((1, 512), sharp_ref[0], F32)
    for h in range(1, HEADS):
        sharp = jnp.where(lane // SL == h, sharp_ref[h], sharp)
    inv_sharp = 1.0 / sharp
    rr = lax.broadcasted_iota(jnp.int32, (256, 256), 0)
    cc = lax.broadcasted_iota(jnp.int32, (256, 256), 1)
    s.ones[...] = jnp.where(rr // SL == cc // SL, 1.0, 0.0).astype(BF16)
    s.bdm[...] = jnp.zeros_like(s.bdm)
    s.bdg[...] = jnp.zeros_like(s.bdg)
    low = lax.broadcasted_iota(jnp.int32, (HD, 128), 1) < SL

    def pack_diag(t):
        return jnp.where(low, t[:HD], t[HD:])

    def spread_diag(v):
        return jnp.concatenate([jnp.where(low, v, 0.0), jnp.where(low, 0.0, v)], axis=0).astype(BF16)

    loads[4].wait()
    w1 = s.ws[...].astype(F32)
    w2 = jnp.concatenate([w1, w1], axis=1)
    s.bdw[...] = jnp.zeros_like(s.bdw)
    for j in range(PAIRS):
        s.bdw[64 * j : 64 * j + 64, 128 * j : 128 * j + 128] = spread_diag(w2)

    for i in (0, 2, 3):
        loads[i].wait()
    mass = jnp.zeros((1, 512), F32)
    for r in range(0, ROWS, CH):
        rows = slice(r, r + CH)
        normed, _ = norm_rows(s.mp[rows, :].astype(F32))
        nh = normed.astype(BF16)
        s.nh[rows, :] = nh
        s.feat[rows, :] = dot(nh, s.wa[...]).astype(BF16)
        proj = dot(nh, s.wp[...]).astype(BF16)
        s.proj[rows, :] = proj
        logits = (
            jnp.concatenate(
                [
                    dot(
                        proj[:, 128 * g : 128 * g + 128],
                        s.bdw[128 * g : 128 * g + 128, 256 * g : 256 * g + 256],
                    )
                    for g in range(2)
                ],
                axis=1,
            )
            * inv_sharp
        )
        e = jnp.exp(logits)
        a = e / seg_sum(e, s.ones[...])
        s.asg[rows, :] = a
        s.ah[rows, :] = a.astype(BF16)
        mass = mass + jnp.sum(a, axis=0, keepdims=True)

    def head_sums(values, out):
        for g in range(2):
            t = tdot(values[:, 128 * g : 128 * g + 128], s.ah[:, 256 * g : 256 * g + 256])
            for j in range(2):
                out[2 * g + j, 0:HD, :] = pack_diag(
                    t[64 * j : 64 * j + 64, 128 * j : 128 * j + 128]
                )

    head_sums(s.feat, s.a_p)
    for j in range(PAIRS):
        s.a_p[j, HD:, :] = jnp.broadcast_to(mass[:, 128 * j : 128 * j + 128], (8, 128))

    def reduce_pairs(part, buf_y, buf_z, sem_y, sem_z):
        def put_y(i):
            t = at_y(i)
            return remote(part.at[t], buf_y.at[i], sem_y.at[0, i], sem_y.at[1, i], dev_y(t))

        def put_z(i):
            return remote(
                buf_z.at[z], buf_z.at[z], sem_z.at[0, i], sem_z.at[1, i], dev_z(at_z(i))
            )

        def got_z(i):
            f = from_z(i)
            return remote(buf_z.at[f], buf_z.at[f], sem_z.at[0, i], sem_z.at[1, i], dev_z(f))

        def start():
            each(NY - 1, lambda i: put_y(i).start())

        def middle():
            each(NY - 1, lambda i: put_y(i).wait_recv())
            buf_z[z] = part[y] + buf_y[0] + buf_y[1] + buf_y[2]
            each(NZ - 1, lambda i: put_z(i).start())

        def finish():
            each(NZ - 1, lambda i: got_z(i).wait_recv())
            total = buf_z[0]
            for i in range(1, NZ):
                total = total + buf_z[i]
            return total

        def drain():
            each(NY - 1, lambda i: put_y(i).wait_send())
            each(NZ - 1, lambda i: put_z(i).wait_send())

        return start, middle, finish, drain

    def gather_pairs(buf, sem):
        def put(i):
            return remote(buf.at[y], buf.at[y], sem.at[0, i], sem.at[1, i], dev_y(at_y(i)))

        def got(i):
            f = from_y(i)
            return remote(buf.at[f], buf.at[f], sem.at[0, i], sem.at[1, i], dev_y(f))

        def start():
            each(NY - 1, lambda i: put(i).start())

        def wait():
            each(NY - 1, lambda i: got(i).wait_recv())

        def drain():
            each(NY - 1, lambda i: put(i).wait_send())

        return start, wait, drain

    pl.semaphore_wait(barrier, 1 + (KXY - 1) + (NZ - 1))
    a_start, a_middle, a_finish, a_drain = reduce_pairs(s.a_p, s.a_y, s.a_z, s.a_ys, s.a_zs)
    am_start, am_wait, am_drain = gather_pairs(s.a_m, s.a_ms)
    a_start()
    a_middle()
    for i in (5, 1, 6, 7, 8):
        loads[i].wait()
    total = a_finish()

    wt = s.wt[...].astype(F32)
    inv_mass = 1.0 / (total[HD : HD + 1] + EPS)
    tokens = total[:HD] * inv_mass
    qkv = hdot(wt, tokens, (0, 0))
    q, kk, v = qkv[:HD], qkv[HD : 2 * HD], qkv[2 * HD :]
    r2 = lax.broadcasted_iota(jnp.int32, (128, 128), 0) // SL
    c2 = lax.broadcasted_iota(jnp.int32, (128, 128), 1) // SL
    scores = hdot(q, kk, (0, 0)) * HD ** (-0.5)
    expo = jnp.where(r2 == c2, jnp.exp(jnp.where(r2 == c2, scores, 0.0)), 0.0)
    att = expo / jnp.sum(expo, axis=-1, keepdims=True)
    s.a_m[y] = hdot(v, att, (1, 1))
    am_start()
    am_wait()
    for j in range(PAIRS):
        s.bdm[64 * j : 64 * j + 64, 128 * j : 128 * j + 128] = spread_diag(s.a_m[j])

    for r in range(0, ROWS, CH):
        rows = slice(r, r + CH)
        spread = jnp.concatenate(
            [
                dot_t(
                    s.ah[rows, 256 * g : 256 * g + 256],
                    s.bdm[128 * g : 128 * g + 128, 256 * g : 256 * g + 256],
                )
                for g in range(2)
            ],
            axis=1,
        ).astype(BF16)
        s.spread[rows, :] = spread
        res = (s.mp[rows, :].astype(F32) + dot(spread, s.wc[...])).astype(BF16).astype(F32)
        n2, inv2 = norm_rows(res)
        n2h = n2.astype(BF16)
        s.n2h[rows, :] = n2h
        sens = s.ls[rows, :]
        upd = res
        gn2 = jnp.zeros((CH, C), F32)
        for f in range(0, FF, 256):
            hid = dot(n2h, s.we[:, f : f + 256])
            gact = dot_t(sens, s.wd[f : f + 256, :])
            h2 = hid * hid
            u = 0.5 + 0.5 * jnp.tanh(hid * (GELU + GELU * 0.044715 * h2))
            act = hid * u
            slope = u + act * (1.0 - u) * (2.0 * GELU + 6.0 * GELU * 0.044715 * h2)
            acth = act.astype(BF16)
            gh = (gact * slope).astype(BF16)
            s.act[rows, f : f + 256] = acth
            s.gh[rows, f : f + 256] = gh
            upd = upd + dot(acth, s.wd[f : f + 256, :])
            gn2 = gn2 + dot_t(gh, s.we[:, f : f + 256])
        s.upd[rows, :] = upd.astype(BF16)
        gres = sens.astype(F32) + norm_back(n2, inv2, gn2)
        s.gres[rows, :] = gres
        grh = gres.astype(BF16)
        s.grh[rows, :] = grh
        s.gspr[rows, :] = dot_t(grh, s.wc[...]).astype(BF16)

    head_sums(s.gspr, s.b_p)
    b_start, b_middle, b_finish, b_drain = reduce_pairs(s.b_p, s.b_y, s.b_z, s.b_ys, s.b_zs)
    bm_start, bm_wait, bm_drain = gather_pairs(s.b_m, s.b_ms)
    b_start()
    out_upd = pltpu.make_async_copy(s.upd, o_upd, s.out_sem.at[0])
    out_upd.start()

    for b in range(4):
        s.e_all[:, 8 * b : 8 * b + 8, :] = tdot(
            s.n2h[...], s.gh[:, 256 * b : 256 * b + 256]
        ).reshape(32, 8, C)
    for b in range(4):
        s.e_all[8 * b : 8 * b + 8, 32:64, :] = tdot(
            s.act[:, 256 * b : 256 * b + 256], s.ls[...]
        ).reshape(8, 32, C)
    s.e_all[:, 64:72, :] = tdot(s.spread[...], s.grh[...]).reshape(32, 8, C)
    e_core = remote(
        s.e_all.at[pl.ds((1 - c) * KXY, KXY)], s.e_core, s.e_cs.at[0], s.e_cs.at[1], other
    )
    e_core.start()
    b_middle()

    for r in range(0, ROWS, CH):
        rows = slice(r, r + CH)
        for g in range(2):
            s.ga[rows, 256 * g : 256 * g + 256] = dot(
                s.gspr[rows, 128 * g : 128 * g + 128],
                s.bdm[128 * g : 128 * g + 128, 256 * g : 256 * g + 256],
            )

    def scatter_xy(src, buf, sem):
        def put(i):
            xx, yy = at_xy(i)
            return remote(
                src.at[xx * NY + yy], buf.at[i], sem.at[0, i], sem.at[1, i], dev_xy(xx, yy)
            )

        def start():
            each(KXY - 1, lambda i: put(i).start())

        def wait():
            each(KXY - 1, lambda i: put(i).wait_recv())

        def drain():
            each(KXY - 1, lambda i: put(i).wait_send())

        return start, wait, drain

    def gather_xy(buf, sem):
        def put(i):
            return remote(
                buf.at[own], buf.at[own], sem.at[0, i], sem.at[1, i], dev_xy(*at_xy(i))
            )

        def got(i):
            xx, yy = from_xy(i)
            f = c * KXY + xx * NY + yy
            return remote(buf.at[f], buf.at[f], sem.at[0, i], sem.at[1, i], dev_xy(xx, yy))

        def start():
            each(KXY - 1, lambda i: put(i).start())

        def wait():
            each(KXY - 1, lambda i: got(i).wait_recv())

        def drain():
            each(KXY - 1, lambda i: put(i).wait_send())

        return start, wait, drain

    def gather_core(buf, sem):
        mine, theirs = pl.ds(c * KXY, KXY), pl.ds((1 - c) * KXY, KXY)
        put = remote(buf.at[mine], buf.at[mine], sem.at[0], sem.at[1], other)
        got = remote(buf.at[theirs], buf.at[theirs], sem.at[0], sem.at[1], other)
        return put.start, got.wait_recv, put.wait_send

    e_core.wait_recv()

    def add_core(i):
        s.e_core[i] = s.e_core[i] + s.e_all[c * KXY + i]

    each(KXY, add_core)
    ex_start, ex_wait, ex_drain = scatter_xy(s.e_core, s.e_xy, s.e_xys)
    ex_start()

    gm = b_finish()
    dv = hdot(gm, att, (1, 0))
    datt = hdot(gm, v, (0, 0))
    dsc = att * (datt - jnp.sum(att * datt, axis=-1, keepdims=True)) * HD ** (-0.5)
    dq = hdot(kk, dsc, (1, 1))
    dk = hdot(q, dsc, (1, 0))
    dqkv = jnp.concatenate([dq, dk, dv], axis=0)
    tokenmap = hdot(tokens, dqkv, (1, 1))
    dtok = hdot(wt, dqkv, (1, 0))
    gsum = dtok * inv_mass
    s.b_m[y, 0:HD, :] = gsum
    s.b_m[y, HD:, :] = jnp.broadcast_to(-jnp.sum(gsum * tokens, axis=0, keepdims=True), (8, 128))
    bm_start()
    bm_wait()
    for j in range(PAIRS):
        s.bdg[64 * j : 64 * j + 64, 128 * j : 128 * j + 128] = spread_diag(s.b_m[j, 0:HD, :])
    gmass = jnp.concatenate([s.b_m[j, HD : HD + 1, :] for j in range(PAIRS)], axis=1)

    for r in range(0, ROWS, CH):
        rows = slice(r, r + CH)
        ga = s.ga[rows, :] + gmass
        ga = ga + jnp.concatenate(
            [
                dot(
                    s.feat[rows, 128 * g : 128 * g + 128],
                    s.bdg[128 * g : 128 * g + 128, 256 * g : 256 * g + 256],
                )
                for g in range(2)
            ],
            axis=1,
        )
        a = s.asg[rows, :]
        gl = (a * (ga - seg_sum(a * ga, s.ones[...])) * inv_sharp).astype(BF16)
        s.gl[rows, :] = gl
        s.gp[rows, :] = jnp.concatenate(
            [
                dot_t(
                    gl[:, 256 * g : 256 * g + 256],
                    s.bdw[128 * g : 128 * g + 128, 256 * g : 256 * g + 256],
                )
                for g in range(2)
            ],
            axis=1,
        ).astype(BF16)
        s.gf[rows, :] = jnp.concatenate(
            [
                dot_t(
                    s.ah[rows, 256 * g : 256 * g + 256],
                    s.bdg[128 * g : 128 * g + 128, 256 * g : 256 * g + 256],
                )
                for g in range(2)
            ],
            axis=1,
        ).astype(BF16)

    s.l_all[:, 0:8, :] = tdot(s.nh[...], s.gf[...]).reshape(32, 8, C)
    s.l_all[:, 8:16, :] = tdot(s.nh[...], s.gp[...]).reshape(32, 8, C)
    slices = jnp.zeros((HD, 128), F32)
    for g in range(2):
        t = tdot(s.proj[:, 128 * g : 128 * g + 128], s.gl[:, 256 * g : 256 * g + 256])
        for j in range(2):
            slices = slices + pack_diag(t[64 * j : 64 * j + 64, 128 * j : 128 * j + 128])
    tokenmap = jnp.where(z == 0, tokenmap, jnp.zeros_like(tokenmap))
    small = jnp.concatenate([slices, tokenmap, jnp.zeros((HD, 32), F32)], axis=1)
    for i in range(32):
        s.l_all[i, 16:17, :] = small[i : i + 1, :]
    l_core = remote(
        s.l_all.at[pl.ds((1 - c) * KXY, KXY)], s.l_core, s.l_cs.at[0], s.l_cs.at[1], other
    )
    l_core.start()

    ex_wait()
    part = s.e_core[k]
    for i in range(KXY - 1):
        part = part + s.e_xy[i]
    s.e_part[...] = part

    def e_putz(i):
        t = at_z(i)
        return remote(
            s.e_part.at[pl.ds(pl.multiple_of(8 * t, 8), 8)],
            s.e_z.at[z],
            s.e_zs.at[0, i],
            s.e_zs.at[1, i],
            dev_z(t),
        )

    def e_gotz(i):
        f = from_z(i)
        return remote(s.e_z.at[f], s.e_z.at[f], s.e_zs.at[0, i], s.e_zs.at[1, i], dev_z(f))

    def e_putzo(i):
        return remote(
            s.e_part.at[pl.ds(64, 8)],
            s.e_zo.at[z],
            s.e_zos.at[0, i],
            s.e_zos.at[1, i],
            dev_z(at_z(i)),
        )

    def e_gotzo(i):
        f = from_z(i)
        return remote(s.e_zo.at[f], s.e_zo.at[f], s.e_zos.at[0, i], s.e_zos.at[1, i], dev_z(f))

    def e_startz(i):
        e_putz(i).start()
        e_putzo(i).start()

    each(NZ - 1, e_startz)
    s.e_z[z] = s.e_part[pl.ds(pl.multiple_of(8 * z, 8), 8), :]
    s.e_zo[z] = s.e_part[64:72, :]

    l_core.wait_recv()

    def add_core_late(i):
        s.l_core[i] = s.l_core[i] + s.l_all[c * KXY + i]

    each(KXY, add_core_late)
    lx_start, lx_wait, lx_drain = scatter_xy(s.l_core, s.l_xy, s.l_xys)
    lx_start()

    each(NZ - 1, lambda i: e_gotz(i).wait_recv())
    total = s.e_z[0]
    for i in range(1, NZ):
        total = total + s.e_z[i]
    myrows = pl.ds(pl.multiple_of(8 * z, 8), 8)
    s.e_fin[own, myrows, :] = total * scale

    def e_putzg(i):
        piece = s.e_fin.at[own, myrows]
        return remote(piece, piece, s.e_zgs.at[0, i], s.e_zgs.at[1, i], dev_z(at_z(i)))

    def e_gotzg(i):
        f = from_z(i)
        piece = s.e_fin.at[own, pl.ds(pl.multiple_of(8 * f, 8), 8)]
        return remote(piece, piece, s.e_zgs.at[0, i], s.e_zgs.at[1, i], dev_z(f))

    each(NZ - 1, lambda i: e_putzg(i).start())
    each(NZ - 1, lambda i: e_gotzo(i).wait_recv())
    total = s.e_zo[0]
    for i in range(1, NZ):
        total = total + s.e_zo[i]
    s.e_fin[own, 64:72, :] = total * scale

    lx_wait()
    part = s.l_core[k]
    for i in range(KXY - 1):
        part = part + s.l_xy[i]
    s.l_z[z] = part

    def l_putz(i):
        return remote(
            s.l_z.at[z], s.l_z.at[z], s.l_zs.at[0, i], s.l_zs.at[1, i], dev_z(at_z(i))
        )

    def l_gotz(i):
        f = from_z(i)
        return remote(s.l_z.at[f], s.l_z.at[f], s.l_zs.at[0, i], s.l_zs.at[1, i], dev_z(f))

    each(NZ - 1, lambda i: l_putz(i).start())

    each(NZ - 1, lambda i: e_gotzg(i).wait_recv())
    eg_start, eg_wait, eg_drain = gather_xy(s.e_fin, s.e_xygs)
    eg_start()

    for r in range(0, ROWS, CH):
        rows = slice(r, r + CH)
        normed, inv = norm_rows(s.mp[rows, :].astype(F32))
        gn = dot_t(s.gf[rows, :], s.wa[...]) + dot_t(s.gp[rows, :], s.wp[...])
        s.pgr[rows, :] = (s.gres[rows, :] + norm_back(normed, inv, gn)).astype(BF16)
    out_pg = pltpu.make_async_copy(s.pgr, o_pg, s.out_sem.at[1])
    out_pg.start()

    each(NZ - 1, lambda i: l_gotz(i).wait_recv())
    total = s.l_z[0]
    for i in range(1, NZ):
        total = total + s.l_z[i]
    s.l_fin[own] = total * scale
    lg_start, lg_wait, lg_drain = gather_xy(s.l_fin, s.l_xygs)
    lg_start()

    eg_wait()
    ec_start, ec_wait, ec_drain = gather_core(s.e_fin, s.e_cgs)
    ec_start()
    lg_wait()
    lc_start, lc_wait, lc_drain = gather_core(s.l_fin, s.l_cgs)
    lc_start()

    ec_wait()
    outs = [out_upd, out_pg]
    for b in range(4):
        outs.append(
            pltpu.make_async_copy(
                s.e_fin.at[:, pl.ds(8 * b, 8), :],
                o_up.at[:, :, pl.ds(256 * b, 256)],
                s.out_sem.at[2 + b],
            )
        )
    outs.append(pltpu.make_async_copy(s.e_fin.at[:, pl.ds(32, 32), :], o_down, s.out_sem.at[6]))
    outs.append(pltpu.make_async_copy(s.e_fin.at[:, pl.ds(64, 8), :], o_out, s.out_sem.at[7]))
    for o in outs[2:]:
        o.start()
    lc_wait()
    late = [
        pltpu.make_async_copy(s.l_fin.at[:, pl.ds(0, 8), :], o_feat, s.out_sem.at[8]),
        pltpu.make_async_copy(s.l_fin.at[:, pl.ds(8, 8), :], o_proj, s.out_sem.at[9]),
    ]
    for o in late:
        o.start()
    rows = [s.l_fin[i, 16:17, :] for i in range(32)]
    small = jnp.concatenate(rows, axis=0)
    o_slice[...] = small[:, 0:SL] + small[:, SL : 2 * SL]
    o_tok[...] = small[:, 128 : 128 + 3 * HD]

    a_drain()
    am_drain()
    b_drain()
    bm_drain()
    e_core.wait_send()
    ex_drain()
    l_core.wait_send()
    lx_drain()
    each(NZ - 1, lambda i: e_putz(i).wait_send())
    each(NZ - 1, lambda i: e_putzo(i).wait_send())
    each(NZ - 1, lambda i: e_putzg(i).wait_send())
    each(NZ - 1, lambda i: l_putz(i).wait_send())
    eg_drain()
    lg_drain()
    ec_drain()
    lc_drain()
    for o in outs + late:
        o.wait()


def body(mp, ls, wa, wp, ws, wt, wc, we, wd, sharp):
    scale = (lax.axis_size("dp") * lax.axis_size("point") * ROWS) ** (-0.5)
    anyspace = pl.BlockSpec(memory_space=pl.ANY)
    vmem = pl.BlockSpec(memory_space=pltpu.VMEM)
    outs = pl.pallas_call(
        functools.partial(kernel, scale),
        out_shape=(
            jax.ShapeDtypeStruct((ROWS, C), BF16),
            jax.ShapeDtypeStruct((ROWS, C), BF16),
            jax.ShapeDtypeStruct((32, 8, C), F32),
            jax.ShapeDtypeStruct((32, 8, C), F32),
            jax.ShapeDtypeStruct((HD, SL), F32),
            jax.ShapeDtypeStruct((HD, 3 * HD), F32),
            jax.ShapeDtypeStruct((32, 8, C), F32),
            jax.ShapeDtypeStruct((32, 8, FF), F32),
            jax.ShapeDtypeStruct((32, 32, C), F32),
        ),
        in_specs=[anyspace] * 9 + [pl.BlockSpec(memory_space=pltpu.SMEM)],
        out_specs=(anyspace,) * 4 + (vmem,) * 2 + (anyspace,) * 3,
        scratch_shapes=list(SCRATCH.values()),
        compiler_params=pltpu.CompilerParams(
            collective_id=0, has_side_effects=True, vmem_limit_bytes=48 << 20
        ),
        name="layer",
    )(mp[0], ls[0], wa, wp, ws, wt, wc, we, wd, sharp)
    upd, pg, feat, proj, sl, tok, out, up, down = outs
    return (
        upd[None],
        pg[None],
        feat.reshape(C, C),
        proj.reshape(C, C),
        sl,
        tok,
        out.reshape(C, C),
        up.reshape(C, FF),
        down.reshape(FF, C),
    )


def solution(mesh):
    split = P("dp", "point", None)
    return jax.shard_map(
        body,
        mesh=mesh,
        in_specs=(split, split) + (P(),) * 8,
        out_specs=(split, split) + (P(),) * 7,
        check_vma=False,
    )
```

```python
import functools

import jax
import jax.numpy as jnp
from jax import lax
from jax.experimental import pallas as pl
from jax.experimental.pallas import tpu as pltpu
from jax.sharding import PartitionSpec as P

F32 = jnp.float32
BF16 = jnp.bfloat16
MESH = pl.DeviceIdType.MESH
EPS = 1e-05
GELU = 0.7978845608028654
HIGH = lax.Precision.HIGHEST

NX, NC, NZ, NY = 4, 2, 8, 4
ROWS = 512
C, FF, HEADS, HD, SL = 256, 1024, 8, 32, 64
PAIRS = 4
KXY = NX * NY
PARTS = ((16, 24), (16, 16))
LROWS = 17
CH = 512


def dot(a, b):
    return jnp.dot(a, b, preferred_element_type=F32)


def dot_t(a, b):
    return lax.dot_general(a, b, (((1,), (1,)), ((), ())), preferred_element_type=F32)


def tdot(a, b):
    return lax.dot_general(a, b, (((0,), (0,)), ((), ())), preferred_element_type=F32)


def hdot(a, b, dims):
    return lax.dot_general(
        a, b, ((dims[:1], dims[1:]), ((), ())), precision=HIGH, preferred_element_type=F32
    )


def norm_rows(v):
    center = v - jnp.mean(v, axis=-1, keepdims=True)
    inv = lax.rsqrt(jnp.mean(center * center, axis=-1, keepdims=True) + EPS)
    return center * inv, inv


def norm_back(normed, inv, g):
    return inv * (
        g - jnp.mean(g, axis=-1, keepdims=True) - normed * jnp.mean(g * normed, axis=-1, keepdims=True)
    )


def seg_sum(v, ones):
    hi = v.astype(BF16)
    lo = (v - hi.astype(F32)).astype(BF16)
    return jnp.concatenate(
        [
            dot(hi[:, 256 * g : 256 * g + 256], ones) + dot(lo[:, 256 * g : 256 * g + 256], ones)
            for g in range(2)
        ],
        axis=1,
    )


def each(n, f):
    def step(i, carry):
        f(i)
        return carry

    lax.fori_loop(0, n, step, 0)


def remote(src, dst, ss, rs, dev):
    return pltpu.make_async_remote_copy(
        src_ref=src, dst_ref=dst, send_sem=ss, recv_sem=rs, device_id=dev, device_id_type=MESH
    )


SCRATCH = dict(
    mp=pltpu.VMEM((ROWS, C), BF16),
    ls=pltpu.VMEM((ROWS, C), BF16),
    wa=pltpu.VMEM((C, C), BF16),
    wp=pltpu.VMEM((C, C), BF16),
    ws=pltpu.VMEM((HD, SL), BF16),
    wt=pltpu.VMEM((HD, 3 * HD), BF16),
    wc=pltpu.VMEM((C, C), BF16),
    we=pltpu.VMEM((C, FF), BF16),
    wd=pltpu.VMEM((FF, C), BF16),
    in_sem=pltpu.SemaphoreType.DMA((9,)),
    nh=pltpu.VMEM((ROWS, C), BF16),
    feat=pltpu.VMEM((ROWS, C), BF16),
    proj=pltpu.VMEM((ROWS, C), BF16),
    asg=pltpu.VMEM((ROWS, 512), F32),
    ah=pltpu.VMEM((ROWS, 512), BF16),
    bdw=pltpu.VMEM((C, 512), BF16),
    bdm=pltpu.VMEM((C, 512), BF16),
    bdg=pltpu.VMEM((C, 512), BF16),
    ones=pltpu.VMEM((256, 256), BF16),
    spread=pltpu.VMEM((ROWS, C), BF16),
    n2h=pltpu.VMEM((ROWS, C), BF16),
    act=pltpu.VMEM((ROWS, FF), BF16),
    gh=pltpu.VMEM((ROWS, FF), BF16),
    gres=pltpu.VMEM((ROWS, C), F32),
    grh=pltpu.VMEM((ROWS, C), BF16),
    gspr=pltpu.VMEM((ROWS, C), BF16),
    ga=pltpu.VMEM((ROWS, 512), F32),
    gl=pltpu.VMEM((ROWS, 512), BF16),
    gf=pltpu.VMEM((ROWS, C), BF16),
    gp=pltpu.VMEM((ROWS, C), BF16),
    upd=pltpu.VMEM((ROWS, C), BF16),
    pgr=pltpu.VMEM((ROWS, C), BF16),
    slc=pltpu.VMEM((HD, SL), F32),
    tok=pltpu.VMEM((HD, 3 * HD), F32),
    out_sem=pltpu.SemaphoreType.DMA((13,)),
    a_p=pltpu.VMEM((PAIRS, 40, 128), F32),
    a_y=pltpu.VMEM((3, 40, 128), F32),
    a_z=pltpu.VMEM((NZ, 40, 128), F32),
    a_m=pltpu.VMEM((PAIRS, HD, 128), F32),
    a_ys=pltpu.SemaphoreType.DMA((2, 3)),
    a_zs=pltpu.SemaphoreType.DMA((2, 7)),
    a_ms=pltpu.SemaphoreType.DMA((2, 3)),
    b_p=pltpu.VMEM((PAIRS, HD, 128), F32),
    b_y=pltpu.VMEM((3, HD, 128), F32),
    b_z=pltpu.VMEM((NZ, HD, 128), F32),
    b_m=pltpu.VMEM((PAIRS, 40, 128), F32),
    b_ys=pltpu.SemaphoreType.DMA((2, 3)),
    b_zs=pltpu.SemaphoreType.DMA((2, 7)),
    b_ms=pltpu.SemaphoreType.DMA((2, 3)),
    l_all=pltpu.VMEM((2 * KXY, LROWS, C), F32),
    l_core=pltpu.VMEM((KXY, LROWS, C), F32),
    l_xy=pltpu.VMEM((KXY - 1, LROWS, C), F32),
    l_z=pltpu.VMEM((NZ, LROWS, C), F32),
    l_fin=pltpu.VMEM((2 * KXY, LROWS, C), F32),
    l_cs=pltpu.SemaphoreType.DMA((2,)),
    l_xys=pltpu.SemaphoreType.DMA((2, KXY - 1)),
    l_zs=pltpu.SemaphoreType.DMA((2, 7)),
    l_xygs=pltpu.SemaphoreType.DMA((2, KXY - 1)),
    l_cgs=pltpu.SemaphoreType.DMA((2,)),
)


def early_scratch(p, ru, rv):
    f = lambda *shape: pltpu.VMEM(shape + (C,), F32)
    d = lambda *shape: pltpu.SemaphoreType.DMA((2,) + shape)
    names = dict(
        u=f(32, ru), v=f(32, rv), uc=f(KXY, ru), vc=f(KXY, rv),
        ux=f(3, 4, ru), vy=f(3, 4, rv), u1=f(4, ru), v1=f(4, rv),
        uy=f(3, ru), vx=f(3, rv), part=f(ru + rv),
        z=pltpu.VMEM((NZ, 8, 128), F32), zo=f(NZ, 8), zf=f(32),
        uf=f(32, ru), vf=f(32, rv),
        us=d(4), vs=d(4), uxs=d(3), vys=d(3), uys=d(3), vxs=d(3),
        zs=d(7), zos=d(7), zgs=d(7), uygs=d(3), vxgs=d(3), uxgs=d(3), vygs=d(3), ugs=d(4), vgs=d(4),
    )
    return {"e%d_%s" % (p, n): spec for n, spec in names.items()}


for p, rows in enumerate(PARTS):
    SCRATCH.update(early_scratch(p, *rows))


class Names:
    pass


class Axis:
    def __init__(self, n, me, dev):
        self.n, self.me, self.dev = n, me, dev

    def to(self, i):
        return lax.rem(self.me + i + 1, self.n)

    def frm(self, i):
        return lax.rem(self.me + self.n - 1 - i, self.n)


class Early:
    def __init__(self, s, p, rows, place, scale):
        for name in early_scratch(0, 1, 1):
            setattr(self, name[3:], getattr(s, "e%d_%s" % (p, name[3:])))
        self.ru, self.rv = rows
        self.out = self.rv > 16
        self.scale = scale
        x, c, z, y = place
        self.x, self.c, self.pz, self.y = x, c, z, y
        self.ax = Axis(NX, x, lambda t: (t * NC + c, z * NY + y))
        self.ay = Axis(NY, y, lambda t: (x * NC + c, z * NY + t))
        self.az = Axis(NZ, z, lambda t: (x * NC + c, t * NY + y))
        self.other = (x * NC + (1 - c), z * NY + y)
        self.first = ((self.ax, self.u, self.uc, self.ux, self.u1, self.us, self.uxs),
                      (self.ay, self.v, self.vc, self.vy, self.v1, self.vs, self.vys))
        self.second = ((self.ay, self.u1, self.uy, self.uys, 0, self.ru),
                       (self.ax, self.v1, self.vx, self.vxs, self.ru, self.rv))
        self.fin2 = ((self.ay, self.uf, 16 * c + 4 * x, self.uygs),
                     (self.ax, self.vf, 16 * c + 4 * y, self.vxgs))
        self.fin1 = ((self.ax, self.uf, self.uxgs, self.ugs), (self.ay, self.vf, self.vygs, self.vgs))
        self.sent = []

    def block(self, c, t):
        return pl.ds(16 * c + 4 * t, 4)

    def core_start(self):
        for o in (0, 1, 2, 3):
            for ax, full, half, _, _, sem, _ in self.first:
                self.core_copy(ax, full, half, sem, o).start()

    def core_copy(self, ax, full, half, sem, o):
        t = lax.rem(ax.me + 1 + o, 4)
        return remote(
            full.at[self.block(1 - self.c, t)], half.at[pl.ds(4 * t, 4)], sem.at[0, o], sem.at[1, o],
            self.other,
        )

    def st1_copy(self, ax, half, slots, sem, i):
        t = ax.to(i)
        return remote(half.at[pl.ds(4 * t, 4)], slots.at[i], sem.at[0, i], sem.at[1, i], ax.dev(t))

    def st1_start(self):
        for o in (0, 1, 2, 3):
            for ax, full, half, slots, _, sem, sem1 in self.first:
                self.core_copy(ax, full, half, sem, o).wait_recv()
                t = lax.rem(ax.me + 1 + o, 4)
                mine = pl.ds(4 * t, 4)
                half[mine] = half[mine] + full[self.block(self.c, t)]
                if o < 3:
                    self.st1_copy(ax, half, slots, sem1, o).start()

    def st2_copy(self, ax, src, slots, sem, i):
        t = ax.to(i)
        return remote(src.at[t], slots.at[i], sem.at[0, i], sem.at[1, i], ax.dev(t))

    def st2_start(self):
        for (ax, _, half, slots, one, _, sem1), (ax2, src, slots2, sem2, _, _) in zip(
            self.first, self.second
        ):
            for i in range(3):
                self.st1_copy(ax, half, slots, sem1, i).wait_recv()
            one[...] = half[pl.ds(4 * ax.me, 4)] + slots[0] + slots[1] + slots[2]
            for i in range(3):
                self.st2_copy(ax2, src, slots2, sem2, i).start()

    def tile(self, t):
        return (
            pl.ds(pl.multiple_of(8 * (t // 2), 8), 8),
            pl.ds(pl.multiple_of(128 * (t % 2), 128), 128),
        )

    def z_copy(self, i):
        t = self.az.to(i)
        rows, lanes = self.tile(t)
        return remote(
            self.part.at[rows, lanes], self.z.at[self.pz], self.zs.at[0, i], self.zs.at[1, i],
            self.az.dev(t),
        )

    def z_got(self, i):
        f = self.az.frm(i)
        return remote(
            self.z.at[f], self.z.at[f], self.zs.at[0, i], self.zs.at[1, i], self.az.dev(f)
        )

    def zo_copy(self, i):
        t = self.az.to(i)
        return remote(
            self.part.at[pl.ds(32, 8)], self.zo.at[self.pz], self.zos.at[0, i], self.zos.at[1, i],
            self.az.dev(t),
        )

    def zo_got(self, i):
        f = self.az.frm(i)
        return remote(
            self.zo.at[f], self.zo.at[f], self.zos.at[0, i], self.zos.at[1, i], self.az.dev(f)
        )

    def z_start(self):
        for ax, src, slots, sem, at, n in self.second:
            for i in range(3):
                self.st2_copy(ax, src, slots, sem, i).wait_recv()
            self.part[at : at + n, :] = src[ax.me] + slots[0] + slots[1] + slots[2]
        each(7, lambda i: self.z_copy(i).start())
        rows, lanes = self.tile(self.pz)
        self.z[self.pz] = self.part[rows, lanes]
        if self.out:
            each(7, lambda i: self.zo_copy(i).start())
            self.zo[self.pz] = self.part[32:40, :]

    def zg_copy(self, i):
        piece = self.zf.at[self.tile(self.pz)]
        return remote(
            piece, piece, self.zgs.at[0, i], self.zgs.at[1, i], self.az.dev(self.az.to(i))
        )

    def zg_got(self, i):
        f = self.az.frm(i)
        piece = self.zf.at[self.tile(f)]
        return remote(piece, piece, self.zgs.at[0, i], self.zgs.at[1, i], self.az.dev(f))

    def zg_start(self):
        each(7, lambda i: self.z_got(i).wait_recv())
        total = self.z[0]
        for i in range(1, NZ):
            total = total + self.z[i]
        self.zf[self.tile(self.pz)] = total * self.scale
        each(7, lambda i: self.zg_copy(i).start())

    def fin2_copy(self, ax, fin, base, sem, i):
        piece = fin.at[base + ax.me]
        return remote(piece, piece, sem.at[0, i], sem.at[1, i], ax.dev(ax.to(i)))

    def fin2_got(self, ax, fin, base, sem, i):
        f = ax.frm(i)
        piece = fin.at[base + f]
        return remote(piece, piece, sem.at[0, i], sem.at[1, i], ax.dev(f))

    def st2g_start(self):
        own_u = 16 * self.c + 4 * self.x + self.y
        own_v = 16 * self.c + 4 * self.y + self.x
        if self.out:
            each(7, lambda i: self.zo_got(i).wait_recv())
            total = self.zo[0]
            for i in range(1, NZ):
                total = total + self.zo[i]
            self.vf[own_v, 16:24, :] = total * self.scale
        each(7, lambda i: self.zg_got(i).wait_recv())
        self.uf[own_u] = self.zf[0:16, :]
        self.vf[own_v, 0:16, :] = self.zf[16:32, :]
        for ax, fin, base, sem in self.fin2:
            for i in range(3):
                self.fin2_copy(ax, fin, base, sem, i).start()

    def fin1_copy(self, ax, fin, sem, i):
        piece = fin.at[self.block(self.c, ax.me)]
        return remote(piece, piece, sem.at[0, i], sem.at[1, i], ax.dev(ax.to(i)))

    def fin1_got(self, ax, fin, sem, i):
        f = ax.frm(i)
        piece = fin.at[self.block(self.c, f)]
        return remote(piece, piece, sem.at[0, i], sem.at[1, i], ax.dev(f))

    def coreg_copy(self, ax, fin, sem, o):
        piece = fin.at[self.block(self.c, lax.rem(ax.me + NX - o, 4))]
        return remote(piece, piece, sem.at[0, o], sem.at[1, o], self.other)

    def coreg_got(self, ax, fin, sem, o):
        piece = fin.at[self.block(1 - self.c, lax.rem(ax.me + NX - o, 4))]
        return remote(piece, piece, sem.at[0, o], sem.at[1, o], self.other)

    def st1g_start(self):
        for (ax2, fin, base, sem2), (ax, _, sem1, semc) in zip(self.fin2, self.fin1):
            for i in range(3):
                self.fin2_got(ax2, fin, base, sem2, i).wait_recv()
            for i in range(3):
                self.fin1_copy(ax, fin, sem1, i).start()
            self.coreg_copy(ax, fin, semc, 0).start()

    def coreg_start(self):
        for i in (0, 2, 1):
            for ax, fin, sem1, semc in self.fin1:
                self.fin1_got(ax, fin, sem1, i).wait_recv()
                self.coreg_copy(ax, fin, semc, i + 1).start()

    def coreg_wait(self):
        for ax, fin, _, semc in self.fin1:
            for o in range(4):
                self.coreg_got(ax, fin, semc, o).wait_recv()

    def drain(self):
        for (ax, full, half, slots, _, sem, sem1), (ax2, src, slots2, sem2, _, _) in zip(
            self.first, self.second
        ):
            for o in range(4):
                self.core_copy(ax, full, half, sem, o).wait_send()
            for i in range(3):
                self.st1_copy(ax, half, slots, sem1, i).wait_send()
                self.st2_copy(ax2, src, slots2, sem2, i).wait_send()
        each(7, lambda i: self.z_copy(i).wait_send())
        each(7, lambda i: self.zg_copy(i).wait_send())
        if self.out:
            each(7, lambda i: self.zo_copy(i).wait_send())
        for (ax2, fin, base, sem2), (ax, _, sem1, semc) in zip(self.fin2, self.fin1):
            for i in range(3):
                self.fin2_copy(ax2, fin, base, sem2, i).wait_send()
                self.fin1_copy(ax, fin, sem1, i).wait_send()
            for o in range(4):
                self.coreg_copy(ax, fin, semc, o).wait_send()


def kernel(scale, *refs):
    ins, rest = refs[:10], refs[10:]
    (o_upd, o_pg, o_feat, o_proj, o_slice, o_tok, o_out, o_up, o_down) = rest[:9]
    s = Names()
    for name, ref in zip(SCRATCH, rest[9:]):
        setattr(s, name, ref)

    dp, pt = lax.axis_index("dp"), lax.axis_index("point")
    x, c = dp // NC, dp % NC
    z, y = pt // NY, pt % NY
    k = x * NY + y
    own = c * KXY + k
    other = (x * NC + (1 - c), pt)

    def at_y(i):
        return lax.rem(y + i + 1, NY)

    def from_y(i):
        return lax.rem(y + NY - 1 - i, NY)

    def at_z(i):
        return lax.rem(z + i + 1, NZ)

    def from_z(i):
        return lax.rem(z + NZ - 1 - i, NZ)

    def at_xy(i):
        j = i + 1
        return lax.rem(x + j // NY, NX), lax.rem(y + j % NY, NY)

    def from_xy(i):
        j = i + 1
        return lax.rem(x + NX - j // NY, NX), lax.rem(y + NY - j % NY, NY)

    def at_x(i):
        return lax.rem(x + i + 1, NX)

    def from_x(i):
        return lax.rem(x + NX - 1 - i, NX)

    def dev_x(xx):
        return (xx * NC + c, pt)

    def dev_y(yy):
        return (dp, z * NY + yy)

    def dev_z(zz):
        return (dp, zz * NY + y)

    def dev_xy(xx, yy):
        return (xx * NC + c, z * NY + yy)

    barrier = pltpu.get_barrier_semaphore()
    pl.semaphore_signal(barrier, inc=1, device_id=other, device_id_type=MESH)
    each(
        KXY - 1,
        lambda i: pl.semaphore_signal(
            barrier, inc=1, device_id=dev_xy(*at_xy(i)), device_id_type=MESH
        ),
    )
    each(
        NZ - 1,
        lambda i: pl.semaphore_signal(barrier, inc=1, device_id=dev_z(at_z(i)), device_id_type=MESH),
    )

    in_dst = (s.mp, s.ls, s.wa, s.wp, s.ws, s.wt, s.wc, s.we, s.wd)
    loads = [pltpu.make_async_copy(a, b, s.in_sem.at[i]) for i, (a, b) in enumerate(zip(ins, in_dst))]
    order = (0, 2, 3, 4, 5, 1, 6, 7, 8)
    for i in order:
        loads[i].start()
    sharp_ref = ins[9]

    lane = lax.broadcasted_iota(jnp.int32, (1, 512), 1)
    sharp = jnp.full((1, 512), sharp_ref[0], F32)
    for h in range(1, HEADS):
        sharp = jnp.where(lane // SL == h, sharp_ref[h], sharp)
    inv_sharp = 1.0 / sharp
    rr = lax.broadcasted_iota(jnp.int32, (256, 256), 0)
    cc = lax.broadcasted_iota(jnp.int32, (256, 256), 1)
    s.ones[...] = jnp.where(rr // SL == cc // SL, 1.0, 0.0).astype(BF16)
    s.bdm[...] = jnp.zeros_like(s.bdm)
    s.bdg[...] = jnp.zeros_like(s.bdg)
    low = lax.broadcasted_iota(jnp.int32, (HD, 128), 1) < SL

    def pack_diag(t):
        return jnp.where(low, t[:HD], t[HD:])

    def spread_diag(v):
        return jnp.concatenate([jnp.where(low, v, 0.0), jnp.where(low, 0.0, v)], axis=0).astype(BF16)

    loads[4].wait()
    w1 = s.ws[...].astype(F32)
    w2 = jnp.concatenate([w1, w1], axis=1)
    s.bdw[...] = jnp.zeros_like(s.bdw)
    for j in range(PAIRS):
        s.bdw[64 * j : 64 * j + 64, 128 * j : 128 * j + 128] = spread_diag(w2)

    for i in (0, 2, 3):
        loads[i].wait()
    mass = jnp.zeros((1, 512), F32)
    for r in range(0, ROWS, CH):
        rows = slice(r, r + CH)
        normed, _ = norm_rows(s.mp[rows, :].astype(F32))
        nh = normed.astype(BF16)
        s.nh[rows, :] = nh
        s.feat[rows, :] = dot(nh, s.wa[...]).astype(BF16)
        proj = dot(nh, s.wp[...]).astype(BF16)
        s.proj[rows, :] = proj
        logits = (
            jnp.concatenate(
                [
                    dot(
                        proj[:, 128 * g : 128 * g + 128],
                        s.bdw[128 * g : 128 * g + 128, 256 * g : 256 * g + 256],
                    )
                    for g in range(2)
                ],
                axis=1,
            )
            * inv_sharp
        )
        e = jnp.exp(logits)
        a = e / seg_sum(e, s.ones[...])
        s.asg[rows, :] = a
        s.ah[rows, :] = a.astype(BF16)
        mass = mass + jnp.sum(a, axis=0, keepdims=True)

    def head_sums(values, out):
        for g in range(2):
            t = tdot(values[:, 128 * g : 128 * g + 128], s.ah[:, 256 * g : 256 * g + 256])
            for j in range(2):
                out[2 * g + j, 0:HD, :] = pack_diag(
                    t[64 * j : 64 * j + 64, 128 * j : 128 * j + 128]
                )

    head_sums(s.feat, s.a_p)
    for j in range(PAIRS):
        s.a_p[j, HD:, :] = jnp.broadcast_to(mass[:, 128 * j : 128 * j + 128], (8, 128))

    def reduce_pairs(part, buf_y, buf_z, sem_y, sem_z):
        def put_y(i):
            t = at_y(i)
            return remote(part.at[t], buf_y.at[i], sem_y.at[0, i], sem_y.at[1, i], dev_y(t))

        def put_z(i):
            return remote(
                buf_z.at[z], buf_z.at[z], sem_z.at[0, i], sem_z.at[1, i], dev_z(at_z(i))
            )

        def got_z(i):
            f = from_z(i)
            return remote(buf_z.at[f], buf_z.at[f], sem_z.at[0, i], sem_z.at[1, i], dev_z(f))

        def start():
            each(NY - 1, lambda i: put_y(i).start())

        def middle():
            each(NY - 1, lambda i: put_y(i).wait_recv())
            buf_z[z] = part[y] + buf_y[0] + buf_y[1] + buf_y[2]
            each(NZ - 1, lambda i: put_z(i).start())

        def finish():
            each(NZ - 1, lambda i: got_z(i).wait_recv())
            total = buf_z[0]
            for i in range(1, NZ):
                total = total + buf_z[i]
            return total

        def drain():
            each(NY - 1, lambda i: put_y(i).wait_send())
            each(NZ - 1, lambda i: put_z(i).wait_send())

        return start, middle, finish, drain

    def gather_pairs(buf, sem):
        def put(i):
            return remote(buf.at[y], buf.at[y], sem.at[0, i], sem.at[1, i], dev_y(at_y(i)))

        def got(i):
            f = from_y(i)
            return remote(buf.at[f], buf.at[f], sem.at[0, i], sem.at[1, i], dev_y(f))

        def start():
            each(NY - 1, lambda i: put(i).start())

        def wait():
            each(NY - 1, lambda i: got(i).wait_recv())

        def drain():
            each(NY - 1, lambda i: put(i).wait_send())

        return start, wait, drain

    pl.semaphore_wait(barrier, 1 + (KXY - 1) + (NZ - 1))
    a_start, a_middle, a_finish, a_drain = reduce_pairs(s.a_p, s.a_y, s.a_z, s.a_ys, s.a_zs)
    am_start, am_wait, am_drain = gather_pairs(s.a_m, s.a_ms)
    a_start()
    a_middle()
    for i in (5, 1, 6, 7, 8):
        loads[i].wait()
    total = a_finish()

    wt = s.wt[...].astype(F32)
    inv_mass = 1.0 / (total[HD : HD + 1] + EPS)
    tokens = total[:HD] * inv_mass
    qkv = hdot(wt, tokens, (0, 0))
    q, kk, v = qkv[:HD], qkv[HD : 2 * HD], qkv[2 * HD :]
    r2 = lax.broadcasted_iota(jnp.int32, (128, 128), 0) // SL
    c2 = lax.broadcasted_iota(jnp.int32, (128, 128), 1) // SL
    scores = hdot(q, kk, (0, 0)) * HD ** (-0.5)
    expo = jnp.where(r2 == c2, jnp.exp(jnp.where(r2 == c2, scores, 0.0)), 0.0)
    att = expo / jnp.sum(expo, axis=-1, keepdims=True)
    s.a_m[y] = hdot(v, att, (1, 1))
    am_start()
    am_wait()
    for j in range(PAIRS):
        s.bdm[64 * j : 64 * j + 64, 128 * j : 128 * j + 128] = spread_diag(s.a_m[j])

    for r in range(0, ROWS, CH):
        rows = slice(r, r + CH)
        spread = jnp.concatenate(
            [
                dot_t(
                    s.ah[rows, 256 * g : 256 * g + 256],
                    s.bdm[128 * g : 128 * g + 128, 256 * g : 256 * g + 256],
                )
                for g in range(2)
            ],
            axis=1,
        ).astype(BF16)
        s.spread[rows, :] = spread
        res = (s.mp[rows, :].astype(F32) + dot(spread, s.wc[...])).astype(BF16).astype(F32)
        n2, inv2 = norm_rows(res)
        n2h = n2.astype(BF16)
        s.n2h[rows, :] = n2h
        sens = s.ls[rows, :]
        upd = res
        gn2 = jnp.zeros((CH, C), F32)
        for f in range(0, FF, 256):
            hid = dot(n2h, s.we[:, f : f + 256])
            gact = dot_t(sens, s.wd[f : f + 256, :])
            h2 = hid * hid
            u = 0.5 + 0.5 * jnp.tanh(hid * (GELU + GELU * 0.044715 * h2))
            act = hid * u
            slope = u + act * (1.0 - u) * (2.0 * GELU + 6.0 * GELU * 0.044715 * h2)
            acth = act.astype(BF16)
            gh = (gact * slope).astype(BF16)
            s.act[rows, f : f + 256] = acth
            s.gh[rows, f : f + 256] = gh
            upd = upd + dot(acth, s.wd[f : f + 256, :])
            gn2 = gn2 + dot_t(gh, s.we[:, f : f + 256])
        s.upd[rows, :] = upd.astype(BF16)
        gres = sens.astype(F32) + norm_back(n2, inv2, gn2)
        s.gres[rows, :] = gres
        grh = gres.astype(BF16)
        s.grh[rows, :] = grh
        s.gspr[rows, :] = dot_t(grh, s.wc[...]).astype(BF16)

    head_sums(s.gspr, s.b_p)
    b_start, b_middle, b_finish, b_drain = reduce_pairs(s.b_p, s.b_y, s.b_z, s.b_ys, s.b_zs)
    bm_start, bm_wait, bm_drain = gather_pairs(s.b_m, s.b_ms)
    b_start()
    outs = []

    def write(src, dst):
        copy = pltpu.make_async_copy(src, dst, s.out_sem.at[len(outs)])
        copy.start()
        outs.append(copy)

    write(s.upd, o_upd)

    early = [Early(s, p, PARTS[p], (x, c, z, y), scale) for p in range(len(PARTS))]
    for p, e in enumerate(early):
        for b in range(2):
            f = 256 * (2 * p + b)
            e.u[:, 8 * b : 8 * b + 8, :] = tdot(s.n2h[...], s.gh[:, f : f + 256]).reshape(32, 8, C)
            e.v[16 * b : 16 * b + 16, 0:16, :] = tdot(s.act[:, f : f + 256], s.ls[...]).reshape(
                16, 16, C
            )
        if p == 0:
            e.v[:, 16:24, :] = tdot(s.spread[...], s.grh[...]).reshape(32, 8, C)
        e.core_start()
    for e in early:
        e.st1_start()
    b_middle()

    for r in range(0, ROWS, CH):
        rows = slice(r, r + CH)
        for g in range(2):
            s.ga[rows, 256 * g : 256 * g + 256] = dot(
                s.gspr[rows, 128 * g : 128 * g + 128],
                s.bdm[128 * g : 128 * g + 128, 256 * g : 256 * g + 256],
            )

    def scatter_xy(src, buf, sem):
        def put(i):
            xx, yy = at_xy(i)
            return remote(
                src.at[xx * NY + yy], buf.at[i], sem.at[0, i], sem.at[1, i], dev_xy(xx, yy)
            )

        def start():
            each(KXY - 1, lambda i: put(i).start())

        def wait():
            each(KXY - 1, lambda i: put(i).wait_recv())

        def drain():
            each(KXY - 1, lambda i: put(i).wait_send())

        return start, wait, drain

    def gather_xy(buf, sem):
        def put(i):
            return remote(
                buf.at[own], buf.at[own], sem.at[0, i], sem.at[1, i], dev_xy(*at_xy(i))
            )

        def got(i):
            xx, yy = from_xy(i)
            f = c * KXY + xx * NY + yy
            return remote(buf.at[f], buf.at[f], sem.at[0, i], sem.at[1, i], dev_xy(xx, yy))

        def start():
            each(KXY - 1, lambda i: put(i).start())

        def wait():
            each(KXY - 1, lambda i: got(i).wait_recv())

        def drain():
            each(KXY - 1, lambda i: put(i).wait_send())

        return start, wait, drain

    def gather_core(buf, sem):
        mine, theirs = pl.ds(c * KXY, KXY), pl.ds((1 - c) * KXY, KXY)
        put = remote(buf.at[mine], buf.at[mine], sem.at[0], sem.at[1], other)
        got = remote(buf.at[theirs], buf.at[theirs], sem.at[0], sem.at[1], other)
        return put.start, got.wait_recv, put.wait_send

    gm = b_finish()
    dv = hdot(gm, att, (1, 0))
    datt = hdot(gm, v, (0, 0))
    dsc = att * (datt - jnp.sum(att * datt, axis=-1, keepdims=True)) * HD ** (-0.5)
    dq = hdot(kk, dsc, (1, 1))
    dk = hdot(q, dsc, (1, 0))
    dqkv = jnp.concatenate([dq, dk, dv], axis=0)
    tokenmap = hdot(tokens, dqkv, (1, 1))
    dtok = hdot(wt, dqkv, (1, 0))
    gsum = dtok * inv_mass
    s.b_m[y, 0:HD, :] = gsum
    s.b_m[y, HD:, :] = jnp.broadcast_to(-jnp.sum(gsum * tokens, axis=0, keepdims=True), (8, 128))
    bm_start()
    for e in early:
        e.st2_start()
    bm_wait()
    for j in range(PAIRS):
        s.bdg[64 * j : 64 * j + 64, 128 * j : 128 * j + 128] = spread_diag(s.b_m[j, 0:HD, :])
    gmass = jnp.concatenate([s.b_m[j, HD : HD + 1, :] for j in range(PAIRS)], axis=1)

    for r in range(0, ROWS, CH):
        rows = slice(r, r + CH)
        ga = s.ga[rows, :] + gmass
        ga = ga + jnp.concatenate(
            [
                dot(
                    s.feat[rows, 128 * g : 128 * g + 128],
                    s.bdg[128 * g : 128 * g + 128, 256 * g : 256 * g + 256],
                )
                for g in range(2)
            ],
            axis=1,
        )
        a = s.asg[rows, :]
        gl = (a * (ga - seg_sum(a * ga, s.ones[...])) * inv_sharp).astype(BF16)
        s.gl[rows, :] = gl
        s.gp[rows, :] = jnp.concatenate(
            [
                dot_t(
                    gl[:, 256 * g : 256 * g + 256],
                    s.bdw[128 * g : 128 * g + 128, 256 * g : 256 * g + 256],
                )
                for g in range(2)
            ],
            axis=1,
        ).astype(BF16)
        s.gf[rows, :] = jnp.concatenate(
            [
                dot_t(
                    s.ah[rows, 256 * g : 256 * g + 256],
                    s.bdg[128 * g : 128 * g + 128, 256 * g : 256 * g + 256],
                )
                for g in range(2)
            ],
            axis=1,
        ).astype(BF16)

    s.l_all[:, 0:8, :] = tdot(s.nh[...], s.gf[...]).reshape(32, 8, C)
    s.l_all[:, 8:16, :] = tdot(s.nh[...], s.gp[...]).reshape(32, 8, C)
    slices = jnp.zeros((HD, 128), F32)
    for g in range(2):
        t = tdot(s.proj[:, 128 * g : 128 * g + 128], s.gl[:, 256 * g : 256 * g + 256])
        for j in range(2):
            slices = slices + pack_diag(t[64 * j : 64 * j + 64, 128 * j : 128 * j + 128])
    tokenmap = jnp.where(z == 0, tokenmap, jnp.zeros_like(tokenmap))
    small = jnp.concatenate([slices, tokenmap, jnp.zeros((HD, 32), F32)], axis=1)
    for i in range(32):
        s.l_all[i, 16:17, :] = small[i : i + 1, :]
    l_core = remote(
        s.l_all.at[pl.ds((1 - c) * KXY, KXY)], s.l_core, s.l_cs.at[0], s.l_cs.at[1], other
    )
    l_core.start()

    l_core.wait_recv()

    def add_core_late(i):
        s.l_core[i] = s.l_core[i] + s.l_all[c * KXY + i]

    each(KXY, add_core_late)
    lx_start, lx_wait, lx_drain = scatter_xy(s.l_core, s.l_xy, s.l_xys)
    lx_start()

    for e in early:
        e.z_start()

    for r in range(0, ROWS, CH):
        rows = slice(r, r + CH)
        normed, inv = norm_rows(s.mp[rows, :].astype(F32))
        gn = dot_t(s.gf[rows, :], s.wa[...]) + dot_t(s.gp[rows, :], s.wp[...])
        s.pgr[rows, :] = (s.gres[rows, :] + norm_back(normed, inv, gn)).astype(BF16)
    write(s.pgr, o_pg)

    for e in early:
        e.zg_start()

    lx_wait()
    part = s.l_core[k]
    for i in range(KXY - 1):
        part = part + s.l_xy[i]
    s.l_z[z] = part

    def l_putz(i):
        return remote(
            s.l_z.at[z], s.l_z.at[z], s.l_zs.at[0, i], s.l_zs.at[1, i], dev_z(at_z(i))
        )

    def l_gotz(i):
        f = from_z(i)
        return remote(s.l_z.at[f], s.l_z.at[f], s.l_zs.at[0, i], s.l_zs.at[1, i], dev_z(f))

    each(NZ - 1, lambda i: l_putz(i).start())

    for e in early:
        e.st2g_start()
    each(NZ - 1, lambda i: l_gotz(i).wait_recv())
    total = s.l_z[0]
    for i in range(1, NZ):
        total = total + s.l_z[i]
    s.l_fin[own] = total * scale
    lg_start, lg_wait, lg_drain = gather_xy(s.l_fin, s.l_xygs)
    lg_start()

    for e in early:
        e.st1g_start()
    early[0].coreg_start()
    lg_wait()
    lc_start, lc_wait, lc_drain = gather_core(s.l_fin, s.l_cgs)
    lc_start()
    for e in early[1:]:
        e.coreg_start()
    for p, e in enumerate(early):
        e.coreg_wait()
        for b in range(2):
            write(
                e.uf.at[:, pl.ds(8 * b, 8), :], o_up.at[:, :, pl.ds(256 * (2 * p + b), 256)]
            )
        write(e.vf.at[:, pl.ds(0, 16), :], o_down.at[pl.ds(32 * p, 32)])
        if p == 0:
            write(e.vf.at[:, pl.ds(16, 8), :], o_out)
    lc_wait()
    write(s.l_fin.at[:, pl.ds(0, 8), :], o_feat)
    write(s.l_fin.at[:, pl.ds(8, 8), :], o_proj)
    rows = [s.l_fin[i, 16:17, :] for i in range(32)]
    small = jnp.concatenate(rows, axis=0)
    s.slc[...] = small[:, 0:SL] + small[:, SL : 2 * SL]
    s.tok[...] = small[:, 128 : 128 + 3 * HD]
    write(s.slc, o_slice)
    write(s.tok, o_tok)

    a_drain()
    am_drain()
    b_drain()
    bm_drain()
    l_core.wait_send()
    lx_drain()
    each(NZ - 1, lambda i: l_putz(i).wait_send())
    lg_drain()
    lc_drain()
    for e in early:
        e.drain()
    for copy in outs:
        copy.wait()


def store(*refs):
    held, outs, stage, sem = refs[:9], refs[9:18], refs[18:27], refs[27]
    loads = [pltpu.make_async_copy(held[i], stage[i], sem.at[0, i]) for i in range(9)]
    stores = [pltpu.make_async_copy(stage[i], outs[i], sem.at[1, i]) for i in range(9)]
    for copy in loads:
        copy.start()
    for i in range(9):
        loads[i].wait()
        stores[i].start()
    for copy in stores:
        copy.wait()


def body(mp, ls, wa, wp, ws, wt, wc, we, wd, sharp):
    scale = (lax.axis_size("dp") * lax.axis_size("point") * ROWS) ** (-0.5)
    hbm = pl.BlockSpec(memory_space=pltpu.HBM)
    results = (
        jax.ShapeDtypeStruct((ROWS, C), BF16),
        jax.ShapeDtypeStruct((ROWS, C), BF16),
        jax.ShapeDtypeStruct((32, 8, C), F32),
        jax.ShapeDtypeStruct((32, 8, C), F32),
        jax.ShapeDtypeStruct((HD, SL), F32),
        jax.ShapeDtypeStruct((HD, 3 * HD), F32),
        jax.ShapeDtypeStruct((32, 8, C), F32),
        jax.ShapeDtypeStruct((32, 8, FF), F32),
        jax.ShapeDtypeStruct((64, 16, C), F32),
    )
    held = pl.pallas_call(
        functools.partial(kernel, scale),
        out_shape=results,
        in_specs=[hbm] * 9 + [pl.BlockSpec(memory_space=pltpu.SMEM)],
        out_specs=(hbm,) * 9,
        scratch_shapes=list(SCRATCH.values()),
        compiler_params=pltpu.CompilerParams(
            collective_id=0, has_side_effects=True, vmem_limit_bytes=58 << 20
        ),
        name="layer",
    )(mp[0], ls[0], wa, wp, ws, wt, wc, we, wd, sharp)
    outs = pl.pallas_call(
        store,
        out_shape=results,
        in_specs=[hbm] * 9,
        out_specs=(hbm,) * 9,
        scratch_shapes=[pltpu.VMEM(r.shape, r.dtype) for r in results]
        + [pltpu.SemaphoreType.DMA((2, 9))],
        compiler_params=pltpu.CompilerParams(vmem_limit_bytes=58 << 20),
        name="store",
    )(*held)
    upd, pg, feat, proj, sl, tok, out, up, down = outs
    return (
        upd[None],
        pg[None],
        feat.reshape(C, C),
        proj.reshape(C, C),
        sl,
        tok,
        out.reshape(C, C),
        up.reshape(C, FF),
        down.reshape(FF, C),
    )


def solution(mesh):
    split = P("dp", "point", None)
    return jax.shard_map(
        body,
        mesh=mesh,
        in_specs=(split, split) + (P(),) * 8,
        out_specs=(split, split) + (P(),) * 7,
        check_vma=False,
    )
```

```python
import functools

import jax
import jax.numpy as jnp
from jax import lax
from jax.experimental import pallas as pl
from jax.experimental.pallas import tpu as pltpu
from jax.sharding import PartitionSpec as P

F32 = jnp.float32
BF16 = jnp.bfloat16
MESH = pl.DeviceIdType.MESH
EPS = 1e-05
GELU = 0.7978845608028654
HIGH = lax.Precision.HIGHEST

NX, NC, NZ, NY = 4, 2, 8, 4
ROWS = 512
C, FF, HEADS, HD, SL = 256, 1024, 8, 32, 64
PAIRS = 4
KXY = NX * NY
PARTS = ((16, 24), (16, 16))
LATE = (8, 9)
CH = 512


def dot(a, b):
    return jnp.dot(a, b, preferred_element_type=F32)


def dot_t(a, b):
    return lax.dot_general(a, b, (((1,), (1,)), ((), ())), preferred_element_type=F32)


def tdot(a, b):
    return lax.dot_general(a, b, (((0,), (0,)), ((), ())), preferred_element_type=F32)


def hdot(a, b, dims):
    return lax.dot_general(
        a, b, ((dims[:1], dims[1:]), ((), ())), precision=HIGH, preferred_element_type=F32
    )


def norm_rows(v):
    center = v - jnp.mean(v, axis=-1, keepdims=True)
    inv = lax.rsqrt(jnp.mean(center * center, axis=-1, keepdims=True) + EPS)
    return center * inv, inv


def norm_back(normed, inv, g):
    return inv * (
        g - jnp.mean(g, axis=-1, keepdims=True) - normed * jnp.mean(g * normed, axis=-1, keepdims=True)
    )


def seg_sum(v, ones):
    hi = v.astype(BF16)
    lo = (v - hi.astype(F32)).astype(BF16)
    return jnp.concatenate(
        [
            dot(hi[:, 256 * g : 256 * g + 256], ones) + dot(lo[:, 256 * g : 256 * g + 256], ones)
            for g in range(2)
        ],
        axis=1,
    )


def each(n, f):
    for i in range(n):
        f(i)


def remote(src, dst, ss, rs, dev):
    return pltpu.make_async_remote_copy(
        src_ref=src, dst_ref=dst, send_sem=ss, recv_sem=rs, device_id=dev, device_id_type=MESH
    )


def whole(ref, sem, n, dev):
    part = ref.at[pl.ds(0, n)]
    return remote(part, part, sem.at[0], sem.at[1], dev)


SCRATCH = dict(
    mp=pltpu.VMEM((ROWS, C), BF16),
    ls=pltpu.VMEM((ROWS, C), BF16),
    wa=pltpu.VMEM((C, C), BF16),
    wp=pltpu.VMEM((C, C), BF16),
    ws=pltpu.VMEM((HD, SL), BF16),
    wt=pltpu.VMEM((HD, 3 * HD), BF16),
    wc=pltpu.VMEM((C, C), BF16),
    we=pltpu.VMEM((C, FF), BF16),
    wd=pltpu.VMEM((FF, C), BF16),
    in_sem=pltpu.SemaphoreType.DMA((9,)),
    nh=pltpu.VMEM((ROWS, C), BF16),
    feat=pltpu.VMEM((ROWS, C), BF16),
    proj=pltpu.VMEM((ROWS, C), BF16),
    asg=pltpu.VMEM((ROWS, 512), F32),
    ah=pltpu.VMEM((ROWS, 512), BF16),
    bdw=pltpu.VMEM((C, 512), BF16),
    bdm=pltpu.VMEM((C, 512), BF16),
    bdg=pltpu.VMEM((C, 512), BF16),
    ones=pltpu.VMEM((256, 256), BF16),
    spread=pltpu.VMEM((ROWS, C), BF16),
    n2h=pltpu.VMEM((ROWS, C), BF16),
    act=pltpu.VMEM((ROWS, FF), BF16),
    gh=pltpu.VMEM((ROWS, FF), BF16),
    gres=pltpu.VMEM((ROWS, C), F32),
    grh=pltpu.VMEM((ROWS, C), BF16),
    gspr=pltpu.VMEM((ROWS, C), BF16),
    ga=pltpu.VMEM((ROWS, 512), F32),
    gl=pltpu.VMEM((ROWS, 512), BF16),
    gf=pltpu.VMEM((ROWS, C), BF16),
    gp=pltpu.VMEM((ROWS, C), BF16),
    upd=pltpu.VMEM((ROWS, C), BF16),
    pgr=pltpu.VMEM((ROWS, C), BF16),
    slc=pltpu.VMEM((HD, SL), F32),
    tok=pltpu.VMEM((HD, 3 * HD), F32),
    out_sem=pltpu.SemaphoreType.DMA((13,)),
    a_p=pltpu.VMEM((PAIRS, 33, 128), F32),
    a_y=pltpu.VMEM((3, 33, 128), F32),
    a_z=pltpu.VMEM((NZ, 33, 128), F32),
    a_m=pltpu.VMEM((PAIRS, HD, 128), F32),
    a_ys=pltpu.SemaphoreType.DMA((2,)),
    a_zs=pltpu.SemaphoreType.DMA((2,)),
    a_ms=pltpu.SemaphoreType.DMA((2,)),
    b_p=pltpu.VMEM((PAIRS, HD, 128), F32),
    b_y=pltpu.VMEM((3, HD, 128), F32),
    b_z=pltpu.VMEM((NZ, HD, 128), F32),
    b_m=pltpu.VMEM((PAIRS, 33, 128), F32),
    b_ys=pltpu.SemaphoreType.DMA((2,)),
    b_zs=pltpu.SemaphoreType.DMA((2,)),
    b_ms=pltpu.SemaphoreType.DMA((2,)),
)


def early_scratch(p, ru, rv):
    f = lambda *shape: pltpu.VMEM(shape + (C,), F32)
    d = lambda *shape: pltpu.SemaphoreType.DMA((2,) + shape)
    names = dict(
        u=f(32, ru), v=f(32, rv), uc=f(KXY, ru), vc=f(KXY, rv),
        ux=f(3, 4, ru), vy=f(3, 4, rv), u1=f(4, ru), v1=f(4, rv),
        uy=f(3, ru), vx=f(3, rv), part=f(ru + rv),
        z=pltpu.VMEM((NZ, 8, 128), F32), zo=f(NZ, 8), zf=f(32),
        uf=f(32, ru), vf=f(32, rv),
        us=d(4), vs=d(4), uxs=d(), vys=d(), uys=d(), vxs=d(),
        zs=d(), zos=d(), zgs=d(), uygs=d(), vxgs=d(), uxgs=d(3), vygs=d(3), ugs=d(4), vgs=d(4),
    )
    return {"e%d_%s" % (p, n): spec for n, spec in names.items()}


def late_scratch(p, r):
    f = lambda *shape: pltpu.VMEM(shape + (r, C), F32)
    d = lambda *shape: pltpu.SemaphoreType.DMA((2,) + shape)
    names = dict(
        all=f(32), half=f(KXY), xy=f(KXY - 1), z=f(NZ), fin=f(32),
        cs=d(), xys=d(), zs=d(), gs=d(), cgs=d(),
    )
    return {"l%d_%s" % (p, n): spec for n, spec in names.items()}


for p, rows in enumerate(LATE):
    SCRATCH.update(late_scratch(p, rows))
for p, rows in enumerate(PARTS):
    SCRATCH.update(early_scratch(p, *rows))


class Names:
    pass


class Axis:
    def __init__(self, n, me, dev):
        self.n, self.me, self.dev = n, me, dev

    def to(self, i):
        return lax.rem(self.me + i + 1, self.n)

    def frm(self, i):
        return lax.rem(self.me + self.n - 1 - i, self.n)


class Early:
    def __init__(self, s, p, rows, place, scale):
        for name in early_scratch(0, 1, 1):
            setattr(self, name[3:], getattr(s, "e%d_%s" % (p, name[3:])))
        self.ru, self.rv = rows
        self.out = self.rv > 16
        self.scale = scale
        x, c, z, y = place
        self.x, self.c, self.pz, self.y = x, c, z, y
        self.ax = Axis(NX, x, lambda t: (t * NC + c, z * NY + y))
        self.ay = Axis(NY, y, lambda t: (x * NC + c, z * NY + t))
        self.az = Axis(NZ, z, lambda t: (x * NC + c, t * NY + y))
        self.other = (x * NC + (1 - c), z * NY + y)
        self.first = ((self.ax, self.u, self.uc, self.ux, self.u1, self.us, self.uxs),
                      (self.ay, self.v, self.vc, self.vy, self.v1, self.vs, self.vys))
        self.second = ((self.ay, self.u1, self.uy, self.uys, 0, self.ru),
                       (self.ax, self.v1, self.vx, self.vxs, self.ru, self.rv))
        self.fin2 = ((self.ay, self.uf, 16 * c + 4 * x, self.uygs),
                     (self.ax, self.vf, 16 * c + 4 * y, self.vxgs))
        self.fin1 = ((self.ax, self.uf, self.uxgs, self.ugs), (self.ay, self.vf, self.vygs, self.vgs))
        self.sent = []

    def block(self, c, t):
        return pl.ds(16 * c + 4 * t, 4)

    def core_start(self):
        for o in (0, 1, 2, 3):
            for ax, full, half, _, _, sem, _ in self.first:
                self.core_copy(ax, full, half, sem, o).start()

    def core_copy(self, ax, full, half, sem, o):
        t = lax.rem(ax.me + 1 + o, 4)
        return remote(
            full.at[self.block(1 - self.c, t)], half.at[pl.ds(4 * t, 4)], sem.at[0, o], sem.at[1, o],
            self.other,
        )

    def st1_copy(self, ax, half, slots, sem, i):
        t = ax.to(i)
        return remote(half.at[pl.ds(4 * t, 4)], slots.at[i], sem.at[0], sem.at[1], ax.dev(t))

    def st1_start(self):
        for o in (0, 1, 2, 3):
            for ax, full, half, slots, _, sem, sem1 in self.first:
                self.core_copy(ax, full, half, sem, o).wait_recv()
                t = lax.rem(ax.me + 1 + o, 4)
                mine = pl.ds(4 * t, 4)
                half[mine] = half[mine] + full[self.block(self.c, t)]
                if o < 3:
                    self.st1_copy(ax, half, slots, sem1, o).start()

    def st2_copy(self, ax, src, slots, sem, i):
        t = ax.to(i)
        return remote(src.at[t], slots.at[i], sem.at[0], sem.at[1], ax.dev(t))

    def st2_start(self):
        for (ax, _, half, slots, one, _, sem1), (ax2, src, slots2, sem2, _, _) in zip(
            self.first, self.second
        ):
            whole(slots, sem1, 3, self.other).wait_recv()
            one[...] = half[pl.ds(4 * ax.me, 4)] + slots[0] + slots[1] + slots[2]
            for i in range(3):
                self.st2_copy(ax2, src, slots2, sem2, i).start()

    def tile(self, t):
        return (
            pl.ds(pl.multiple_of(8 * (t // 2), 8), 8),
            pl.ds(pl.multiple_of(128 * (t % 2), 128), 128),
        )

    def z_copy(self, i):
        t = self.az.to(i)
        rows, lanes = self.tile(t)
        return remote(
            self.part.at[rows, lanes], self.z.at[self.pz], self.zs.at[0], self.zs.at[1],
            self.az.dev(t),
        )

    def zo_copy(self, i):
        t = self.az.to(i)
        return remote(
            self.part.at[pl.ds(32, 8)], self.zo.at[self.pz], self.zos.at[0], self.zos.at[1],
            self.az.dev(t),
        )

    def z_start(self):
        for ax, src, slots, sem, at, n in self.second:
            whole(slots, sem, 3, self.other).wait_recv()
            self.part[at : at + n, :] = src[ax.me] + slots[0] + slots[1] + slots[2]
        each(7, lambda i: self.z_copy(i).start())
        rows, lanes = self.tile(self.pz)
        self.z[self.pz] = self.part[rows, lanes]
        if self.out:
            each(7, lambda i: self.zo_copy(i).start())
            self.zo[self.pz] = self.part[32:40, :]

    def zg_copy(self, i):
        piece = self.zf.at[self.tile(self.pz)]
        return remote(
            piece, piece, self.zgs.at[0], self.zgs.at[1], self.az.dev(self.az.to(i))
        )

    def zg_start(self):
        whole(self.z, self.zs, 7, self.other).wait_recv()
        total = self.z[0]
        for i in range(1, NZ):
            total = total + self.z[i]
        self.zf[self.tile(self.pz)] = total * self.scale
        each(7, lambda i: self.zg_copy(i).start())

    def fin2_copy(self, ax, fin, base, sem, i):
        piece = fin.at[base + ax.me]
        return remote(piece, piece, sem.at[0], sem.at[1], ax.dev(ax.to(i)))

    def st2g_start(self):
        own_u = 16 * self.c + 4 * self.x + self.y
        own_v = 16 * self.c + 4 * self.y + self.x
        if self.out:
            whole(self.zo, self.zos, 7, self.other).wait_recv()
            total = self.zo[0]
            for i in range(1, NZ):
                total = total + self.zo[i]
            self.vf[own_v, 16:24, :] = total * self.scale
        whole(self.z, self.zgs, 7, self.other).wait_recv()
        self.uf[own_u] = self.zf[0:16, :]
        self.vf[own_v, 0:16, :] = self.zf[16:32, :]
        for ax, fin, base, sem in self.fin2:
            for i in range(3):
                self.fin2_copy(ax, fin, base, sem, i).start()

    def fin1_copy(self, ax, fin, sem, i):
        piece = fin.at[self.block(self.c, ax.me)]
        return remote(piece, piece, sem.at[0, i], sem.at[1, i], ax.dev(ax.to(i)))

    def fin1_got(self, ax, fin, sem, i):
        f = ax.frm(i)
        piece = fin.at[self.block(self.c, f)]
        return remote(piece, piece, sem.at[0, i], sem.at[1, i], ax.dev(f))

    def coreg_copy(self, ax, fin, sem, o):
        piece = fin.at[self.block(self.c, lax.rem(ax.me + NX - o, 4))]
        return remote(piece, piece, sem.at[0, o], sem.at[1, o], self.other)

    def coreg_got(self, ax, fin, sem, o):
        piece = fin.at[self.block(1 - self.c, lax.rem(ax.me + NX - o, 4))]
        return remote(piece, piece, sem.at[0, o], sem.at[1, o], self.other)

    def st1g_start(self):
        for (ax2, fin, base, sem2), (ax, _, sem1, semc) in zip(self.fin2, self.fin1):
            whole(fin, sem2, 3, self.other).wait_recv()
            for i in range(3):
                self.fin1_copy(ax, fin, sem1, i).start()
            self.coreg_copy(ax, fin, semc, 0).start()

    def coreg_start(self):
        for i in (0, 2, 1):
            for ax, fin, sem1, semc in self.fin1:
                self.fin1_got(ax, fin, sem1, i).wait_recv()
                self.coreg_copy(ax, fin, semc, i + 1).start()

    def coreg_wait(self):
        for ax, fin, _, semc in self.fin1:
            for o in range(4):
                self.coreg_got(ax, fin, semc, o).wait_recv()

    def drain_sums(self):
        for (ax, full, half, slots, _, sem, sem1), (_, _, slots2, sem2, _, _) in zip(
            self.first, self.second
        ):
            for o in range(4):
                self.core_copy(ax, full, half, sem, o).wait_send()
            whole(slots, sem1, 3, self.other).wait_send()
            whole(slots2, sem2, 3, self.other).wait_send()

    def drain(self):
        whole(self.z, self.zs, 7, self.other).wait_send()
        whole(self.z, self.zgs, 7, self.other).wait_send()
        if self.out:
            whole(self.zo, self.zos, 7, self.other).wait_send()
        for (_, fin, _, sem2), (ax, _, sem1, semc) in zip(self.fin2, self.fin1):
            whole(fin, sem2, 3, self.other).wait_send()
            for i in range(3):
                self.fin1_copy(ax, fin, sem1, i).wait_send()
            for o in range(4):
                self.coreg_copy(ax, fin, semc, o).wait_send()


class Late:
    def __init__(self, s, p, place, scale):
        for name in late_scratch(0, 1):
            setattr(self, name[3:], getattr(s, "l%d_%s" % (p, name[3:])))
        self.scale = scale
        x, c, z, y = place
        self.x, self.c, self.pz, self.y = x, c, z, y
        self.k = x * NY + y
        self.own = c * KXY + self.k
        self.az = Axis(NZ, z, lambda t: (x * NC + c, t * NY + y))
        self.other = (x * NC + (1 - c), z * NY + y)

    def dev(self, xx, yy):
        return (xx * NC + self.c, self.pz * NY + yy)

    def to(self, i):
        j = i + 1
        return lax.rem(self.x + j // NY, NX), lax.rem(self.y + j % NY, NY)

    def core_copy(self):
        theirs = pl.ds((1 - self.c) * KXY, KXY)
        return remote(self.all.at[theirs], self.half, self.cs.at[0], self.cs.at[1], self.other)

    def core_start(self):
        self.core_copy().start()

    def xy_copy(self, i):
        xx, yy = self.to(i)
        return remote(
            self.half.at[xx * NY + yy], self.xy.at[i], self.xys.at[0], self.xys.at[1],
            self.dev(xx, yy),
        )

    def xy_start(self):
        self.core_copy().wait_recv()
        self.half[...] = self.half[...] + self.all[pl.ds(self.c * KXY, KXY)]
        each(KXY - 1, lambda i: self.xy_copy(i).start())

    def z_copy(self, i):
        piece = self.z.at[self.pz]
        return remote(
            piece, piece, self.zs.at[0], self.zs.at[1], self.az.dev(self.az.to(i))
        )

    def z_start(self):
        whole(self.xy, self.xys, KXY - 1, self.other).wait_recv()
        part = self.half[self.k]
        for i in range(KXY - 1):
            part = part + self.xy[i]
        self.z[self.pz] = part
        each(NZ - 1, lambda i: self.z_copy(i).start())

    def g_copy(self, i):
        piece = self.fin.at[self.own]
        return remote(piece, piece, self.gs.at[0], self.gs.at[1], self.dev(*self.to(i)))

    def g_start(self):
        whole(self.z, self.zs, NZ - 1, self.other).wait_recv()
        total = self.z[0]
        for i in range(1, NZ):
            total = total + self.z[i]
        self.fin[self.own] = total * self.scale
        each(KXY - 1, lambda i: self.g_copy(i).start())

    def c_copy(self, c):
        mine = self.fin.at[pl.ds(c * KXY, KXY)]
        return remote(mine, mine, self.cgs.at[0], self.cgs.at[1], self.other)

    def c_start(self):
        whole(self.fin, self.gs, KXY - 1, self.other).wait_recv()
        self.c_copy(self.c).start()

    def wait(self):
        self.c_copy(1 - self.c).wait_recv()

    def drain_sums(self):
        self.core_copy().wait_send()
        whole(self.xy, self.xys, KXY - 1, self.other).wait_send()

    def drain(self):
        whole(self.z, self.zs, NZ - 1, self.other).wait_send()
        whole(self.fin, self.gs, KXY - 1, self.other).wait_send()
        self.c_copy(self.c).wait_send()


def kernel(scale, *refs):
    ins, rest = refs[:10], refs[10:]
    (o_upd, o_pg, o_feat, o_proj, o_slice, o_tok, o_out, o_up, o_down) = rest[:9]
    s = Names()
    for name, ref in zip(SCRATCH, rest[9:]):
        setattr(s, name, ref)

    dp, pt = lax.axis_index("dp"), lax.axis_index("point")
    x, c = dp // NC, dp % NC
    z, y = pt // NY, pt % NY
    k = x * NY + y
    own = c * KXY + k
    other = (x * NC + (1 - c), pt)

    def at_y(i):
        return lax.rem(y + i + 1, NY)

    def from_y(i):
        return lax.rem(y + NY - 1 - i, NY)

    def at_z(i):
        return lax.rem(z + i + 1, NZ)

    def from_z(i):
        return lax.rem(z + NZ - 1 - i, NZ)

    def at_xy(i):
        j = i + 1
        return lax.rem(x + j // NY, NX), lax.rem(y + j % NY, NY)

    def from_xy(i):
        j = i + 1
        return lax.rem(x + NX - j // NY, NX), lax.rem(y + NY - j % NY, NY)

    def at_x(i):
        return lax.rem(x + i + 1, NX)

    def from_x(i):
        return lax.rem(x + NX - 1 - i, NX)

    def dev_x(xx):
        return (xx * NC + c, pt)

    def dev_y(yy):
        return (dp, z * NY + yy)

    def dev_z(zz):
        return (dp, zz * NY + y)

    def dev_xy(xx, yy):
        return (xx * NC + c, z * NY + yy)

    barrier = pltpu.get_barrier_semaphore()
    pl.semaphore_signal(barrier, inc=1, device_id=other, device_id_type=MESH)
    each(
        KXY - 1,
        lambda i: pl.semaphore_signal(
            barrier, inc=1, device_id=dev_xy(*at_xy(i)), device_id_type=MESH
        ),
    )
    each(
        NZ - 1,
        lambda i: pl.semaphore_signal(barrier, inc=1, device_id=dev_z(at_z(i)), device_id_type=MESH),
    )

    in_dst = (s.mp, s.ls, s.wa, s.wp, s.ws, s.wt, s.wc, s.we, s.wd)
    loads = [pltpu.make_async_copy(a, b, s.in_sem.at[i]) for i, (a, b) in enumerate(zip(ins, in_dst))]
    order = (0, 2, 3, 4, 5, 1, 6, 7, 8)
    for i in order:
        loads[i].start()
    sharp_ref = ins[9]

    lane = lax.broadcasted_iota(jnp.int32, (1, 512), 1)
    sharp = jnp.full((1, 512), sharp_ref[0], F32)
    for h in range(1, HEADS):
        sharp = jnp.where(lane // SL == h, sharp_ref[h], sharp)
    inv_sharp = 1.0 / sharp
    rr = lax.broadcasted_iota(jnp.int32, (256, 256), 0)
    cc = lax.broadcasted_iota(jnp.int32, (256, 256), 1)
    s.ones[...] = jnp.where(rr // SL == cc // SL, 1.0, 0.0).astype(BF16)
    s.bdm[...] = jnp.zeros_like(s.bdm)
    s.bdg[...] = jnp.zeros_like(s.bdg)
    low = lax.broadcasted_iota(jnp.int32, (HD, 128), 1) < SL

    def pack_diag(t):
        return jnp.where(low, t[:HD], t[HD:])

    def spread_diag(v):
        return jnp.concatenate([jnp.where(low, v, 0.0), jnp.where(low, 0.0, v)], axis=0).astype(BF16)

    loads[4].wait()
    w1 = s.ws[...].astype(F32)
    w2 = jnp.concatenate([w1, w1], axis=1)
    s.bdw[...] = jnp.zeros_like(s.bdw)
    for j in range(PAIRS):
        s.bdw[64 * j : 64 * j + 64, 128 * j : 128 * j + 128] = spread_diag(w2)

    for i in (0, 2, 3):
        loads[i].wait()
    mass = jnp.zeros((1, 512), F32)
    for r in range(0, ROWS, CH):
        rows = slice(r, r + CH)
        normed, _ = norm_rows(s.mp[rows, :].astype(F32))
        nh = normed.astype(BF16)
        s.nh[rows, :] = nh
        s.feat[rows, :] = dot(nh, s.wa[...]).astype(BF16)
        proj = dot(nh, s.wp[...]).astype(BF16)
        s.proj[rows, :] = proj
        logits = (
            jnp.concatenate(
                [
                    dot(
                        proj[:, 128 * g : 128 * g + 128],
                        s.bdw[128 * g : 128 * g + 128, 256 * g : 256 * g + 256],
                    )
                    for g in range(2)
                ],
                axis=1,
            )
            * inv_sharp
        )
        e = jnp.exp(logits)
        a = e / seg_sum(e, s.ones[...])
        s.asg[rows, :] = a
        s.ah[rows, :] = a.astype(BF16)
        mass = mass + jnp.sum(a, axis=0, keepdims=True)

    def head_sums(values, out):
        for g in range(2):
            t = tdot(values[:, 128 * g : 128 * g + 128], s.ah[:, 256 * g : 256 * g + 256])
            for j in range(2):
                out[2 * g + j, 0:HD, :] = pack_diag(
                    t[64 * j : 64 * j + 64, 128 * j : 128 * j + 128]
                )

    head_sums(s.feat, s.a_p)
    for j in range(PAIRS):
        s.a_p[j, HD:, :] = mass[:, 128 * j : 128 * j + 128]

    def reduce_pairs(part, buf_y, buf_z, sem_y, sem_z):
        def put_y(i):
            t = at_y(i)
            return remote(part.at[t], buf_y.at[i], sem_y.at[0], sem_y.at[1], dev_y(t))

        def put_z(i):
            return remote(
                buf_z.at[z], buf_z.at[z], sem_z.at[0], sem_z.at[1], dev_z(at_z(i))
            )

        def start():
            each(NY - 1, lambda i: put_y(i).start())

        def middle():
            whole(buf_y, sem_y, NY - 1, other).wait_recv()
            buf_z[z] = part[y] + buf_y[0] + buf_y[1] + buf_y[2]
            each(NZ - 1, lambda i: put_z(i).start())

        def finish():
            whole(buf_z, sem_z, NZ - 1, other).wait_recv()
            total = buf_z[0]
            for i in range(1, NZ):
                total = total + buf_z[i]
            return total

        def drain():
            whole(buf_y, sem_y, NY - 1, other).wait_send()
            whole(buf_z, sem_z, NZ - 1, other).wait_send()

        return start, middle, finish, drain

    def gather_pairs(buf, sem):
        def put(i):
            return remote(buf.at[y], buf.at[y], sem.at[0], sem.at[1], dev_y(at_y(i)))

        def start():
            each(NY - 1, lambda i: put(i).start())

        def wait():
            whole(buf, sem, NY - 1, other).wait_recv()

        def drain():
            whole(buf, sem, NY - 1, other).wait_send()

        return start, wait, drain

    pl.semaphore_wait(barrier, 1 + (KXY - 1) + (NZ - 1))
    a_start, a_middle, a_finish, a_drain = reduce_pairs(s.a_p, s.a_y, s.a_z, s.a_ys, s.a_zs)
    am_start, am_wait, am_drain = gather_pairs(s.a_m, s.a_ms)
    a_start()
    a_middle()
    for i in (5, 1, 6, 7, 8):
        loads[i].wait()
    total = a_finish()

    wt = s.wt[...].astype(F32)
    inv_mass = 1.0 / (total[HD : HD + 1] + EPS)
    tokens = total[:HD] * inv_mass
    qkv = hdot(wt, tokens, (0, 0))
    q, kk, v = qkv[:HD], qkv[HD : 2 * HD], qkv[2 * HD :]
    r2 = lax.broadcasted_iota(jnp.int32, (128, 128), 0) // SL
    c2 = lax.broadcasted_iota(jnp.int32, (128, 128), 1) // SL
    scores = hdot(q, kk, (0, 0)) * HD ** (-0.5)
    expo = jnp.where(r2 == c2, jnp.exp(jnp.where(r2 == c2, scores, 0.0)), 0.0)
    att = expo / jnp.sum(expo, axis=-1, keepdims=True)
    s.a_m[y] = hdot(v, att, (1, 1))
    am_start()
    am_wait()
    for j in range(PAIRS):
        s.bdm[64 * j : 64 * j + 64, 128 * j : 128 * j + 128] = spread_diag(s.a_m[j])

    for r in range(0, ROWS, CH):
        rows = slice(r, r + CH)
        spread = jnp.concatenate(
            [
                dot_t(
                    s.ah[rows, 256 * g : 256 * g + 256],
                    s.bdm[128 * g : 128 * g + 128, 256 * g : 256 * g + 256],
                )
                for g in range(2)
            ],
            axis=1,
        ).astype(BF16)
        s.spread[rows, :] = spread
        res = (s.mp[rows, :].astype(F32) + dot(spread, s.wc[...])).astype(BF16).astype(F32)
        n2, inv2 = norm_rows(res)
        n2h = n2.astype(BF16)
        s.n2h[rows, :] = n2h
        sens = s.ls[rows, :]
        upd = res
        gn2 = jnp.zeros((CH, C), F32)
        for f in range(0, FF, 256):
            hid = dot(n2h, s.we[:, f : f + 256])
            gact = dot_t(sens, s.wd[f : f + 256, :])
            h2 = hid * hid
            u = 0.5 + 0.5 * jnp.tanh(hid * (GELU + GELU * 0.044715 * h2))
            act = hid * u
            slope = u + act * (1.0 - u) * (2.0 * GELU + 6.0 * GELU * 0.044715 * h2)
            acth = act.astype(BF16)
            gh = (gact * slope).astype(BF16)
            s.act[rows, f : f + 256] = acth
            s.gh[rows, f : f + 256] = gh
            upd = upd + dot(acth, s.wd[f : f + 256, :])
            gn2 = gn2 + dot_t(gh, s.we[:, f : f + 256])
        s.upd[rows, :] = upd.astype(BF16)
        gres = sens.astype(F32) + norm_back(n2, inv2, gn2)
        s.gres[rows, :] = gres
        grh = gres.astype(BF16)
        s.grh[rows, :] = grh
        s.gspr[rows, :] = dot_t(grh, s.wc[...]).astype(BF16)

    head_sums(s.gspr, s.b_p)
    b_start, b_middle, b_finish, b_drain = reduce_pairs(s.b_p, s.b_y, s.b_z, s.b_ys, s.b_zs)
    bm_start, bm_wait, bm_drain = gather_pairs(s.b_m, s.b_ms)
    b_start()
    outs = []

    def write(src, dst):
        copy = pltpu.make_async_copy(src, dst, s.out_sem.at[len(outs)])
        copy.start()
        outs.append(copy)

    write(s.upd, o_upd)

    early = [Early(s, p, PARTS[p], (x, c, z, y), scale) for p in range(len(PARTS))]
    for p, e in enumerate(early):
        for b in range(2):
            f = 256 * (2 * p + b)
            e.u[:, 8 * b : 8 * b + 8, :] = tdot(s.n2h[...], s.gh[:, f : f + 256]).reshape(32, 8, C)
            e.v[16 * b : 16 * b + 16, 0:16, :] = tdot(s.act[:, f : f + 256], s.ls[...]).reshape(
                16, 16, C
            )
        if p == 0:
            e.v[:, 16:24, :] = tdot(s.spread[...], s.grh[...]).reshape(32, 8, C)
        e.core_start()
    early[0].st1_start()
    b_middle()

    for r in range(0, ROWS, CH):
        rows = slice(r, r + CH)
        for g in range(2):
            s.ga[rows, 256 * g : 256 * g + 256] = dot(
                s.gspr[rows, 128 * g : 128 * g + 128],
                s.bdm[128 * g : 128 * g + 128, 256 * g : 256 * g + 256],
            )

    early[1].st1_start()

    gm = b_finish()
    dv = hdot(gm, att, (1, 0))
    datt = hdot(gm, v, (0, 0))
    dsc = att * (datt - jnp.sum(att * datt, axis=-1, keepdims=True)) * HD ** (-0.5)
    dq = hdot(kk, dsc, (1, 1))
    dk = hdot(q, dsc, (1, 0))
    dqkv = jnp.concatenate([dq, dk, dv], axis=0)
    tokenmap = hdot(tokens, dqkv, (1, 1))
    dtok = hdot(wt, dqkv, (1, 0))
    gsum = dtok * inv_mass
    s.b_m[y, 0:HD, :] = gsum
    s.b_m[y, HD:, :] = -jnp.sum(gsum * tokens, axis=0, keepdims=True)
    bm_start()
    for e in early:
        e.st2_start()
    bm_wait()
    for j in range(PAIRS):
        s.bdg[64 * j : 64 * j + 64, 128 * j : 128 * j + 128] = spread_diag(s.b_m[j, 0:HD, :])
    gmass = jnp.concatenate([s.b_m[j, HD : HD + 1, :] for j in range(PAIRS)], axis=1)

    late = [Late(s, p, (x, c, z, y), scale) for p in range(len(LATE))]
    first, second = late
    early[0].z_start()
    s.gf[...] = jnp.concatenate(
        [
            dot_t(
                s.ah[:, 256 * g : 256 * g + 256],
                s.bdg[128 * g : 128 * g + 128, 256 * g : 256 * g + 256],
            )
            for g in range(2)
        ],
        axis=1,
    ).astype(BF16)
    first.all[...] = tdot(s.nh[...], s.gf[...]).reshape(32, 8, C)
    first.core_start()
    ga = s.ga[...] + gmass
    ga = ga + jnp.concatenate(
        [
            dot(
                s.feat[:, 128 * g : 128 * g + 128],
                s.bdg[128 * g : 128 * g + 128, 256 * g : 256 * g + 256],
            )
            for g in range(2)
        ],
        axis=1,
    )
    a = s.asg[...]
    gl = (a * (ga - seg_sum(a * ga, s.ones[...])) * inv_sharp).astype(BF16)
    s.gl[...] = gl
    s.gp[...] = jnp.concatenate(
        [
            dot_t(
                gl[:, 256 * g : 256 * g + 256],
                s.bdw[128 * g : 128 * g + 128, 256 * g : 256 * g + 256],
            )
            for g in range(2)
        ],
        axis=1,
    ).astype(BF16)
    second.all[:, 0:8, :] = tdot(s.nh[...], s.gp[...]).reshape(32, 8, C)
    slices = jnp.zeros((HD, 128), F32)
    for g in range(2):
        t = tdot(s.proj[:, 128 * g : 128 * g + 128], s.gl[:, 256 * g : 256 * g + 256])
        for j in range(2):
            slices = slices + pack_diag(t[64 * j : 64 * j + 64, 128 * j : 128 * j + 128])
    tokenmap = jnp.where(z == 0, tokenmap, jnp.zeros_like(tokenmap))
    small = jnp.concatenate([slices, tokenmap, jnp.zeros((HD, 32), F32)], axis=1)
    for i in range(32):
        second.all[i, 8:9, :] = small[i : i + 1, :]
    second.core_start()
    first.xy_start()
    second.xy_start()
    early[1].z_start()

    for r in range(0, ROWS, CH):
        rows = slice(r, r + CH)
        normed, inv = norm_rows(s.mp[rows, :].astype(F32))
        gn = dot_t(s.gf[rows, :], s.wa[...]) + dot_t(s.gp[rows, :], s.wp[...])
        s.pgr[rows, :] = (s.gres[rows, :] + norm_back(normed, inv, gn)).astype(BF16)
    write(s.pgr, o_pg)
    a_drain()
    am_drain()
    b_drain()
    bm_drain()
    for e in early:
        e.drain_sums()

    early[0].zg_start()
    first.z_start()
    early[1].zg_start()
    second.z_start()
    early[0].st2g_start()
    first.g_start()
    early[1].st2g_start()
    second.g_start()
    early[0].st1g_start()
    early[1].st1g_start()
    for part in late:
        part.drain_sums()
    first.c_start()
    second.c_start()
    early[0].coreg_start()
    early[1].coreg_start()
    for part in late:
        part.wait()
    write(first.fin, o_feat)
    write(second.fin.at[:, pl.ds(0, 8), :], o_proj)
    rows = [second.fin[i, 8:9, :] for i in range(32)]
    small = jnp.concatenate(rows, axis=0)
    s.slc[...] = small[:, 0:SL] + small[:, SL : 2 * SL]
    s.tok[...] = small[:, 128 : 128 + 3 * HD]
    write(s.slc, o_slice)
    write(s.tok, o_tok)
    for p, e in enumerate(early):
        e.coreg_wait()
        for b in range(2):
            write(
                e.uf.at[:, pl.ds(8 * b, 8), :], o_up.at[:, :, pl.ds(256 * (2 * p + b), 256)]
            )
        write(e.vf.at[:, pl.ds(0, 16), :], o_down.at[pl.ds(32 * p, 32)])
        if p == 0:
            write(e.vf.at[:, pl.ds(16, 8), :], o_out)
    for part in late:
        part.drain()
    for e in early:
        e.drain()
    for copy in outs:
        copy.wait()


def store(*refs):
    held, outs, stage, sem = refs[:9], refs[9:18], refs[18:27], refs[27]
    loads = [pltpu.make_async_copy(held[i], stage[i], sem.at[0, i]) for i in range(9)]
    stores = [pltpu.make_async_copy(stage[i], outs[i], sem.at[1, i]) for i in range(9)]
    for copy in loads:
        copy.start()
    for i in range(9):
        loads[i].wait()
        stores[i].start()
    for copy in stores:
        copy.wait()


def body(mp, ls, wa, wp, ws, wt, wc, we, wd, sharp):
    scale = (lax.axis_size("dp") * lax.axis_size("point") * ROWS) ** (-0.5)
    hbm = pl.BlockSpec(memory_space=pltpu.HBM)
    results = (
        jax.ShapeDtypeStruct((ROWS, C), BF16),
        jax.ShapeDtypeStruct((ROWS, C), BF16),
        jax.ShapeDtypeStruct((32, 8, C), F32),
        jax.ShapeDtypeStruct((32, 8, C), F32),
        jax.ShapeDtypeStruct((HD, SL), F32),
        jax.ShapeDtypeStruct((HD, 3 * HD), F32),
        jax.ShapeDtypeStruct((32, 8, C), F32),
        jax.ShapeDtypeStruct((32, 8, FF), F32),
        jax.ShapeDtypeStruct((64, 16, C), F32),
    )
    held = pl.pallas_call(
        functools.partial(kernel, scale),
        out_shape=results,
        in_specs=[hbm] * 9 + [pl.BlockSpec(memory_space=pltpu.SMEM)],
        out_specs=(hbm,) * 9,
        scratch_shapes=list(SCRATCH.values()),
        compiler_params=pltpu.CompilerParams(
            collective_id=0, has_side_effects=True, vmem_limit_bytes=58 << 20
        ),
        name="layer",
    )(mp[0], ls[0], wa, wp, ws, wt, wc, we, wd, sharp)
    outs = pl.pallas_call(
        store,
        out_shape=results,
        in_specs=[hbm] * 9,
        out_specs=(hbm,) * 9,
        scratch_shapes=[pltpu.VMEM(r.shape, r.dtype) for r in results]
        + [pltpu.SemaphoreType.DMA((2, 9))],
        compiler_params=pltpu.CompilerParams(vmem_limit_bytes=58 << 20),
        name="store",
    )(*held)
    upd, pg, feat, proj, sl, tok, out, up, down = outs
    return (
        upd[None],
        pg[None],
        feat.reshape(C, C),
        proj.reshape(C, C),
        sl,
        tok,
        out.reshape(C, C),
        up.reshape(C, FF),
        down.reshape(FF, C),
    )


def solution(mesh):
    split = P("dp", "point", None)
    return jax.shard_map(
        body,
        mesh=mesh,
        in_specs=(split, split) + (P(),) * 8,
        out_specs=(split, split) + (P(),) * 7,
        check_vma=False,
    )
```

```python
import functools

import jax
import jax.numpy as jnp
from jax import lax
from jax.experimental import pallas as pl
from jax.experimental.pallas import tpu as pltpu
from jax.sharding import PartitionSpec as P

F32 = jnp.float32
BF16 = jnp.bfloat16
MESH = pl.DeviceIdType.MESH
EPS = 1e-05
GELU = 0.7978845608028654
HIGH = lax.Precision.HIGHEST

NX, NC, NZ, NY = 4, 2, 8, 4
ROWS = 512
C, FF, HEADS, HD, SL = 256, 1024, 8, 32, 64
PAIRS = 4
KXY = NX * NY
PARTS = ((16, 24), (16, 16))
LATE = (9,)
CH = 512


def dot(a, b):
    return jnp.dot(a, b, preferred_element_type=F32)


def dot_t(a, b):
    return lax.dot_general(a, b, (((1,), (1,)), ((), ())), preferred_element_type=F32)


def tdot(a, b):
    return lax.dot_general(a, b, (((0,), (0,)), ((), ())), preferred_element_type=F32)


def hdot(a, b, dims):
    return lax.dot_general(
        a, b, ((dims[:1], dims[1:]), ((), ())), precision=HIGH, preferred_element_type=F32
    )


def norm_rows(v):
    center = v - jnp.mean(v, axis=-1, keepdims=True)
    inv = lax.rsqrt(jnp.mean(center * center, axis=-1, keepdims=True) + EPS)
    return center * inv, inv


def norm_back(normed, inv, g):
    return inv * (
        g - jnp.mean(g, axis=-1, keepdims=True) - normed * jnp.mean(g * normed, axis=-1, keepdims=True)
    )


def seg_sum(v, ones):
    hi = v.astype(BF16)
    lo = (v - hi.astype(F32)).astype(BF16)
    return jnp.concatenate(
        [
            dot(hi[:, 256 * g : 256 * g + 256], ones) + dot(lo[:, 256 * g : 256 * g + 256], ones)
            for g in range(2)
        ],
        axis=1,
    )


def each(n, f):
    for i in range(n):
        f(i)


def remote(src, dst, ss, rs, dev):
    return pltpu.make_async_remote_copy(
        src_ref=src, dst_ref=dst, send_sem=ss, recv_sem=rs, device_id=dev, device_id_type=MESH
    )


def whole(ref, sem, n, dev):
    part = ref.at[pl.ds(0, n)]
    return remote(part, part, sem.at[0], sem.at[1], dev)


SCRATCH = dict(
    mp=pltpu.VMEM((ROWS, C), BF16),
    ls=pltpu.VMEM((ROWS, C), BF16),
    wa=pltpu.VMEM((C, C), BF16),
    wp=pltpu.VMEM((C, C), BF16),
    ws=pltpu.VMEM((HD, SL), BF16),
    wt=pltpu.VMEM((HD, 3 * HD), BF16),
    wc=pltpu.VMEM((C, C), BF16),
    we=pltpu.VMEM((C, FF), BF16),
    wd=pltpu.VMEM((FF, C), BF16),
    in_sem=pltpu.SemaphoreType.DMA((9,)),
    nh=pltpu.VMEM((ROWS, C), BF16),
    feat=pltpu.VMEM((ROWS, C), BF16),
    proj=pltpu.VMEM((ROWS, C), BF16),
    asg=pltpu.VMEM((ROWS, 512), F32),
    ah=pltpu.VMEM((ROWS, 512), BF16),
    bdw=pltpu.VMEM((C, 512), BF16),
    bdm=pltpu.VMEM((C, 512), BF16),
    bdg=pltpu.VMEM((C, 512), BF16),
    ones=pltpu.VMEM((256, 256), BF16),
    spread=pltpu.VMEM((ROWS, C), BF16),
    n2h=pltpu.VMEM((ROWS, C), BF16),
    act=pltpu.VMEM((ROWS, FF), BF16),
    gh=pltpu.VMEM((ROWS, FF), BF16),
    gres=pltpu.VMEM((ROWS, C), F32),
    grh=pltpu.VMEM((ROWS, C), BF16),
    gspr=pltpu.VMEM((ROWS, C), BF16),
    ga=pltpu.VMEM((ROWS, 512), F32),
    gl=pltpu.VMEM((ROWS, 512), BF16),
    gf=pltpu.VMEM((ROWS, C), BF16),
    gp=pltpu.VMEM((ROWS, C), BF16),
    upd=pltpu.VMEM((ROWS, C), BF16),
    res=pltpu.VMEM((ROWS, C), BF16),
    pgr=pltpu.VMEM((ROWS, C), BF16),
    slc=pltpu.VMEM((HD, SL), F32),
    tok=pltpu.VMEM((HD, 3 * HD), F32),
    out_sem=pltpu.SemaphoreType.DMA((13,)),
    a_p=pltpu.VMEM((PAIRS, 33, 128), F32),
    a_y=pltpu.VMEM((3, 33, 128), F32),
    a_z=pltpu.VMEM((NZ, 33, 128), F32),
    a_m=pltpu.VMEM((PAIRS, HD, 128), F32),
    a_ys=pltpu.SemaphoreType.DMA((2,)),
    a_zs=pltpu.SemaphoreType.DMA((2,)),
    a_ms=pltpu.SemaphoreType.DMA((2,)),
    b_p=pltpu.VMEM((PAIRS, HD, 128), F32),
    b_y=pltpu.VMEM((3, HD, 128), F32),
    b_z=pltpu.VMEM((NZ, HD, 128), F32),
    b_m=pltpu.VMEM((PAIRS, 33, 128), F32),
    b_ys=pltpu.SemaphoreType.DMA((2,)),
    b_zs=pltpu.SemaphoreType.DMA((2,)),
    b_ms=pltpu.SemaphoreType.DMA((2,)),
)


def early_scratch(p, ru, rv):
    f = lambda *shape: pltpu.VMEM(shape + (C,), F32)
    d = lambda *shape: pltpu.SemaphoreType.DMA((2,) + shape)
    names = dict(
        u=f(32, ru), v=f(32, rv), uc=f(KXY, ru), vc=f(KXY, rv),
        ux=f(3, 4, ru), vy=f(3, 4, rv), u1=f(4, ru), v1=f(4, rv),
        uy=f(3, ru), vx=f(3, rv), part=f(ru + rv),
        z=pltpu.VMEM((NZ, 8, 128), F32), zo=f(NZ, 8), zf=f(32),
        uf=f(32, ru), vf=f(32, rv),
        us=d(4), vs=d(4), uxs=d(), vys=d(), uys=d(), vxs=d(),
        zs=d(), zos=d(), zgs=d(), uygs=d(), vxgs=d(), uxgs=d(3), vygs=d(3), ugs=d(4), vgs=d(4),
    )
    return {"e%d_%s" % (p, n): spec for n, spec in names.items()}


SCRATCH.update(
    n_all=pltpu.VMEM((PAIRS, C, 128), F32),
    n_y=pltpu.VMEM((3, C, 128), F32),
    n_sum=pltpu.VMEM((C, 128), F32),
    n_z=pltpu.VMEM((NZ, 32, 128), F32),
    f_own=pltpu.VMEM((16, 128), F32),
    f_core=pltpu.VMEM((16, 128), F32),
    f_x=pltpu.VMEM((NX, 16, 128), F32),
    f_all=pltpu.VMEM((NC, NY, NZ, 8, 128), F32),
    f_out=pltpu.VMEM((NZ, 4, 8, C), F32),
    n_ys=pltpu.SemaphoreType.DMA((2,)),
    n_zs=pltpu.SemaphoreType.DMA((2,)),
    f_cs=pltpu.SemaphoreType.DMA((2,)),
    f_xs=pltpu.SemaphoreType.DMA((2,)),
    f_zs=pltpu.SemaphoreType.DMA((2,)),
    f_ys=pltpu.SemaphoreType.DMA((2,)),
    f_gs=pltpu.SemaphoreType.DMA((2,)),
)


def late_scratch(p, r):
    f = lambda *shape: pltpu.VMEM(shape + (r, C), F32)
    d = lambda *shape: pltpu.SemaphoreType.DMA((2,) + shape)
    names = dict(
        all=f(32), half=f(KXY), xy=f(KXY - 1), z=f(NZ), fin=f(32),
        cs=d(), xys=d(), zs=d(), gs=d(), cgs=d(),
    )
    return {"l%d_%s" % (p, n): spec for n, spec in names.items()}


for p, rows in enumerate(LATE):
    SCRATCH.update(late_scratch(p, rows))
for p, rows in enumerate(PARTS):
    SCRATCH.update(early_scratch(p, *rows))


class Names:
    pass


class Axis:
    def __init__(self, n, me, dev):
        self.n, self.me, self.dev = n, me, dev

    def to(self, i):
        return lax.rem(self.me + i + 1, self.n)

    def frm(self, i):
        return lax.rem(self.me + self.n - 1 - i, self.n)


class Early:
    def __init__(self, s, p, rows, place, scale):
        for name in early_scratch(0, 1, 1):
            setattr(self, name[3:], getattr(s, "e%d_%s" % (p, name[3:])))
        self.ru, self.rv = rows
        self.out = self.rv > 16
        self.scale = scale
        x, c, z, y = place
        self.x, self.c, self.pz, self.y = x, c, z, y
        self.ax = Axis(NX, x, lambda t: (t * NC + c, z * NY + y))
        self.ay = Axis(NY, y, lambda t: (x * NC + c, z * NY + t))
        self.az = Axis(NZ, z, lambda t: (x * NC + c, t * NY + y))
        self.other = (x * NC + (1 - c), z * NY + y)
        self.first = ((self.ax, self.u, self.uc, self.ux, self.u1, self.us, self.uxs),
                      (self.ay, self.v, self.vc, self.vy, self.v1, self.vs, self.vys))
        self.second = ((self.ay, self.u1, self.uy, self.uys, 0, self.ru),
                       (self.ax, self.v1, self.vx, self.vxs, self.ru, self.rv))
        self.fin2 = ((self.ay, self.uf, 16 * c + 4 * x, self.uygs),
                     (self.ax, self.vf, 16 * c + 4 * y, self.vxgs))
        self.fin1 = ((self.ax, self.uf, self.uxgs, self.ugs), (self.ay, self.vf, self.vygs, self.vgs))
        self.sent = []

    def block(self, c, t):
        return pl.ds(16 * c + 4 * t, 4)

    def core_start(self):
        for o in (0, 1, 2, 3):
            for ax, full, half, _, _, sem, _ in self.first:
                self.core_copy(ax, full, half, sem, o).start()

    def core_copy(self, ax, full, half, sem, o):
        t = lax.rem(ax.me + 1 + o, 4)
        return remote(
            full.at[self.block(1 - self.c, t)], half.at[pl.ds(4 * t, 4)], sem.at[0, o], sem.at[1, o],
            self.other,
        )

    def st1_copy(self, ax, half, slots, sem, i):
        t = ax.to(i)
        return remote(half.at[pl.ds(4 * t, 4)], slots.at[i], sem.at[0], sem.at[1], ax.dev(t))

    def st1_start(self):
        for o in (0, 1, 2, 3):
            for ax, full, half, slots, _, sem, sem1 in self.first:
                self.core_copy(ax, full, half, sem, o).wait_recv()
                t = lax.rem(ax.me + 1 + o, 4)
                mine = pl.ds(4 * t, 4)
                half[mine] = half[mine] + full[self.block(self.c, t)]
                if o < 3:
                    self.st1_copy(ax, half, slots, sem1, o).start()

    def st2_copy(self, ax, src, slots, sem, i):
        t = ax.to(i)
        return remote(src.at[t], slots.at[i], sem.at[0], sem.at[1], ax.dev(t))

    def st2_start(self):
        for (ax, _, half, slots, one, _, sem1), (ax2, src, slots2, sem2, _, _) in zip(
            self.first, self.second
        ):
            whole(slots, sem1, 3, self.other).wait_recv()
            one[...] = half[pl.ds(4 * ax.me, 4)] + slots[0] + slots[1] + slots[2]
            for i in range(3):
                self.st2_copy(ax2, src, slots2, sem2, i).start()

    def tile(self, t):
        return (
            pl.ds(pl.multiple_of(8 * (t // 2), 8), 8),
            pl.ds(pl.multiple_of(128 * (t % 2), 128), 128),
        )

    def z_copy(self, i):
        t = self.az.to(i)
        rows, lanes = self.tile(t)
        return remote(
            self.part.at[rows, lanes], self.z.at[self.pz], self.zs.at[0], self.zs.at[1],
            self.az.dev(t),
        )

    def zo_copy(self, i):
        t = self.az.to(i)
        return remote(
            self.part.at[pl.ds(32, 8)], self.zo.at[self.pz], self.zos.at[0], self.zos.at[1],
            self.az.dev(t),
        )

    def z_start(self):
        for ax, src, slots, sem, at, n in self.second:
            whole(slots, sem, 3, self.other).wait_recv()
            self.part[at : at + n, :] = src[ax.me] + slots[0] + slots[1] + slots[2]
        each(7, lambda i: self.z_copy(i).start())
        rows, lanes = self.tile(self.pz)
        self.z[self.pz] = self.part[rows, lanes]
        if self.out:
            each(7, lambda i: self.zo_copy(i).start())
            self.zo[self.pz] = self.part[32:40, :]

    def zg_copy(self, i):
        piece = self.zf.at[self.tile(self.pz)]
        return remote(
            piece, piece, self.zgs.at[0], self.zgs.at[1], self.az.dev(self.az.to(i))
        )

    def zg_start(self):
        whole(self.z, self.zs, 7, self.other).wait_recv()
        total = self.z[0]
        for i in range(1, NZ):
            total = total + self.z[i]
        self.zf[self.tile(self.pz)] = total * self.scale
        each(7, lambda i: self.zg_copy(i).start())

    def fin2_copy(self, ax, fin, base, sem, i):
        piece = fin.at[base + ax.me]
        return remote(piece, piece, sem.at[0], sem.at[1], ax.dev(ax.to(i)))

    def st2g_start(self):
        own_u = 16 * self.c + 4 * self.x + self.y
        own_v = 16 * self.c + 4 * self.y + self.x
        if self.out:
            whole(self.zo, self.zos, 7, self.other).wait_recv()
            total = self.zo[0]
            for i in range(1, NZ):
                total = total + self.zo[i]
            self.vf[own_v, 16:24, :] = total * self.scale
        whole(self.z, self.zgs, 7, self.other).wait_recv()
        self.uf[own_u] = self.zf[0:16, :]
        self.vf[own_v, 0:16, :] = self.zf[16:32, :]
        for ax, fin, base, sem in self.fin2:
            for i in range(3):
                self.fin2_copy(ax, fin, base, sem, i).start()

    def fin1_copy(self, ax, fin, sem, i):
        piece = fin.at[self.block(self.c, ax.me)]
        return remote(piece, piece, sem.at[0, i], sem.at[1, i], ax.dev(ax.to(i)))

    def fin1_got(self, ax, fin, sem, i):
        f = ax.frm(i)
        piece = fin.at[self.block(self.c, f)]
        return remote(piece, piece, sem.at[0, i], sem.at[1, i], ax.dev(f))

    def coreg_copy(self, ax, fin, sem, o):
        piece = fin.at[self.block(self.c, lax.rem(ax.me + NX - o, 4))]
        return remote(piece, piece, sem.at[0, o], sem.at[1, o], self.other)

    def coreg_got(self, ax, fin, sem, o):
        piece = fin.at[self.block(1 - self.c, lax.rem(ax.me + NX - o, 4))]
        return remote(piece, piece, sem.at[0, o], sem.at[1, o], self.other)

    def st1g_start(self):
        for (ax2, fin, base, sem2), (ax, _, sem1, semc) in zip(self.fin2, self.fin1):
            whole(fin, sem2, 3, self.other).wait_recv()
            for i in range(3):
                self.fin1_copy(ax, fin, sem1, i).start()
            self.coreg_copy(ax, fin, semc, 0).start()

    def coreg_start(self):
        for i in (0, 2, 1):
            for ax, fin, sem1, semc in self.fin1:
                self.fin1_got(ax, fin, sem1, i).wait_recv()
                self.coreg_copy(ax, fin, semc, i + 1).start()

    def coreg_wait(self):
        for ax, fin, _, semc in self.fin1:
            for o in range(4):
                self.coreg_got(ax, fin, semc, o).wait_recv()

    def drain_sums(self):
        for (ax, full, half, slots, _, sem, sem1), (_, _, slots2, sem2, _, _) in zip(
            self.first, self.second
        ):
            for o in range(4):
                self.core_copy(ax, full, half, sem, o).wait_send()
            whole(slots, sem1, 3, self.other).wait_send()
            whole(slots2, sem2, 3, self.other).wait_send()

    def drain(self):
        whole(self.z, self.zs, 7, self.other).wait_send()
        whole(self.z, self.zgs, 7, self.other).wait_send()
        if self.out:
            whole(self.zo, self.zos, 7, self.other).wait_send()
        for (_, fin, _, sem2), (ax, _, sem1, semc) in zip(self.fin2, self.fin1):
            whole(fin, sem2, 3, self.other).wait_send()
            for i in range(3):
                self.fin1_copy(ax, fin, sem1, i).wait_send()
            for o in range(4):
                self.coreg_copy(ax, fin, semc, o).wait_send()


class Late:
    def __init__(self, s, p, place, scale):
        for name in late_scratch(0, 1):
            setattr(self, name[3:], getattr(s, "l%d_%s" % (p, name[3:])))
        self.scale = scale
        x, c, z, y = place
        self.x, self.c, self.pz, self.y = x, c, z, y
        self.k = x * NY + y
        self.own = c * KXY + self.k
        self.az = Axis(NZ, z, lambda t: (x * NC + c, t * NY + y))
        self.other = (x * NC + (1 - c), z * NY + y)

    def dev(self, xx, yy):
        return (xx * NC + self.c, self.pz * NY + yy)

    def to(self, i):
        j = i + 1
        return lax.rem(self.x + j // NY, NX), lax.rem(self.y + j % NY, NY)

    def core_copy(self):
        theirs = pl.ds((1 - self.c) * KXY, KXY)
        return remote(self.all.at[theirs], self.half, self.cs.at[0], self.cs.at[1], self.other)

    def core_start(self):
        self.core_copy().start()

    def xy_copy(self, i):
        xx, yy = self.to(i)
        return remote(
            self.half.at[xx * NY + yy], self.xy.at[i], self.xys.at[0], self.xys.at[1],
            self.dev(xx, yy),
        )

    def xy_start(self):
        self.core_copy().wait_recv()
        self.half[...] = self.half[...] + self.all[pl.ds(self.c * KXY, KXY)]
        each(KXY - 1, lambda i: self.xy_copy(i).start())

    def z_copy(self, i):
        piece = self.z.at[self.pz]
        return remote(
            piece, piece, self.zs.at[0], self.zs.at[1], self.az.dev(self.az.to(i))
        )

    def z_start(self):
        whole(self.xy, self.xys, KXY - 1, self.other).wait_recv()
        part = self.half[self.k]
        for i in range(KXY - 1):
            part = part + self.xy[i]
        self.z[self.pz] = part
        each(NZ - 1, lambda i: self.z_copy(i).start())

    def g_copy(self, i):
        piece = self.fin.at[self.own]
        return remote(piece, piece, self.gs.at[0], self.gs.at[1], self.dev(*self.to(i)))

    def g_start(self):
        whole(self.z, self.zs, NZ - 1, self.other).wait_recv()
        total = self.z[0]
        for i in range(1, NZ):
            total = total + self.z[i]
        self.fin[self.own] = total * self.scale
        each(KXY - 1, lambda i: self.g_copy(i).start())

    def c_copy(self, c):
        mine = self.fin.at[pl.ds(c * KXY, KXY)]
        return remote(mine, mine, self.cgs.at[0], self.cgs.at[1], self.other)

    def c_start(self):
        whole(self.fin, self.gs, KXY - 1, self.other).wait_recv()
        self.c_copy(self.c).start()

    def wait(self):
        self.c_copy(1 - self.c).wait_recv()

    def drain_sums(self):
        self.core_copy().wait_send()
        whole(self.xy, self.xys, KXY - 1, self.other).wait_send()

    def drain(self):
        whole(self.z, self.zs, NZ - 1, self.other).wait_send()
        whole(self.fin, self.gs, KXY - 1, self.other).wait_send()
        self.c_copy(self.c).wait_send()


def kernel(scale, *refs):
    ins, rest = refs[:10], refs[10:]
    (o_upd, o_pg, o_feat, o_proj, o_slice, o_tok, o_out, o_up, o_down) = rest[:9]
    s = Names()
    for name, ref in zip(SCRATCH, rest[9:]):
        setattr(s, name, ref)

    dp, pt = lax.axis_index("dp"), lax.axis_index("point")
    x, c = dp // NC, dp % NC
    z, y = pt // NY, pt % NY
    k = x * NY + y
    own = c * KXY + k
    other = (x * NC + (1 - c), pt)

    def at_y(i):
        return lax.rem(y + i + 1, NY)

    def from_y(i):
        return lax.rem(y + NY - 1 - i, NY)

    def at_z(i):
        return lax.rem(z + i + 1, NZ)

    def from_z(i):
        return lax.rem(z + NZ - 1 - i, NZ)

    def at_xy(i):
        j = i + 1
        return lax.rem(x + j // NY, NX), lax.rem(y + j % NY, NY)

    def from_xy(i):
        j = i + 1
        return lax.rem(x + NX - j // NY, NX), lax.rem(y + NY - j % NY, NY)

    def at_x(i):
        return lax.rem(x + i + 1, NX)

    def from_x(i):
        return lax.rem(x + NX - 1 - i, NX)

    def dev_x(xx):
        return (xx * NC + c, pt)

    def dev_y(yy):
        return (dp, z * NY + yy)

    def dev_z(zz):
        return (dp, zz * NY + y)

    def dev_xy(xx, yy):
        return (xx * NC + c, z * NY + yy)

    barrier = pltpu.get_barrier_semaphore()
    pl.semaphore_signal(barrier, inc=1, device_id=other, device_id_type=MESH)
    each(
        KXY - 1,
        lambda i: pl.semaphore_signal(
            barrier, inc=1, device_id=dev_xy(*at_xy(i)), device_id_type=MESH
        ),
    )
    each(
        NZ - 1,
        lambda i: pl.semaphore_signal(barrier, inc=1, device_id=dev_z(at_z(i)), device_id_type=MESH),
    )

    in_dst = (s.mp, s.ls, s.wa, s.wp, s.ws, s.wt, s.wc, s.we, s.wd)
    loads = [pltpu.make_async_copy(a, b, s.in_sem.at[i]) for i, (a, b) in enumerate(zip(ins, in_dst))]
    order = (0, 2, 3, 4, 5, 1, 6, 7, 8)
    for i in order:
        loads[i].start()
    sharp_ref = ins[9]

    lane = lax.broadcasted_iota(jnp.int32, (1, 512), 1)
    sharp = jnp.full((1, 512), sharp_ref[0], F32)
    for h in range(1, HEADS):
        sharp = jnp.where(lane // SL == h, sharp_ref[h], sharp)
    inv_sharp = 1.0 / sharp
    rr = lax.broadcasted_iota(jnp.int32, (256, 256), 0)
    cc = lax.broadcasted_iota(jnp.int32, (256, 256), 1)
    s.ones[...] = jnp.where(rr // SL == cc // SL, 1.0, 0.0).astype(BF16)
    s.bdm[...] = jnp.zeros_like(s.bdm)
    s.bdg[...] = jnp.zeros_like(s.bdg)
    low = lax.broadcasted_iota(jnp.int32, (HD, 128), 1) < SL

    def pack_diag(t):
        return jnp.where(low, t[:HD], t[HD:])

    def spread_diag(v):
        return jnp.concatenate([jnp.where(low, v, 0.0), jnp.where(low, 0.0, v)], axis=0).astype(BF16)

    loads[4].wait()
    w1 = s.ws[...].astype(F32)
    w2 = jnp.concatenate([w1, w1], axis=1)
    s.bdw[...] = jnp.zeros_like(s.bdw)
    for j in range(PAIRS):
        s.bdw[64 * j : 64 * j + 64, 128 * j : 128 * j + 128] = spread_diag(w2)

    for i in (0, 2, 3):
        loads[i].wait()
    mass = jnp.zeros((1, 512), F32)
    for r in range(0, ROWS, CH):
        rows = slice(r, r + CH)
        normed, _ = norm_rows(s.mp[rows, :].astype(F32))
        nh = normed.astype(BF16)
        s.nh[rows, :] = nh
        s.feat[rows, :] = dot(nh, s.wa[...]).astype(BF16)
        proj = dot(nh, s.wp[...]).astype(BF16)
        s.proj[rows, :] = proj
        logits = (
            jnp.concatenate(
                [
                    dot(
                        proj[:, 128 * g : 128 * g + 128],
                        s.bdw[128 * g : 128 * g + 128, 256 * g : 256 * g + 256],
                    )
                    for g in range(2)
                ],
                axis=1,
            )
            * inv_sharp
        )
        e = jnp.exp(logits)
        a = e / seg_sum(e, s.ones[...])
        s.asg[rows, :] = a
        s.ah[rows, :] = a.astype(BF16)
        mass = mass + jnp.sum(a, axis=0, keepdims=True)

    def head_sums(values, out):
        for g in range(2):
            t = tdot(values[:, 128 * g : 128 * g + 128], s.ah[:, 256 * g : 256 * g + 256])
            for j in range(2):
                out[2 * g + j, 0:HD, :] = pack_diag(
                    t[64 * j : 64 * j + 64, 128 * j : 128 * j + 128]
                )

    head_sums(s.feat, s.a_p)
    for j in range(PAIRS):
        s.a_p[j, HD:, :] = mass[:, 128 * j : 128 * j + 128]

    def reduce_pairs(part, buf_y, buf_z, sem_y, sem_z):
        def put_y(i):
            t = at_y(i)
            return remote(part.at[t], buf_y.at[i], sem_y.at[0], sem_y.at[1], dev_y(t))

        def put_z(i):
            return remote(
                buf_z.at[z], buf_z.at[z], sem_z.at[0], sem_z.at[1], dev_z(at_z(i))
            )

        def start():
            each(NY - 1, lambda i: put_y(i).start())

        def middle():
            whole(buf_y, sem_y, NY - 1, other).wait_recv()
            buf_z[z] = part[y] + buf_y[0] + buf_y[1] + buf_y[2]
            each(NZ - 1, lambda i: put_z(i).start())

        def finish():
            whole(buf_z, sem_z, NZ - 1, other).wait_recv()
            total = buf_z[0]
            for i in range(1, NZ):
                total = total + buf_z[i]
            return total

        def drain():
            whole(buf_y, sem_y, NY - 1, other).wait_send()
            whole(buf_z, sem_z, NZ - 1, other).wait_send()

        return start, middle, finish, drain

    def gather_pairs(buf, sem):
        def put(i):
            return remote(buf.at[y], buf.at[y], sem.at[0], sem.at[1], dev_y(at_y(i)))

        def start():
            each(NY - 1, lambda i: put(i).start())

        def wait():
            whole(buf, sem, NY - 1, other).wait_recv()

        def drain():
            whole(buf, sem, NY - 1, other).wait_send()

        return start, wait, drain

    pl.semaphore_wait(barrier, 1 + (KXY - 1) + (NZ - 1))
    a_start, a_middle, a_finish, a_drain = reduce_pairs(s.a_p, s.a_y, s.a_z, s.a_ys, s.a_zs)
    am_start, am_wait, am_drain = gather_pairs(s.a_m, s.a_ms)
    a_start()
    a_middle()

    for g in range(2):
        t = tdot(s.nh[...], s.ah[:, 256 * g : 256 * g + 256])
        for j in range(2):
            s.n_all[2 * g + j] = t[:, 128 * j : 128 * j + 128]

    def n_puty(i):
        t = at_y(i)
        return remote(s.n_all.at[t], s.n_y.at[i], s.n_ys.at[0], s.n_ys.at[1], dev_y(t))

    def n_putz(i):
        t = at_z(i)
        rows = pl.ds(pl.multiple_of(32 * t, 32), 32)
        return remote(s.n_sum.at[rows], s.n_z.at[z], s.n_zs.at[0], s.n_zs.at[1], dev_z(t))

    each(NY - 1, lambda i: n_puty(i).start())
    for i in (5, 1, 6, 7, 8):
        loads[i].wait()
    total = a_finish()

    wt = s.wt[...].astype(F32)
    inv_mass = 1.0 / (total[HD : HD + 1] + EPS)
    tokens = total[:HD] * inv_mass
    qkv = hdot(wt, tokens, (0, 0))
    q, kk, v = qkv[:HD], qkv[HD : 2 * HD], qkv[2 * HD :]
    r2 = lax.broadcasted_iota(jnp.int32, (128, 128), 0) // SL
    c2 = lax.broadcasted_iota(jnp.int32, (128, 128), 1) // SL
    scores = hdot(q, kk, (0, 0)) * HD ** (-0.5)
    expo = jnp.where(r2 == c2, jnp.exp(jnp.where(r2 == c2, scores, 0.0)), 0.0)
    att = expo / jnp.sum(expo, axis=-1, keepdims=True)
    s.a_m[y] = hdot(v, att, (1, 1))
    am_start()
    am_wait()
    for j in range(PAIRS):
        s.bdm[64 * j : 64 * j + 64, 128 * j : 128 * j + 128] = spread_diag(s.a_m[j])

    whole(s.n_y, s.n_ys, NY - 1, other).wait_recv()
    s.n_sum[...] = s.n_all[y] + s.n_y[0] + s.n_y[1] + s.n_y[2]
    each(NZ - 1, lambda i: n_putz(i).start())
    s.n_z[z] = s.n_sum[pl.ds(pl.multiple_of(32 * z, 32), 32), :]

    for r in range(0, ROWS, CH):
        rows = slice(r, r + CH)
        spread = jnp.concatenate(
            [
                dot_t(
                    s.ah[rows, 256 * g : 256 * g + 256],
                    s.bdm[128 * g : 128 * g + 128, 256 * g : 256 * g + 256],
                )
                for g in range(2)
            ],
            axis=1,
        ).astype(BF16)
        s.spread[rows, :] = spread
        res = (s.mp[rows, :].astype(F32) + dot(spread, s.wc[...])).astype(BF16).astype(F32)
        n2, inv2 = norm_rows(res)
        n2h = n2.astype(BF16)
        s.n2h[rows, :] = n2h
        sens = s.ls[rows, :]
        s.res[rows, :] = res.astype(BF16)
        gn2 = jnp.zeros((CH, C), F32)
        for f in range(0, FF, 256):
            hid = dot(n2h, s.we[:, f : f + 256])
            gact = dot_t(sens, s.wd[f : f + 256, :])
            h2 = hid * hid
            u = 0.5 + 0.5 * jnp.tanh(hid * (GELU + GELU * 0.044715 * h2))
            act = hid * u
            slope = u + act * (1.0 - u) * (2.0 * GELU + 6.0 * GELU * 0.044715 * h2)
            acth = act.astype(BF16)
            gh = (gact * slope).astype(BF16)
            s.act[rows, f : f + 256] = acth
            s.gh[rows, f : f + 256] = gh
            gn2 = gn2 + dot_t(gh, s.we[:, f : f + 256])
        gres = sens.astype(F32) + norm_back(n2, inv2, gn2)
        s.gres[rows, :] = gres
        grh = gres.astype(BF16)
        s.grh[rows, :] = grh
        s.gspr[rows, :] = dot_t(grh, s.wc[...]).astype(BF16)

    head_sums(s.gspr, s.b_p)
    b_start, b_middle, b_finish, b_drain = reduce_pairs(s.b_p, s.b_y, s.b_z, s.b_ys, s.b_zs)
    bm_start, bm_wait, bm_drain = gather_pairs(s.b_m, s.b_ms)
    b_start()
    outs = []

    def write(src, dst):
        copy = pltpu.make_async_copy(src, dst, s.out_sem.at[len(outs)])
        copy.start()
        outs.append(copy)


    early = [Early(s, p, PARTS[p], (x, c, z, y), scale) for p in range(len(PARTS))]
    for p, e in enumerate(early):
        for b in range(2):
            f = 256 * (2 * p + b)
            e.u[:, 8 * b : 8 * b + 8, :] = tdot(s.n2h[...], s.gh[:, f : f + 256]).reshape(32, 8, C)
            e.v[16 * b : 16 * b + 16, 0:16, :] = tdot(s.act[:, f : f + 256], s.ls[...]).reshape(
                16, 16, C
            )
        if p == 0:
            e.v[:, 16:24, :] = tdot(s.spread[...], s.grh[...]).reshape(32, 8, C)
        e.core_start()
    early[0].st1_start()
    b_middle()

    for r in range(0, ROWS, CH):
        rows = slice(r, r + CH)
        for g in range(2):
            s.ga[rows, 256 * g : 256 * g + 256] = dot(
                s.gspr[rows, 128 * g : 128 * g + 128],
                s.bdm[128 * g : 128 * g + 128, 256 * g : 256 * g + 256],
            )

    early[1].st1_start()
    s.upd[...] = (s.res[...].astype(F32) + dot(s.act[...], s.wd[...])).astype(BF16)
    write(s.upd, o_upd)

    gm = b_finish()
    dv = hdot(gm, att, (1, 0))
    datt = hdot(gm, v, (0, 0))
    dsc = att * (datt - jnp.sum(att * datt, axis=-1, keepdims=True)) * HD ** (-0.5)
    dq = hdot(kk, dsc, (1, 1))
    dk = hdot(q, dsc, (1, 0))
    dqkv = jnp.concatenate([dq, dk, dv], axis=0)
    tokenmap = hdot(tokens, dqkv, (1, 1))
    dtok = hdot(wt, dqkv, (1, 0))
    gsum = dtok * inv_mass
    s.b_m[y, 0:HD, :] = gsum
    s.b_m[y, HD:, :] = -jnp.sum(gsum * tokens, axis=0, keepdims=True)
    bm_start()

    whole(s.n_z, s.n_zs, NZ - 1, other).wait_recv()
    nsum = s.n_z[0]
    for i in range(1, NZ):
        nsum = nsum + s.n_z[i]
    nhi = nsum.astype(BF16)
    nlo = (nsum - nhi.astype(F32)).astype(BF16)
    gsd = spread_diag(gsum)
    fblock = dot_t(nhi, gsd) + dot_t(nlo, gsd)
    s.f_own[...] = jnp.concatenate([fblock[:16], fblock[16:]], axis=1)
    f_core = remote(s.f_own, s.f_core, s.f_cs.at[0], s.f_cs.at[1], other)
    f_core.start()

    def f_putx(i):
        t = lax.rem(x + i + 1, NX)
        piece = s.f_x.at[x]
        return remote(piece, piece, s.f_xs.at[0], s.f_xs.at[1], (t * NC + c, pt))

    def f_x_start():
        f_core.wait_recv()
        s.f_x[x] = s.f_own[...] + s.f_core[...]
        each(NX - 1, lambda i: f_putx(i).start())

    def f_putz(i):
        piece = s.f_all.at[c, y, z]
        return remote(piece, piece, s.f_zs.at[0], s.f_zs.at[1], dev_z(at_z(i)))

    def f_z_start():
        whole(s.f_x, s.f_xs, NX - 1, other).wait_recv()
        half = pl.ds(pl.multiple_of(8 * c, 8), 8)
        total = s.f_x[0, half, :] + s.f_x[1, half, :] + s.f_x[2, half, :] + s.f_x[3, half, :]
        s.f_all[c, y, z] = total * scale
        each(NZ - 1, lambda i: f_putz(i).start())

    def f_puty(i):
        piece = s.f_all.at[c, y]
        return remote(piece, piece, s.f_ys.at[0], s.f_ys.at[1], dev_y(at_y(i)))

    def f_y_start():
        whole(s.f_all.at[0, 0], s.f_zs, NZ - 1, other).wait_recv()
        each(NY - 1, lambda i: f_puty(i).start())

    def f_give(core):
        piece = s.f_all.at[core]
        return remote(piece, piece, s.f_gs.at[0], s.f_gs.at[1], other)

    def f_give_start():
        whole(s.f_all.at[0], s.f_ys, NY - 1, other).wait_recv()
        f_give(c).start()

    def f_finish():
        f_give(1 - c).wait_recv()
        left = lax.broadcasted_iota(jnp.int32, (64, 128), 1) < 64
        for core in range(NC):
            for j in range(2):
                a0 = s.f_all[core, 2 * j].reshape(64, 128)
                a1 = s.f_all[core, 2 * j + 1].reshape(64, 128)
                lo = jnp.where(left, a0, pltpu.roll(a1, 64, 1))
                hi = jnp.where(left, pltpu.roll(a0, 64, 1), a1)
                lanes = slice(128 * j, 128 * j + 128)
                s.f_out[:, core, :, lanes] = lo.reshape(NZ, 8, 128)
                s.f_out[:, 2 + core, :, lanes] = hi.reshape(NZ, 8, 128)

    def f_drain():
        whole(s.n_y, s.n_ys, NY - 1, other).wait_send()
        whole(s.n_z, s.n_zs, NZ - 1, other).wait_send()
        f_core.wait_send()
        whole(s.f_x, s.f_xs, NX - 1, other).wait_send()
        whole(s.f_all.at[0, 0], s.f_zs, NZ - 1, other).wait_send()
        whole(s.f_all.at[0], s.f_ys, NY - 1, other).wait_send()
        f_give(c).wait_send()

    for e in early:
        e.st2_start()
    f_x_start()
    bm_wait()
    for j in range(PAIRS):
        s.bdg[64 * j : 64 * j + 64, 128 * j : 128 * j + 128] = spread_diag(s.b_m[j, 0:HD, :])
    gmass = jnp.concatenate([s.b_m[j, HD : HD + 1, :] for j in range(PAIRS)], axis=1)

    late = [Late(s, p, (x, c, z, y), scale) for p in range(len(LATE))]
    second = late[0]
    early[0].z_start()
    ga = s.ga[...] + gmass
    ga = ga + jnp.concatenate(
        [
            dot(
                s.feat[:, 128 * g : 128 * g + 128],
                s.bdg[128 * g : 128 * g + 128, 256 * g : 256 * g + 256],
            )
            for g in range(2)
        ],
        axis=1,
    )
    a = s.asg[...]
    gl = (a * (ga - seg_sum(a * ga, s.ones[...])) * inv_sharp).astype(BF16)
    s.gl[...] = gl
    s.gp[...] = jnp.concatenate(
        [
            dot_t(
                gl[:, 256 * g : 256 * g + 256],
                s.bdw[128 * g : 128 * g + 128, 256 * g : 256 * g + 256],
            )
            for g in range(2)
        ],
        axis=1,
    ).astype(BF16)
    second.all[:, 0:8, :] = tdot(s.nh[...], s.gp[...]).reshape(32, 8, C)
    slices = jnp.zeros((HD, 128), F32)
    for g in range(2):
        t = tdot(s.proj[:, 128 * g : 128 * g + 128], s.gl[:, 256 * g : 256 * g + 256])
        for j in range(2):
            slices = slices + pack_diag(t[64 * j : 64 * j + 64, 128 * j : 128 * j + 128])
    tokenmap = jnp.where(z == 0, tokenmap, jnp.zeros_like(tokenmap))
    small = jnp.concatenate([slices, tokenmap, jnp.zeros((HD, 32), F32)], axis=1)
    for i in range(32):
        second.all[i, 8:9, :] = small[i : i + 1, :]
    second.core_start()
    f_z_start()
    second.xy_start()
    early[1].z_start()
    s.gf[...] = jnp.concatenate(
        [
            dot_t(
                s.ah[:, 256 * g : 256 * g + 256],
                s.bdg[128 * g : 128 * g + 128, 256 * g : 256 * g + 256],
            )
            for g in range(2)
        ],
        axis=1,
    ).astype(BF16)

    for r in range(0, ROWS, CH):
        rows = slice(r, r + CH)
        normed, inv = norm_rows(s.mp[rows, :].astype(F32))
        gn = dot_t(s.gf[rows, :], s.wa[...]) + dot_t(s.gp[rows, :], s.wp[...])
        s.pgr[rows, :] = (s.gres[rows, :] + norm_back(normed, inv, gn)).astype(BF16)
    write(s.pgr, o_pg)
    a_drain()
    am_drain()
    b_drain()
    bm_drain()
    for e in early:
        e.drain_sums()

    early[0].zg_start()
    f_y_start()
    early[1].zg_start()
    second.z_start()
    early[0].st2g_start()
    f_give_start()
    early[1].st2g_start()
    second.g_start()
    early[0].st1g_start()
    early[1].st1g_start()
    f_finish()
    write(s.f_out, o_feat)
    f_drain()
    for part in late:
        part.drain_sums()
    second.c_start()
    early[0].coreg_start()
    early[1].coreg_start()
    for part in late:
        part.wait()
    write(second.fin.at[:, pl.ds(0, 8), :], o_proj)
    rows = [second.fin[i, 8:9, :] for i in range(32)]
    small = jnp.concatenate(rows, axis=0)
    s.slc[...] = small[:, 0:SL] + small[:, SL : 2 * SL]
    s.tok[...] = small[:, 128 : 128 + 3 * HD]
    write(s.slc, o_slice)
    write(s.tok, o_tok)
    for p, e in enumerate(early):
        e.coreg_wait()
        for b in range(2):
            write(
                e.uf.at[:, pl.ds(8 * b, 8), :], o_up.at[:, :, pl.ds(256 * (2 * p + b), 256)]
            )
        write(e.vf.at[:, pl.ds(0, 16), :], o_down.at[pl.ds(32 * p, 32)])
        if p == 0:
            write(e.vf.at[:, pl.ds(16, 8), :], o_out)
    for part in late:
        part.drain()
    for e in early:
        e.drain()
    for copy in outs:
        copy.wait()


def store(*refs):
    held, outs, stage, sem = refs[:9], refs[9:18], refs[18:27], refs[27]
    parts = [(7, pl.ds(8 * q, 8)) for q in range(4)]
    parts += [(8, pl.ds(16 * q, 16)) for q in range(4)]
    parts += [(i, pl.ds(0, held[i].shape[0])) for i in (0, 1, 2, 3, 6, 4, 5)]
    loads, stores = [], []
    for n, (i, rows) in enumerate(parts):
        piece = stage[i].at[rows]
        loads.append(pltpu.make_async_copy(held[i].at[rows], piece, sem.at[0, n]))
        stores.append(pltpu.make_async_copy(piece, outs[i].at[rows], sem.at[1, n]))
    for copy in loads:
        copy.start()
    for n in range(len(parts)):
        loads[n].wait()
        stores[n].start()
    for copy in stores:
        copy.wait()


def body(mp, ls, wa, wp, ws, wt, wc, we, wd, sharp):
    scale = (lax.axis_size("dp") * lax.axis_size("point") * ROWS) ** (-0.5)
    hbm = pl.BlockSpec(memory_space=pltpu.HBM)
    results = (
        jax.ShapeDtypeStruct((ROWS, C), BF16),
        jax.ShapeDtypeStruct((ROWS, C), BF16),
        jax.ShapeDtypeStruct((NZ, 4, 8, C), F32),
        jax.ShapeDtypeStruct((32, 8, C), F32),
        jax.ShapeDtypeStruct((HD, SL), F32),
        jax.ShapeDtypeStruct((HD, 3 * HD), F32),
        jax.ShapeDtypeStruct((32, 8, C), F32),
        jax.ShapeDtypeStruct((32, 8, FF), F32),
        jax.ShapeDtypeStruct((64, 16, C), F32),
    )
    held = pl.pallas_call(
        functools.partial(kernel, scale),
        out_shape=results,
        in_specs=[hbm] * 9 + [pl.BlockSpec(memory_space=pltpu.SMEM)],
        out_specs=(hbm,) * 9,
        scratch_shapes=list(SCRATCH.values()),
        compiler_params=pltpu.CompilerParams(
            collective_id=0, has_side_effects=True, vmem_limit_bytes=58 << 20
        ),
        name="layer",
    )(mp[0], ls[0], wa, wp, ws, wt, wc, we, wd, sharp)
    outs = pl.pallas_call(
        store,
        out_shape=results,
        in_specs=[hbm] * 9,
        out_specs=(hbm,) * 9,
        scratch_shapes=[pltpu.VMEM(r.shape, r.dtype) for r in results]
        + [pltpu.SemaphoreType.DMA((2, 15))],
        compiler_params=pltpu.CompilerParams(vmem_limit_bytes=58 << 20),
        name="store",
    )(*held)
    upd, pg, feat, proj, sl, tok, out, up, down = outs
    return (
        upd[None],
        pg[None],
        feat.reshape(C, C),
        proj.reshape(C, C),
        sl,
        tok,
        out.reshape(C, C),
        up.reshape(C, FF),
        down.reshape(FF, C),
    )


def solution(mesh):
    split = P("dp", "point", None)
    return jax.shard_map(
        body,
        mesh=mesh,
        in_specs=(split, split) + (P(),) * 8,
        out_specs=(split, split) + (P(),) * 7,
        check_vma=False,
    )
```

```python
import functools

import jax
import jax.numpy as jnp
from jax import lax
from jax.experimental import pallas as pl
from jax.experimental.pallas import tpu as pltpu
from jax.sharding import PartitionSpec as P

F32 = jnp.float32
BF16 = jnp.bfloat16
MESH = pl.DeviceIdType.MESH
EPS = 1e-05
GELU = 0.7978845608028654
HIGH = lax.Precision.HIGHEST

NX, NC, NZ, NY = 4, 2, 8, 4
ROWS = 512
C, FF, HEADS, HD, SL = 256, 1024, 8, 32, 64
PAIRS = 4
KXY = NX * NY
PARTS = ((16, 24), (16, 16))
LATE = (9,)
CH = 512


def dot(a, b):
    return jnp.dot(a, b, preferred_element_type=F32)


def dot_t(a, b):
    return lax.dot_general(a, b, (((1,), (1,)), ((), ())), preferred_element_type=F32)


def tdot(a, b):
    return lax.dot_general(a, b, (((0,), (0,)), ((), ())), preferred_element_type=F32)


def hdot(a, b, dims):
    return lax.dot_general(
        a, b, ((dims[:1], dims[1:]), ((), ())), precision=HIGH, preferred_element_type=F32
    )


def norm_rows(v):
    center = v - jnp.mean(v, axis=-1, keepdims=True)
    inv = lax.rsqrt(jnp.mean(center * center, axis=-1, keepdims=True) + EPS)
    return center * inv, inv


def norm_back(normed, inv, g):
    return inv * (
        g - jnp.mean(g, axis=-1, keepdims=True) - normed * jnp.mean(g * normed, axis=-1, keepdims=True)
    )


def seg_sum(v, ones):
    hi = v.astype(BF16)
    lo = (v - hi.astype(F32)).astype(BF16)
    return jnp.concatenate(
        [
            dot(hi[:, 256 * g : 256 * g + 256], ones) + dot(lo[:, 256 * g : 256 * g + 256], ones)
            for g in range(2)
        ],
        axis=1,
    )


def each(n, f):
    for i in range(n):
        f(i)


def remote(src, dst, ss, rs, dev):
    return pltpu.make_async_remote_copy(
        src_ref=src, dst_ref=dst, send_sem=ss, recv_sem=rs, device_id=dev, device_id_type=MESH
    )


def whole(ref, sem, n, dev):
    part = ref.at[pl.ds(0, n)]
    return remote(part, part, sem.at[0], sem.at[1], dev)


SCRATCH = dict(
    mp=pltpu.VMEM((ROWS, C), BF16),
    ls=pltpu.VMEM((ROWS, C), BF16),
    wa=pltpu.VMEM((C, C), BF16),
    wp=pltpu.VMEM((C, C), BF16),
    ws=pltpu.VMEM((HD, SL), BF16),
    wt=pltpu.VMEM((HD, 3 * HD), BF16),
    wc=pltpu.VMEM((C, C), BF16),
    we=pltpu.VMEM((C, FF), BF16),
    wd=pltpu.VMEM((FF, C), BF16),
    in_sem=pltpu.SemaphoreType.DMA((9,)),
    nh=pltpu.VMEM((ROWS, C), BF16),
    feat=pltpu.VMEM((ROWS, C), BF16),
    proj=pltpu.VMEM((ROWS, C), BF16),
    asg=pltpu.VMEM((ROWS, 512), F32),
    ah=pltpu.VMEM((ROWS, 512), BF16),
    bdw=pltpu.VMEM((C, 512), BF16),
    bdm=pltpu.VMEM((C, 512), BF16),
    bdg=pltpu.VMEM((C, 512), BF16),
    ones=pltpu.VMEM((256, 256), BF16),
    spread=pltpu.VMEM((ROWS, C), BF16),
    n2h=pltpu.VMEM((ROWS, C), BF16),
    act=pltpu.VMEM((ROWS, FF), BF16),
    gh=pltpu.VMEM((ROWS, FF), BF16),
    gres=pltpu.VMEM((ROWS, C), F32),
    grh=pltpu.VMEM((ROWS, C), BF16),
    gspr=pltpu.VMEM((ROWS, C), BF16),
    ga=pltpu.VMEM((ROWS, 512), F32),
    gl=pltpu.VMEM((ROWS, 512), BF16),
    gf=pltpu.VMEM((ROWS, C), BF16),
    gp=pltpu.VMEM((ROWS, C), BF16),
    upd=pltpu.VMEM((ROWS, C), BF16),
    res=pltpu.VMEM((ROWS, C), BF16),
    pgr=pltpu.VMEM((ROWS, C), BF16),
    slc=pltpu.VMEM((HD, SL), F32),
    tok=pltpu.VMEM((HD, 3 * HD), F32),
    out_sem=pltpu.SemaphoreType.DMA((13,)),
    a_p=pltpu.VMEM((PAIRS, 33, 128), F32),
    a_y=pltpu.VMEM((3, 33, 128), F32),
    a_z=pltpu.VMEM((NZ, 33, 128), F32),
    a_m=pltpu.VMEM((PAIRS, HD, 128), F32),
    a_ys=pltpu.SemaphoreType.DMA((2,)),
    a_zs=pltpu.SemaphoreType.DMA((2,)),
    a_ms=pltpu.SemaphoreType.DMA((2,)),
    b_p=pltpu.VMEM((PAIRS, HD, 128), F32),
    b_y=pltpu.VMEM((3, HD, 128), F32),
    b_z=pltpu.VMEM((NZ, HD, 128), F32),
    b_m=pltpu.VMEM((PAIRS, 33, 128), F32),
    b_ys=pltpu.SemaphoreType.DMA((2,)),
    b_zs=pltpu.SemaphoreType.DMA((2,)),
    b_ms=pltpu.SemaphoreType.DMA((2,)),
)


def early_scratch(p, ru, rv):
    f = lambda *shape: pltpu.VMEM(shape + (C,), F32)
    d = lambda *shape: pltpu.SemaphoreType.DMA((2,) + shape)
    names = dict(
        u=f(32, ru), v=f(32, rv), uc=f(KXY, ru), vc=f(KXY, rv),
        ux=f(3, 4, ru), vy=f(3, 4, rv), u1=f(4, ru), v1=f(4, rv),
        uy=f(3, ru), vx=f(3, rv), part=f(ru + rv),
        z=pltpu.VMEM((NZ, 8, 128), F32), zo=f(NZ, 8), zf=f(32),
        uf=f(32, ru), vf=f(32, rv),
        us=d(4), vs=d(4), uxs=d(), vys=d(), uys=d(), vxs=d(),
        zs=d(), zos=d(), zgs=d(), uygs=d(), vxgs=d(), uxgs=d(3), vygs=d(3), ugs=d(4), vgs=d(4),
    )
    return {"e%d_%s" % (p, n): spec for n, spec in names.items()}


SCRATCH.update(
    n_all=pltpu.VMEM((PAIRS, C, 128), F32),
    n_y=pltpu.VMEM((3, C, 128), F32),
    n_sum=pltpu.VMEM((C, 128), F32),
    n_z=pltpu.VMEM((NZ, 32, 128), F32),
    f_own=pltpu.VMEM((16, 128), F32),
    f_core=pltpu.VMEM((16, 128), F32),
    f_x=pltpu.VMEM((NX, 16, 128), F32),
    f_all=pltpu.VMEM((NC, NY, NZ, 8, 128), F32),
    f_out=pltpu.VMEM((NZ, 4, 8, C), F32),
    n_ys=pltpu.SemaphoreType.DMA((2,)),
    n_zs=pltpu.SemaphoreType.DMA((2,)),
    f_cs=pltpu.SemaphoreType.DMA((2,)),
    f_xs=pltpu.SemaphoreType.DMA((2,)),
    f_zs=pltpu.SemaphoreType.DMA((2,)),
    f_ys=pltpu.SemaphoreType.DMA((2,)),
    f_gs=pltpu.SemaphoreType.DMA((2,)),
)


def late_scratch(p, r):
    f = lambda *shape: pltpu.VMEM(shape + (r, C), F32)
    d = lambda *shape: pltpu.SemaphoreType.DMA((2,) + shape)
    names = dict(
        all=f(32), half=f(KXY), xy=f(KXY - 1), z=f(NZ), fin=f(32),
        cs=d(), xys=d(), zs=d(), gs=d(), cgs=d(),
    )
    return {"l%d_%s" % (p, n): spec for n, spec in names.items()}


for p, rows in enumerate(LATE):
    SCRATCH.update(late_scratch(p, rows))
for p, rows in enumerate(PARTS):
    SCRATCH.update(early_scratch(p, *rows))


class Names:
    pass


class Axis:
    def __init__(self, n, me, dev):
        self.n, self.me, self.dev = n, me, dev

    def to(self, i):
        return lax.rem(self.me + i + 1, self.n)

    def frm(self, i):
        return lax.rem(self.me + self.n - 1 - i, self.n)


class Early:
    def __init__(self, s, p, rows, place, scale):
        for name in early_scratch(0, 1, 1):
            setattr(self, name[3:], getattr(s, "e%d_%s" % (p, name[3:])))
        self.ru, self.rv = rows
        self.out = self.rv > 16
        self.scale = scale
        x, c, z, y = place
        self.x, self.c, self.pz, self.y = x, c, z, y
        self.ax = Axis(NX, x, lambda t: (t * NC + c, z * NY + y))
        self.ay = Axis(NY, y, lambda t: (x * NC + c, z * NY + t))
        self.az = Axis(NZ, z, lambda t: (x * NC + c, t * NY + y))
        self.other = (x * NC + (1 - c), z * NY + y)
        self.first = ((self.ax, self.u, self.uc, self.ux, self.u1, self.us, self.uxs),
                      (self.ay, self.v, self.vc, self.vy, self.v1, self.vs, self.vys))
        self.second = ((self.ay, self.u1, self.uy, self.uys, 0, self.ru),
                       (self.ax, self.v1, self.vx, self.vxs, self.ru, self.rv))
        self.fin2 = ((self.ay, self.uf, 16 * c + 4 * x, self.uygs),
                     (self.ax, self.vf, 16 * c + 4 * y, self.vxgs))
        self.fin1 = ((self.ax, self.uf, self.uxgs, self.ugs), (self.ay, self.vf, self.vygs, self.vgs))
        self.sent = []

    def block(self, c, t):
        return pl.ds(16 * c + 4 * t, 4)

    def core_start(self):
        for o in (0, 1, 2, 3):
            for ax, full, half, _, _, sem, _ in self.first:
                self.core_copy(ax, full, half, sem, o).start()

    def core_copy(self, ax, full, half, sem, o):
        t = lax.rem(ax.me + 1 + o, 4)
        return remote(
            full.at[self.block(1 - self.c, t)], half.at[pl.ds(4 * t, 4)], sem.at[0, o], sem.at[1, o],
            self.other,
        )

    def st1_copy(self, ax, half, slots, sem, i):
        t = ax.to(i)
        return remote(half.at[pl.ds(4 * t, 4)], slots.at[i], sem.at[0], sem.at[1], ax.dev(t))

    def st1_start(self):
        for o in (0, 1, 2, 3):
            for ax, full, half, slots, _, sem, sem1 in self.first:
                self.core_copy(ax, full, half, sem, o).wait_recv()
                t = lax.rem(ax.me + 1 + o, 4)
                mine = pl.ds(4 * t, 4)
                half[mine] = half[mine] + full[self.block(self.c, t)]
                if o < 3:
                    self.st1_copy(ax, half, slots, sem1, o).start()

    def st2_copy(self, ax, src, slots, sem, i):
        t = ax.to(i)
        return remote(src.at[t], slots.at[i], sem.at[0], sem.at[1], ax.dev(t))

    def st2_start(self):
        for (ax, _, half, slots, one, _, sem1), (ax2, src, slots2, sem2, _, _) in zip(
            self.first, self.second
        ):
            whole(slots, sem1, 3, self.other).wait_recv()
            one[...] = half[pl.ds(4 * ax.me, 4)] + slots[0] + slots[1] + slots[2]
            for i in range(3):
                self.st2_copy(ax2, src, slots2, sem2, i).start()

    def tile(self, t):
        return (
            pl.ds(pl.multiple_of(8 * (t // 2), 8), 8),
            pl.ds(pl.multiple_of(128 * (t % 2), 128), 128),
        )

    def z_copy(self, i):
        t = self.az.to(i)
        rows, lanes = self.tile(t)
        return remote(
            self.part.at[rows, lanes], self.z.at[self.pz], self.zs.at[0], self.zs.at[1],
            self.az.dev(t),
        )

    def zo_copy(self, i):
        t = self.az.to(i)
        return remote(
            self.part.at[pl.ds(32, 8)], self.zo.at[self.pz], self.zos.at[0], self.zos.at[1],
            self.az.dev(t),
        )

    def z_start(self):
        for ax, src, slots, sem, at, n in self.second:
            whole(slots, sem, 3, self.other).wait_recv()
            self.part[at : at + n, :] = src[ax.me] + slots[0] + slots[1] + slots[2]
        each(7, lambda i: self.z_copy(i).start())
        rows, lanes = self.tile(self.pz)
        self.z[self.pz] = self.part[rows, lanes]
        if self.out:
            each(7, lambda i: self.zo_copy(i).start())
            self.zo[self.pz] = self.part[32:40, :]

    def zg_copy(self, i):
        piece = self.zf.at[self.tile(self.pz)]
        return remote(
            piece, piece, self.zgs.at[0], self.zgs.at[1], self.az.dev(self.az.to(i))
        )

    def zg_start(self):
        whole(self.z, self.zs, 7, self.other).wait_recv()
        total = self.z[0]
        for i in range(1, NZ):
            total = total + self.z[i]
        self.zf[self.tile(self.pz)] = total * self.scale
        each(7, lambda i: self.zg_copy(i).start())

    def fin2_copy(self, ax, fin, base, sem, i):
        piece = fin.at[base + ax.me]
        return remote(piece, piece, sem.at[0], sem.at[1], ax.dev(ax.to(i)))

    def st2g_start(self):
        own_u = 16 * self.c + 4 * self.x + self.y
        own_v = 16 * self.c + 4 * self.y + self.x
        if self.out:
            whole(self.zo, self.zos, 7, self.other).wait_recv()
            total = self.zo[0]
            for i in range(1, NZ):
                total = total + self.zo[i]
            self.vf[own_v, 16:24, :] = total * self.scale
        whole(self.z, self.zgs, 7, self.other).wait_recv()
        self.uf[own_u] = self.zf[0:16, :]
        self.vf[own_v, 0:16, :] = self.zf[16:32, :]
        for ax, fin, base, sem in self.fin2:
            for i in range(3):
                self.fin2_copy(ax, fin, base, sem, i).start()

    def fin1_copy(self, ax, fin, sem, i):
        piece = fin.at[self.block(self.c, ax.me)]
        return remote(piece, piece, sem.at[0, i], sem.at[1, i], ax.dev(ax.to(i)))

    def fin1_got(self, ax, fin, sem, i):
        f = ax.frm(i)
        piece = fin.at[self.block(self.c, f)]
        return remote(piece, piece, sem.at[0, i], sem.at[1, i], ax.dev(f))

    def coreg_copy(self, ax, fin, sem, o):
        piece = fin.at[self.block(self.c, lax.rem(ax.me + NX - o, 4))]
        return remote(piece, piece, sem.at[0, o], sem.at[1, o], self.other)

    def coreg_got(self, ax, fin, sem, o):
        piece = fin.at[self.block(1 - self.c, lax.rem(ax.me + NX - o, 4))]
        return remote(piece, piece, sem.at[0, o], sem.at[1, o], self.other)

    def st1g_start(self):
        for (ax2, fin, base, sem2), (ax, _, sem1, semc) in zip(self.fin2, self.fin1):
            whole(fin, sem2, 3, self.other).wait_recv()
            for i in range(3):
                self.fin1_copy(ax, fin, sem1, i).start()
            self.coreg_copy(ax, fin, semc, 0).start()

    def coreg_start(self):
        for i in (0, 2, 1):
            for ax, fin, sem1, semc in self.fin1:
                self.fin1_got(ax, fin, sem1, i).wait_recv()
                self.coreg_copy(ax, fin, semc, i + 1).start()

    def coreg_wait(self):
        for ax, fin, _, semc in self.fin1:
            for o in range(4):
                self.coreg_got(ax, fin, semc, o).wait_recv()

    def drain_sums(self):
        for (ax, full, half, slots, _, sem, sem1), (_, _, slots2, sem2, _, _) in zip(
            self.first, self.second
        ):
            for o in range(4):
                self.core_copy(ax, full, half, sem, o).wait_send()
            whole(slots, sem1, 3, self.other).wait_send()
            whole(slots2, sem2, 3, self.other).wait_send()

    def drain(self):
        whole(self.z, self.zs, 7, self.other).wait_send()
        whole(self.z, self.zgs, 7, self.other).wait_send()
        if self.out:
            whole(self.zo, self.zos, 7, self.other).wait_send()
        for (_, fin, _, sem2), (ax, _, sem1, semc) in zip(self.fin2, self.fin1):
            whole(fin, sem2, 3, self.other).wait_send()
            for i in range(3):
                self.fin1_copy(ax, fin, sem1, i).wait_send()
            for o in range(4):
                self.coreg_copy(ax, fin, semc, o).wait_send()


class Late:
    def __init__(self, s, p, place, scale):
        for name in late_scratch(0, 1):
            setattr(self, name[3:], getattr(s, "l%d_%s" % (p, name[3:])))
        self.scale = scale
        x, c, z, y = place
        self.x, self.c, self.pz, self.y = x, c, z, y
        self.k = x * NY + y
        self.own = c * KXY + self.k
        self.az = Axis(NZ, z, lambda t: (x * NC + c, t * NY + y))
        self.other = (x * NC + (1 - c), z * NY + y)

    def dev(self, xx, yy):
        return (xx * NC + self.c, self.pz * NY + yy)

    def to(self, i):
        j = i + 1
        return lax.rem(self.x + j // NY, NX), lax.rem(self.y + j % NY, NY)

    def core_copy(self):
        theirs = pl.ds((1 - self.c) * KXY, KXY)
        return remote(self.all.at[theirs], self.half, self.cs.at[0], self.cs.at[1], self.other)

    def core_start(self):
        self.core_copy().start()

    def xy_copy(self, i):
        xx, yy = self.to(i)
        return remote(
            self.half.at[xx * NY + yy], self.xy.at[i], self.xys.at[0], self.xys.at[1],
            self.dev(xx, yy),
        )

    def xy_start(self):
        self.core_copy().wait_recv()
        self.half[...] = self.half[...] + self.all[pl.ds(self.c * KXY, KXY)]
        each(KXY - 1, lambda i: self.xy_copy(i).start())

    def z_copy(self, i):
        piece = self.z.at[self.pz]
        return remote(
            piece, piece, self.zs.at[0], self.zs.at[1], self.az.dev(self.az.to(i))
        )

    def z_start(self):
        whole(self.xy, self.xys, KXY - 1, self.other).wait_recv()
        part = self.half[self.k]
        for i in range(KXY - 1):
            part = part + self.xy[i]
        self.z[self.pz] = part
        each(NZ - 1, lambda i: self.z_copy(i).start())

    def g_copy(self, i):
        piece = self.fin.at[self.own]
        return remote(piece, piece, self.gs.at[0], self.gs.at[1], self.dev(*self.to(i)))

    def g_start(self):
        whole(self.z, self.zs, NZ - 1, self.other).wait_recv()
        total = self.z[0]
        for i in range(1, NZ):
            total = total + self.z[i]
        self.fin[self.own] = total * self.scale
        each(KXY - 1, lambda i: self.g_copy(i).start())

    def c_copy(self, c):
        mine = self.fin.at[pl.ds(c * KXY, KXY)]
        return remote(mine, mine, self.cgs.at[0], self.cgs.at[1], self.other)

    def c_start(self):
        whole(self.fin, self.gs, KXY - 1, self.other).wait_recv()
        self.c_copy(self.c).start()

    def wait(self):
        self.c_copy(1 - self.c).wait_recv()

    def drain_sums(self):
        self.core_copy().wait_send()
        whole(self.xy, self.xys, KXY - 1, self.other).wait_send()

    def drain(self):
        whole(self.z, self.zs, NZ - 1, self.other).wait_send()
        whole(self.fin, self.gs, KXY - 1, self.other).wait_send()
        self.c_copy(self.c).wait_send()


def kernel(scale, *refs):
    ins, rest = refs[:10], refs[10:]
    (o_upd, o_pg, o_feat, o_proj, o_slice, o_tok, o_out, o_up, o_down) = rest[:9]
    s = Names()
    for name, ref in zip(SCRATCH, rest[9:]):
        setattr(s, name, ref)

    dp, pt = lax.axis_index("dp"), lax.axis_index("point")
    x, c = dp // NC, dp % NC
    z, y = pt // NY, pt % NY
    k = x * NY + y
    own = c * KXY + k
    other = (x * NC + (1 - c), pt)

    def at_y(i):
        return lax.rem(y + i + 1, NY)

    def from_y(i):
        return lax.rem(y + NY - 1 - i, NY)

    def at_z(i):
        return lax.rem(z + i + 1, NZ)

    def from_z(i):
        return lax.rem(z + NZ - 1 - i, NZ)

    def at_xy(i):
        j = i + 1
        return lax.rem(x + j // NY, NX), lax.rem(y + j % NY, NY)

    def from_xy(i):
        j = i + 1
        return lax.rem(x + NX - j // NY, NX), lax.rem(y + NY - j % NY, NY)

    def at_x(i):
        return lax.rem(x + i + 1, NX)

    def from_x(i):
        return lax.rem(x + NX - 1 - i, NX)

    def dev_x(xx):
        return (xx * NC + c, pt)

    def dev_y(yy):
        return (dp, z * NY + yy)

    def dev_z(zz):
        return (dp, zz * NY + y)

    def dev_xy(xx, yy):
        return (xx * NC + c, z * NY + yy)

    in_dst = (s.mp, s.ls, s.wa, s.wp, s.ws, s.wt, s.wc, s.we, s.wd)
    loads = [pltpu.make_async_copy(a, b, s.in_sem.at[i]) for i, (a, b) in enumerate(zip(ins, in_dst))]
    order = (0, 2, 3, 4, 5, 1, 6, 7, 8)
    for i in order:
        loads[i].start()
    barrier = pltpu.get_barrier_semaphore()
    pl.semaphore_signal(barrier, inc=1, device_id=other, device_id_type=MESH)
    each(
        KXY - 1,
        lambda i: pl.semaphore_signal(
            barrier, inc=1, device_id=dev_xy(*at_xy(i)), device_id_type=MESH
        ),
    )
    each(
        NZ - 1,
        lambda i: pl.semaphore_signal(barrier, inc=1, device_id=dev_z(at_z(i)), device_id_type=MESH),
    )

    sharp_ref = ins[9]

    lane = lax.broadcasted_iota(jnp.int32, (1, 512), 1)
    sharp = jnp.full((1, 512), sharp_ref[0], F32)
    for h in range(1, HEADS):
        sharp = jnp.where(lane // SL == h, sharp_ref[h], sharp)
    inv_sharp = 1.0 / sharp
    rr = lax.broadcasted_iota(jnp.int32, (256, 256), 0)
    cc = lax.broadcasted_iota(jnp.int32, (256, 256), 1)
    s.ones[...] = jnp.where(rr // SL == cc // SL, 1.0, 0.0).astype(BF16)
    s.bdm[...] = jnp.zeros_like(s.bdm)
    s.bdg[...] = jnp.zeros_like(s.bdg)
    low = lax.broadcasted_iota(jnp.int32, (HD, 128), 1) < SL

    def pack_diag(t):
        return jnp.where(low, t[:HD], t[HD:])

    def spread_diag(v):
        return jnp.concatenate([jnp.where(low, v, 0.0), jnp.where(low, 0.0, v)], axis=0).astype(BF16)

    loads[4].wait()
    w1 = s.ws[...].astype(F32)
    w2 = jnp.concatenate([w1, w1], axis=1)
    s.bdw[...] = jnp.zeros_like(s.bdw)
    for j in range(PAIRS):
        s.bdw[64 * j : 64 * j + 64, 128 * j : 128 * j + 128] = spread_diag(w2)

    for i in (0, 2, 3):
        loads[i].wait()
    mass = jnp.zeros((1, 512), F32)
    for r in range(0, ROWS, CH):
        rows = slice(r, r + CH)
        normed, _ = norm_rows(s.mp[rows, :].astype(F32))
        nh = normed.astype(BF16)
        s.nh[rows, :] = nh
        s.feat[rows, :] = dot(nh, s.wa[...]).astype(BF16)
        proj = dot(nh, s.wp[...]).astype(BF16)
        s.proj[rows, :] = proj
        logits = (
            jnp.concatenate(
                [
                    dot(
                        proj[:, 128 * g : 128 * g + 128],
                        s.bdw[128 * g : 128 * g + 128, 256 * g : 256 * g + 256],
                    )
                    for g in range(2)
                ],
                axis=1,
            )
            * inv_sharp
        )
        e = jnp.exp(logits)
        a = e / seg_sum(e, s.ones[...])
        s.asg[rows, :] = a
        s.ah[rows, :] = a.astype(BF16)
        mass = mass + jnp.sum(a, axis=0, keepdims=True)

    def head_sums(values, out):
        for g in range(2):
            t = tdot(values[:, 128 * g : 128 * g + 128], s.ah[:, 256 * g : 256 * g + 256])
            for j in range(2):
                out[2 * g + j, 0:HD, :] = pack_diag(
                    t[64 * j : 64 * j + 64, 128 * j : 128 * j + 128]
                )

    head_sums(s.feat, s.a_p)
    for j in range(PAIRS):
        s.a_p[j, HD:, :] = mass[:, 128 * j : 128 * j + 128]

    def reduce_pairs(part, buf_y, buf_z, sem_y, sem_z):
        def put_y(i):
            t = at_y(i)
            return remote(part.at[t], buf_y.at[i], sem_y.at[0], sem_y.at[1], dev_y(t))

        def put_z(i):
            return remote(
                buf_z.at[z], buf_z.at[z], sem_z.at[0], sem_z.at[1], dev_z(at_z(i))
            )

        def start():
            each(NY - 1, lambda i: put_y(i).start())

        def middle():
            whole(buf_y, sem_y, NY - 1, other).wait_recv()
            buf_z[z] = part[y] + buf_y[0] + buf_y[1] + buf_y[2]
            each(NZ - 1, lambda i: put_z(i).start())

        def finish():
            whole(buf_z, sem_z, NZ - 1, other).wait_recv()
            total = buf_z[0]
            for i in range(1, NZ):
                total = total + buf_z[i]
            return total

        def drain():
            whole(buf_y, sem_y, NY - 1, other).wait_send()
            whole(buf_z, sem_z, NZ - 1, other).wait_send()

        return start, middle, finish, drain

    def gather_pairs(buf, sem):
        def put(i):
            return remote(buf.at[y], buf.at[y], sem.at[0], sem.at[1], dev_y(at_y(i)))

        def start():
            each(NY - 1, lambda i: put(i).start())

        def wait():
            whole(buf, sem, NY - 1, other).wait_recv()

        def drain():
            whole(buf, sem, NY - 1, other).wait_send()

        return start, wait, drain

    pl.semaphore_wait(barrier, 1 + (KXY - 1) + (NZ - 1))
    a_start, a_middle, a_finish, a_drain = reduce_pairs(s.a_p, s.a_y, s.a_z, s.a_ys, s.a_zs)
    am_start, am_wait, am_drain = gather_pairs(s.a_m, s.a_ms)
    a_start()
    a_middle()

    for g in range(2):
        t = tdot(s.nh[...], s.ah[:, 256 * g : 256 * g + 256])
        for j in range(2):
            s.n_all[2 * g + j] = t[:, 128 * j : 128 * j + 128]

    def n_puty(i):
        t = at_y(i)
        return remote(s.n_all.at[t], s.n_y.at[i], s.n_ys.at[0], s.n_ys.at[1], dev_y(t))

    def n_putz(i):
        t = at_z(i)
        rows = pl.ds(pl.multiple_of(32 * t, 32), 32)
        return remote(s.n_sum.at[rows], s.n_z.at[z], s.n_zs.at[0], s.n_zs.at[1], dev_z(t))

    each(NY - 1, lambda i: n_puty(i).start())
    for i in (5, 1, 6, 7, 8):
        loads[i].wait()
    total = a_finish()

    wt = s.wt[...].astype(F32)
    inv_mass = 1.0 / (total[HD : HD + 1] + EPS)
    tokens = total[:HD] * inv_mass
    qkv = hdot(wt, tokens, (0, 0))
    q, kk, v = qkv[:HD], qkv[HD : 2 * HD], qkv[2 * HD :]
    r2 = lax.broadcasted_iota(jnp.int32, (128, 128), 0) // SL
    c2 = lax.broadcasted_iota(jnp.int32, (128, 128), 1) // SL
    scores = hdot(q, kk, (0, 0)) * HD ** (-0.5)
    expo = jnp.where(r2 == c2, jnp.exp(jnp.where(r2 == c2, scores, 0.0)), 0.0)
    att = expo / jnp.sum(expo, axis=-1, keepdims=True)
    s.a_m[y] = hdot(v, att, (1, 1))
    am_start()
    am_wait()
    for j in range(PAIRS):
        s.bdm[64 * j : 64 * j + 64, 128 * j : 128 * j + 128] = spread_diag(s.a_m[j])

    whole(s.n_y, s.n_ys, NY - 1, other).wait_recv()
    s.n_sum[...] = s.n_all[y] + s.n_y[0] + s.n_y[1] + s.n_y[2]
    each(NZ - 1, lambda i: n_putz(i).start())
    s.n_z[z] = s.n_sum[pl.ds(pl.multiple_of(32 * z, 32), 32), :]

    for r in range(0, ROWS, CH):
        rows = slice(r, r + CH)
        spread = jnp.concatenate(
            [
                dot_t(
                    s.ah[rows, 256 * g : 256 * g + 256],
                    s.bdm[128 * g : 128 * g + 128, 256 * g : 256 * g + 256],
                )
                for g in range(2)
            ],
            axis=1,
        ).astype(BF16)
        s.spread[rows, :] = spread
        res = (s.mp[rows, :].astype(F32) + dot(spread, s.wc[...])).astype(BF16).astype(F32)
        n2, inv2 = norm_rows(res)
        n2h = n2.astype(BF16)
        s.n2h[rows, :] = n2h
        sens = s.ls[rows, :]
        s.res[rows, :] = res.astype(BF16)
        gn2 = jnp.zeros((CH, C), F32)
        for f in range(0, FF, 256):
            hid = dot(n2h, s.we[:, f : f + 256])
            gact = dot_t(sens, s.wd[f : f + 256, :])
            h2 = hid * hid
            u = 0.5 + 0.5 * jnp.tanh(hid * (GELU + GELU * 0.044715 * h2))
            act = hid * u
            slope = u + act * (1.0 - u) * (2.0 * GELU + 6.0 * GELU * 0.044715 * h2)
            acth = act.astype(BF16)
            gh = (gact * slope).astype(BF16)
            s.act[rows, f : f + 256] = acth
            s.gh[rows, f : f + 256] = gh
            gn2 = gn2 + dot_t(gh, s.we[:, f : f + 256])
        gres = sens.astype(F32) + norm_back(n2, inv2, gn2)
        s.gres[rows, :] = gres
        grh = gres.astype(BF16)
        s.grh[rows, :] = grh
        s.gspr[rows, :] = dot_t(grh, s.wc[...]).astype(BF16)

    head_sums(s.gspr, s.b_p)
    b_start, b_middle, b_finish, b_drain = reduce_pairs(s.b_p, s.b_y, s.b_z, s.b_ys, s.b_zs)
    bm_start, bm_wait, bm_drain = gather_pairs(s.b_m, s.b_ms)
    b_start()
    outs = []

    def write(src, dst):
        copy = pltpu.make_async_copy(src, dst, s.out_sem.at[len(outs)])
        copy.start()
        outs.append(copy)


    early = [Early(s, p, PARTS[p], (x, c, z, y), scale) for p in range(len(PARTS))]
    for p, e in enumerate(early):
        for b in range(2):
            f = 256 * (2 * p + b)
            e.u[:, 8 * b : 8 * b + 8, :] = tdot(s.n2h[...], s.gh[:, f : f + 256]).reshape(32, 8, C)
            e.v[16 * b : 16 * b + 16, 0:16, :] = tdot(s.act[:, f : f + 256], s.ls[...]).reshape(
                16, 16, C
            )
        if p == 0:
            e.v[:, 16:24, :] = tdot(s.spread[...], s.grh[...]).reshape(32, 8, C)
        e.core_start()
    early[0].st1_start()
    b_middle()

    for r in range(0, ROWS, CH):
        rows = slice(r, r + CH)
        for g in range(2):
            s.ga[rows, 256 * g : 256 * g + 256] = dot(
                s.gspr[rows, 128 * g : 128 * g + 128],
                s.bdm[128 * g : 128 * g + 128, 256 * g : 256 * g + 256],
            )

    early[1].st1_start()
    s.upd[...] = (s.res[...].astype(F32) + dot(s.act[...], s.wd[...])).astype(BF16)
    write(s.upd, o_upd)

    early[0].st2_start()
    gm = b_finish()
    dv = hdot(gm, att, (1, 0))
    datt = hdot(gm, v, (0, 0))
    dsc = att * (datt - jnp.sum(att * datt, axis=-1, keepdims=True)) * HD ** (-0.5)
    dq = hdot(kk, dsc, (1, 1))
    dk = hdot(q, dsc, (1, 0))
    dqkv = jnp.concatenate([dq, dk, dv], axis=0)
    tokenmap = hdot(tokens, dqkv, (1, 1))
    dtok = hdot(wt, dqkv, (1, 0))
    gsum = dtok * inv_mass
    s.b_m[y, 0:HD, :] = gsum
    s.b_m[y, HD:, :] = -jnp.sum(gsum * tokens, axis=0, keepdims=True)
    bm_start()

    whole(s.n_z, s.n_zs, NZ - 1, other).wait_recv()
    nsum = s.n_z[0]
    for i in range(1, NZ):
        nsum = nsum + s.n_z[i]
    nhi = nsum.astype(BF16)
    nlo = (nsum - nhi.astype(F32)).astype(BF16)
    gsd = spread_diag(gsum)
    fblock = dot_t(nhi, gsd) + dot_t(nlo, gsd)
    s.f_own[...] = jnp.concatenate([fblock[:16], fblock[16:]], axis=1)
    f_core = remote(s.f_own, s.f_core, s.f_cs.at[0], s.f_cs.at[1], other)
    f_core.start()

    def f_putx(i):
        t = lax.rem(x + i + 1, NX)
        piece = s.f_x.at[x]
        return remote(piece, piece, s.f_xs.at[0], s.f_xs.at[1], (t * NC + c, pt))

    def f_x_start():
        f_core.wait_recv()
        s.f_x[x] = s.f_own[...] + s.f_core[...]
        each(NX - 1, lambda i: f_putx(i).start())

    def f_putz(i):
        piece = s.f_all.at[c, y, z]
        return remote(piece, piece, s.f_zs.at[0], s.f_zs.at[1], dev_z(at_z(i)))

    def f_z_start():
        whole(s.f_x, s.f_xs, NX - 1, other).wait_recv()
        half = pl.ds(pl.multiple_of(8 * c, 8), 8)
        total = s.f_x[0, half, :] + s.f_x[1, half, :] + s.f_x[2, half, :] + s.f_x[3, half, :]
        s.f_all[c, y, z] = total * scale
        each(NZ - 1, lambda i: f_putz(i).start())

    def f_puty(i):
        piece = s.f_all.at[c, y]
        return remote(piece, piece, s.f_ys.at[0], s.f_ys.at[1], dev_y(at_y(i)))

    def f_y_start():
        whole(s.f_all.at[0, 0], s.f_zs, NZ - 1, other).wait_recv()
        each(NY - 1, lambda i: f_puty(i).start())

    def f_give(core):
        piece = s.f_all.at[core]
        return remote(piece, piece, s.f_gs.at[0], s.f_gs.at[1], other)

    def f_give_start():
        whole(s.f_all.at[0], s.f_ys, NY - 1, other).wait_recv()
        f_give(c).start()

    def f_finish():
        f_give(1 - c).wait_recv()
        left = lax.broadcasted_iota(jnp.int32, (64, 128), 1) < 64
        for core in range(NC):
            for j in range(2):
                a0 = s.f_all[core, 2 * j].reshape(64, 128)
                a1 = s.f_all[core, 2 * j + 1].reshape(64, 128)
                lo = jnp.where(left, a0, pltpu.roll(a1, 64, 1))
                hi = jnp.where(left, pltpu.roll(a0, 64, 1), a1)
                lanes = slice(128 * j, 128 * j + 128)
                s.f_out[:, core, :, lanes] = lo.reshape(NZ, 8, 128)
                s.f_out[:, 2 + core, :, lanes] = hi.reshape(NZ, 8, 128)

    def f_drain():
        whole(s.n_y, s.n_ys, NY - 1, other).wait_send()
        whole(s.n_z, s.n_zs, NZ - 1, other).wait_send()
        f_core.wait_send()
        whole(s.f_x, s.f_xs, NX - 1, other).wait_send()
        whole(s.f_all.at[0, 0], s.f_zs, NZ - 1, other).wait_send()
        whole(s.f_all.at[0], s.f_ys, NY - 1, other).wait_send()
        f_give(c).wait_send()

    f_x_start()
    bm_wait()
    for j in range(PAIRS):
        s.bdg[64 * j : 64 * j + 64, 128 * j : 128 * j + 128] = spread_diag(s.b_m[j, 0:HD, :])
    gmass = jnp.concatenate([s.b_m[j, HD : HD + 1, :] for j in range(PAIRS)], axis=1)

    late = [Late(s, p, (x, c, z, y), scale) for p in range(len(LATE))]
    second = late[0]
    early[0].z_start()
    ga = s.ga[...] + gmass
    ga = ga + jnp.concatenate(
        [
            dot(
                s.feat[:, 128 * g : 128 * g + 128],
                s.bdg[128 * g : 128 * g + 128, 256 * g : 256 * g + 256],
            )
            for g in range(2)
        ],
        axis=1,
    )
    a = s.asg[...]
    gl = (a * (ga - seg_sum(a * ga, s.ones[...])) * inv_sharp).astype(BF16)
    s.gl[...] = gl
    s.gp[...] = jnp.concatenate(
        [
            dot_t(
                gl[:, 256 * g : 256 * g + 256],
                s.bdw[128 * g : 128 * g + 128, 256 * g : 256 * g + 256],
            )
            for g in range(2)
        ],
        axis=1,
    ).astype(BF16)
    second.all[:, 0:8, :] = tdot(s.nh[...], s.gp[...]).reshape(32, 8, C)
    slices = jnp.zeros((HD, 128), F32)
    for g in range(2):
        t = tdot(s.proj[:, 128 * g : 128 * g + 128], s.gl[:, 256 * g : 256 * g + 256])
        for j in range(2):
            slices = slices + pack_diag(t[64 * j : 64 * j + 64, 128 * j : 128 * j + 128])
    tokenmap = jnp.where(z == 0, tokenmap, jnp.zeros_like(tokenmap))
    small = jnp.concatenate([slices, tokenmap, jnp.zeros((HD, 32), F32)], axis=1)
    for i in range(32):
        second.all[i, 8:9, :] = small[i : i + 1, :]
    second.core_start()
    early[1].st2_start()
    f_z_start()
    second.xy_start()
    early[1].z_start()
    s.gf[...] = jnp.concatenate(
        [
            dot_t(
                s.ah[:, 256 * g : 256 * g + 256],
                s.bdg[128 * g : 128 * g + 128, 256 * g : 256 * g + 256],
            )
            for g in range(2)
        ],
        axis=1,
    ).astype(BF16)

    for r in range(0, ROWS, CH):
        rows = slice(r, r + CH)
        normed, inv = norm_rows(s.mp[rows, :].astype(F32))
        gn = dot_t(s.gf[rows, :], s.wa[...]) + dot_t(s.gp[rows, :], s.wp[...])
        s.pgr[rows, :] = (s.gres[rows, :] + norm_back(normed, inv, gn)).astype(BF16)
    write(s.pgr, o_pg)
    a_drain()
    am_drain()
    b_drain()
    bm_drain()
    for e in early:
        e.drain_sums()

    early[0].zg_start()
    early[1].zg_start()
    f_y_start()
    early[0].st2g_start()
    second.z_start()
    early[1].st2g_start()
    early[0].st1g_start()
    f_give_start()
    second.g_start()
    early[1].st1g_start()
    f_finish()
    write(s.f_out, o_feat)
    f_drain()
    for part in late:
        part.drain_sums()
    early[0].coreg_start()
    second.c_start()
    early[1].coreg_start()
    for part in late:
        part.wait()
    write(second.fin.at[:, pl.ds(0, 8), :], o_proj)
    rows = [second.fin[i, 8:9, :] for i in range(32)]
    small = jnp.concatenate(rows, axis=0)
    s.slc[...] = small[:, 0:SL] + small[:, SL : 2 * SL]
    s.tok[...] = small[:, 128 : 128 + 3 * HD]
    write(s.slc, o_slice)
    write(s.tok, o_tok)
    for p, e in enumerate(early):
        e.coreg_wait()
        for b in range(2):
            write(
                e.uf.at[:, pl.ds(8 * b, 8), :], o_up.at[:, :, pl.ds(256 * (2 * p + b), 256)]
            )
        write(e.vf.at[:, pl.ds(0, 16), :], o_down.at[pl.ds(32 * p, 32)])
        if p == 0:
            write(e.vf.at[:, pl.ds(16, 8), :], o_out)
    for part in late:
        part.drain()
    for e in early:
        e.drain()
    for copy in outs:
        copy.wait()


def store(*refs):
    held, outs, stage, sem = refs[:9], refs[9:18], refs[18:27], refs[27]
    parts = [(7, pl.ds(8 * q, 8)) for q in range(4)]
    parts += [(8, pl.ds(16 * q, 16)) for q in range(4)]
    parts += [(i, pl.ds(0, held[i].shape[0])) for i in (0, 1, 2, 3, 6, 4, 5)]
    loads, stores = [], []
    for n, (i, rows) in enumerate(parts):
        piece = stage[i].at[rows]
        loads.append(pltpu.make_async_copy(held[i].at[rows], piece, sem.at[0, n]))
        stores.append(pltpu.make_async_copy(piece, outs[i].at[rows], sem.at[1, n]))
    for copy in loads:
        copy.start()
    for n in range(len(parts)):
        loads[n].wait()
        stores[n].start()
    for copy in stores:
        copy.wait()


def body(mp, ls, wa, wp, ws, wt, wc, we, wd, sharp):
    scale = (lax.axis_size("dp") * lax.axis_size("point") * ROWS) ** (-0.5)
    hbm = pl.BlockSpec(memory_space=pltpu.HBM)
    results = (
        jax.ShapeDtypeStruct((ROWS, C), BF16),
        jax.ShapeDtypeStruct((ROWS, C), BF16),
        jax.ShapeDtypeStruct((NZ, 4, 8, C), F32),
        jax.ShapeDtypeStruct((32, 8, C), F32),
        jax.ShapeDtypeStruct((HD, SL), F32),
        jax.ShapeDtypeStruct((HD, 3 * HD), F32),
        jax.ShapeDtypeStruct((32, 8, C), F32),
        jax.ShapeDtypeStruct((32, 8, FF), F32),
        jax.ShapeDtypeStruct((64, 16, C), F32),
    )
    held = pl.pallas_call(
        functools.partial(kernel, scale),
        out_shape=results,
        in_specs=[hbm] * 9 + [pl.BlockSpec(memory_space=pltpu.SMEM)],
        out_specs=(hbm,) * 9,
        scratch_shapes=list(SCRATCH.values()),
        compiler_params=pltpu.CompilerParams(
            collective_id=0, has_side_effects=True, vmem_limit_bytes=58 << 20
        ),
        name="layer",
    )(mp[0], ls[0], wa, wp, ws, wt, wc, we, wd, sharp)
    outs = pl.pallas_call(
        store,
        out_shape=results,
        in_specs=[hbm] * 9,
        out_specs=(hbm,) * 9,
        scratch_shapes=[pltpu.VMEM(r.shape, r.dtype) for r in results]
        + [pltpu.SemaphoreType.DMA((2, 15))],
        compiler_params=pltpu.CompilerParams(vmem_limit_bytes=58 << 20),
        name="store",
    )(*held)
    upd, pg, feat, proj, sl, tok, out, up, down = outs
    return (
        upd[None],
        pg[None],
        feat.reshape(C, C),
        proj.reshape(C, C),
        sl,
        tok,
        out.reshape(C, C),
        up.reshape(C, FF),
        down.reshape(FF, C),
    )


def solution(mesh):
    split = P("dp", "point", None)
    return jax.shard_map(
        body,
        mesh=mesh,
        in_specs=(split, split) + (P(),) * 8,
        out_specs=(split, split) + (P(),) * 7,
        check_vma=False,
    )
```

```python
import functools

import jax
import jax.numpy as jnp
from jax import lax
from jax.experimental import pallas as pl
from jax.experimental.pallas import tpu as pltpu
from jax.sharding import PartitionSpec as P

F32 = jnp.float32
BF16 = jnp.bfloat16
MESH = pl.DeviceIdType.MESH
EPS = 1e-05
GELU = 0.7978845608028654
HIGH = lax.Precision.HIGHEST

NX, NC, NZ, NY = 4, 2, 8, 4
ROWS = 512
C, FF, HEADS, HD, SL = 256, 1024, 8, 32, 64
PAIRS = 4
KXY = NX * NY
PARTS = ((16, 24), (16, 16))
LATE = (9,)
CH = 512


def dot(a, b):
    return jnp.dot(a, b, preferred_element_type=F32)


def dot_t(a, b):
    return lax.dot_general(a, b, (((1,), (1,)), ((), ())), preferred_element_type=F32)


def tdot(a, b):
    return lax.dot_general(a, b, (((0,), (0,)), ((), ())), preferred_element_type=F32)


def hdot(a, b, dims):
    return lax.dot_general(
        a, b, ((dims[:1], dims[1:]), ((), ())), precision=HIGH, preferred_element_type=F32
    )


def norm_rows(v):
    center = v - jnp.mean(v, axis=-1, keepdims=True)
    inv = lax.rsqrt(jnp.mean(center * center, axis=-1, keepdims=True) + EPS)
    return center * inv, inv


def norm_back(normed, inv, g):
    return inv * (
        g - jnp.mean(g, axis=-1, keepdims=True) - normed * jnp.mean(g * normed, axis=-1, keepdims=True)
    )


def seg_sum(v, ones):
    hi = v.astype(BF16)
    lo = (v - hi.astype(F32)).astype(BF16)
    return jnp.concatenate(
        [
            dot(hi[:, 256 * g : 256 * g + 256], ones) + dot(lo[:, 256 * g : 256 * g + 256], ones)
            for g in range(2)
        ],
        axis=1,
    )


def each(n, f):
    for i in range(n):
        f(i)


def remote(src, dst, ss, rs, dev):
    return pltpu.make_async_remote_copy(
        src_ref=src, dst_ref=dst, send_sem=ss, recv_sem=rs, device_id=dev, device_id_type=MESH
    )


def whole(ref, sem, n, dev):
    part = ref.at[pl.ds(0, n)]
    return remote(part, part, sem.at[0], sem.at[1], dev)


SCRATCH = dict(
    mp=pltpu.VMEM((ROWS, C), BF16),
    ls=pltpu.VMEM((ROWS, C), BF16),
    wa=pltpu.VMEM((C, C), BF16),
    wp=pltpu.VMEM((C, C), BF16),
    ws=pltpu.VMEM((HD, SL), BF16),
    wt=pltpu.VMEM((HD, 3 * HD), BF16),
    wc=pltpu.VMEM((C, C), BF16),
    we=pltpu.VMEM((C, FF), BF16),
    wd=pltpu.VMEM((FF, C), BF16),
    in_sem=pltpu.SemaphoreType.DMA((9,)),
    nh=pltpu.VMEM((ROWS, C), BF16),
    feat=pltpu.VMEM((ROWS, C), BF16),
    proj=pltpu.VMEM((ROWS, C), BF16),
    asg=pltpu.VMEM((ROWS, 512), F32),
    ah=pltpu.VMEM((ROWS, 512), BF16),
    bdw=pltpu.VMEM((C, 512), BF16),
    bdm=pltpu.VMEM((C, 512), BF16),
    bdg=pltpu.VMEM((C, 512), BF16),
    ones=pltpu.VMEM((256, 256), BF16),
    spread=pltpu.VMEM((ROWS, C), BF16),
    n2h=pltpu.VMEM((ROWS, C), BF16),
    act=pltpu.VMEM((ROWS, FF), BF16),
    gh=pltpu.VMEM((ROWS, FF), BF16),
    gres=pltpu.VMEM((ROWS, C), F32),
    grh=pltpu.VMEM((ROWS, C), BF16),
    gspr=pltpu.VMEM((ROWS, C), BF16),
    ga=pltpu.VMEM((ROWS, 512), F32),
    gl=pltpu.VMEM((ROWS, 512), BF16),
    gf=pltpu.VMEM((ROWS, C), BF16),
    gp=pltpu.VMEM((ROWS, C), BF16),
    upd=pltpu.VMEM((ROWS, C), BF16),
    res=pltpu.VMEM((ROWS, C), BF16),
    pgr=pltpu.VMEM((ROWS, C), BF16),
    slc=pltpu.VMEM((HD, SL), F32),
    tok=pltpu.VMEM((HD, 3 * HD), F32),
    out_sem=pltpu.SemaphoreType.DMA((13,)),
    a_p=pltpu.VMEM((PAIRS, 33, 128), F32),
    a_y=pltpu.VMEM((3, 33, 128), F32),
    a_z=pltpu.VMEM((NZ, 33, 128), F32),
    a_m=pltpu.VMEM((PAIRS, HD, 128), F32),
    a_ys=pltpu.SemaphoreType.DMA((2,)),
    a_zs=pltpu.SemaphoreType.DMA((2,)),
    a_ms=pltpu.SemaphoreType.DMA((2,)),
    b_p=pltpu.VMEM((PAIRS, HD, 128), F32),
    b_y=pltpu.VMEM((3, HD, 128), F32),
    b_z=pltpu.VMEM((NZ, HD, 128), F32),
    b_m=pltpu.VMEM((PAIRS, 33, 128), F32),
    b_ys=pltpu.SemaphoreType.DMA((2,)),
    b_zs=pltpu.SemaphoreType.DMA((2,)),
    b_ms=pltpu.SemaphoreType.DMA((2,)),
)


def early_scratch(p, ru, rv):
    f = lambda *shape: pltpu.VMEM(shape + (C,), F32)
    d = lambda *shape: pltpu.SemaphoreType.DMA((2,) + shape)
    names = dict(
        u=f(32, ru), v=f(32, rv), uc=f(KXY, ru), vc=f(KXY, rv),
        ux=f(3, 4, ru), vy=f(3, 4, rv), u1=f(4, ru), v1=f(4, rv),
        uy=f(3, ru), vx=f(3, rv), part=f(ru + rv),
        z=pltpu.VMEM((NZ, 8, 128), F32), zo=f(NZ, 8), zf=f(32),
        uf=f(32, ru), vf=f(32, rv),
        us=d(4), vs=d(4), uxs=d(), vys=d(), uys=d(), vxs=d(),
        zs=d(), zos=d(), zgs=d(), uygs=d(), vxgs=d(), uxgs=d(3), vygs=d(3), ugs=d(4), vgs=d(4),
    )
    return {"e%d_%s" % (p, n): spec for n, spec in names.items()}


SCRATCH.update(
    n_all=pltpu.VMEM((PAIRS, C, 128), F32),
    n_y=pltpu.VMEM((3, C, 128), F32),
    n_sum=pltpu.VMEM((C, 128), F32),
    n_z=pltpu.VMEM((NZ, 32, 128), F32),
    f_own=pltpu.VMEM((16, 128), F32),
    f_core=pltpu.VMEM((16, 128), F32),
    f_x=pltpu.VMEM((NX, 16, 128), F32),
    f_all=pltpu.VMEM((NC, NY, NZ, 8, 128), F32),
    f_out=pltpu.VMEM((NZ, 4, 8, C), F32),
    n_ys=pltpu.SemaphoreType.DMA((2,)),
    n_zs=pltpu.SemaphoreType.DMA((2,)),
    f_cs=pltpu.SemaphoreType.DMA((2,)),
    f_xs=pltpu.SemaphoreType.DMA((2,)),
    f_zs=pltpu.SemaphoreType.DMA((2,)),
    f_ys=pltpu.SemaphoreType.DMA((2,)),
    f_gs=pltpu.SemaphoreType.DMA((2,)),
)


def late_scratch(p, r):
    f = lambda *shape: pltpu.VMEM(shape + (r, C), F32)
    d = lambda *shape: pltpu.SemaphoreType.DMA((2,) + shape)
    names = dict(
        all=f(32), half=f(KXY), xy=f(KXY - 1), z=f(NZ), fin=f(32),
        cs=d(), xys=d(), zs=d(), gs=d(), cgs=d(),
    )
    return {"l%d_%s" % (p, n): spec for n, spec in names.items()}


for p, rows in enumerate(LATE):
    SCRATCH.update(late_scratch(p, rows))
for p, rows in enumerate(PARTS):
    SCRATCH.update(early_scratch(p, *rows))


class Names:
    pass


class Axis:
    def __init__(self, n, me, dev):
        self.n, self.me, self.dev = n, me, dev

    def to(self, i):
        return lax.rem(self.me + i + 1, self.n)

    def frm(self, i):
        return lax.rem(self.me + self.n - 1 - i, self.n)


class Early:
    def __init__(self, s, p, rows, place, scale):
        for name in early_scratch(0, 1, 1):
            setattr(self, name[3:], getattr(s, "e%d_%s" % (p, name[3:])))
        self.ru, self.rv = rows
        self.out = self.rv > 16
        self.scale = scale
        x, c, z, y = place
        self.x, self.c, self.pz, self.y = x, c, z, y
        self.ax = Axis(NX, x, lambda t: (t * NC + c, z * NY + y))
        self.ay = Axis(NY, y, lambda t: (x * NC + c, z * NY + t))
        self.az = Axis(NZ, z, lambda t: (x * NC + c, t * NY + y))
        self.other = (x * NC + (1 - c), z * NY + y)
        self.first = ((self.ax, self.u, self.uc, self.ux, self.u1, self.us, self.uxs),
                      (self.ay, self.v, self.vc, self.vy, self.v1, self.vs, self.vys))
        self.second = ((self.ay, self.u1, self.uy, self.uys, 0, self.ru),
                       (self.ax, self.v1, self.vx, self.vxs, self.ru, self.rv))
        self.fin2 = ((self.ay, self.uf, 16 * c + 4 * x, self.uygs),
                     (self.ax, self.vf, 16 * c + 4 * y, self.vxgs))
        self.fin1 = ((self.ax, self.uf, self.uxgs, self.ugs), (self.ay, self.vf, self.vygs, self.vgs))
        self.sent = []

    def block(self, c, t):
        return pl.ds(16 * c + 4 * t, 4)

    def core_start(self):
        for o in (0, 1, 2, 3):
            for ax, full, half, _, _, sem, _ in self.first:
                self.core_copy(ax, full, half, sem, o).start()

    def core_copy(self, ax, full, half, sem, o):
        t = lax.rem(ax.me + 1 + o, 4)
        return remote(
            full.at[self.block(1 - self.c, t)], half.at[pl.ds(4 * t, 4)], sem.at[0, o], sem.at[1, o],
            self.other,
        )

    def st1_copy(self, ax, half, slots, sem, i):
        t = ax.to(i)
        return remote(half.at[pl.ds(4 * t, 4)], slots.at[i], sem.at[0], sem.at[1], ax.dev(t))

    def st1_start(self):
        for o in (0, 1, 2, 3):
            for ax, full, half, slots, _, sem, sem1 in self.first:
                self.core_copy(ax, full, half, sem, o).wait_recv()
                t = lax.rem(ax.me + 1 + o, 4)
                mine = pl.ds(4 * t, 4)
                half[mine] = half[mine] + full[self.block(self.c, t)]
                if o < 3:
                    self.st1_copy(ax, half, slots, sem1, o).start()

    def st2_copy(self, ax, src, slots, sem, i):
        t = ax.to(i)
        return remote(src.at[t], slots.at[i], sem.at[0], sem.at[1], ax.dev(t))

    def st2_start(self):
        for (ax, _, half, slots, one, _, sem1), (ax2, src, slots2, sem2, _, _) in zip(
            self.first, self.second
        ):
            whole(slots, sem1, 3, self.other).wait_recv()
            one[...] = half[pl.ds(4 * ax.me, 4)] + slots[0] + slots[1] + slots[2]
            for i in range(3):
                self.st2_copy(ax2, src, slots2, sem2, i).start()

    def tile(self, t):
        return (
            pl.ds(pl.multiple_of(8 * (t // 2), 8), 8),
            pl.ds(pl.multiple_of(128 * (t % 2), 128), 128),
        )

    def z_copy(self, i):
        t = self.az.to(i)
        rows, lanes = self.tile(t)
        return remote(
            self.part.at[rows, lanes], self.z.at[self.pz], self.zs.at[0], self.zs.at[1],
            self.az.dev(t),
        )

    def zo_copy(self, i):
        t = self.az.to(i)
        return remote(
            self.part.at[pl.ds(32, 8)], self.zo.at[self.pz], self.zos.at[0], self.zos.at[1],
            self.az.dev(t),
        )

    def z_start(self):
        for ax, src, slots, sem, at, n in self.second:
            whole(slots, sem, 3, self.other).wait_recv()
            self.part[at : at + n, :] = src[ax.me] + slots[0] + slots[1] + slots[2]
        each(7, lambda i: self.z_copy(i).start())
        rows, lanes = self.tile(self.pz)
        self.z[self.pz] = self.part[rows, lanes]
        if self.out:
            each(7, lambda i: self.zo_copy(i).start())
            self.zo[self.pz] = self.part[32:40, :]

    def zg_copy(self, i):
        piece = self.zf.at[self.tile(self.pz)]
        return remote(
            piece, piece, self.zgs.at[0], self.zgs.at[1], self.az.dev(self.az.to(i))
        )

    def zg_start(self):
        whole(self.z, self.zs, 7, self.other).wait_recv()
        total = self.z[0]
        for i in range(1, NZ):
            total = total + self.z[i]
        self.zf[self.tile(self.pz)] = total * self.scale
        each(7, lambda i: self.zg_copy(i).start())

    def fin2_copy(self, ax, fin, base, sem, i):
        piece = fin.at[base + ax.me]
        return remote(piece, piece, sem.at[0], sem.at[1], ax.dev(ax.to(i)))

    def st2g_start(self):
        own_u = 16 * self.c + 4 * self.x + self.y
        own_v = 16 * self.c + 4 * self.y + self.x
        if self.out:
            whole(self.zo, self.zos, 7, self.other).wait_recv()
            total = self.zo[0]
            for i in range(1, NZ):
                total = total + self.zo[i]
            self.vf[own_v, 16:24, :] = total * self.scale
        whole(self.z, self.zgs, 7, self.other).wait_recv()
        self.uf[own_u] = self.zf[0:16, :]
        self.vf[own_v, 0:16, :] = self.zf[16:32, :]
        for ax, fin, base, sem in self.fin2:
            for i in range(3):
                self.fin2_copy(ax, fin, base, sem, i).start()

    def fin1_copy(self, ax, fin, sem, i):
        piece = fin.at[self.block(self.c, ax.me)]
        return remote(piece, piece, sem.at[0, i], sem.at[1, i], ax.dev(ax.to(i)))

    def fin1_got(self, ax, fin, sem, i):
        f = ax.frm(i)
        piece = fin.at[self.block(self.c, f)]
        return remote(piece, piece, sem.at[0, i], sem.at[1, i], ax.dev(f))

    def coreg_copy(self, ax, fin, sem, o):
        piece = fin.at[self.block(self.c, lax.rem(ax.me + NX - o, 4))]
        return remote(piece, piece, sem.at[0, o], sem.at[1, o], self.other)

    def coreg_got(self, ax, fin, sem, o):
        piece = fin.at[self.block(1 - self.c, lax.rem(ax.me + NX - o, 4))]
        return remote(piece, piece, sem.at[0, o], sem.at[1, o], self.other)

    def st1g_start(self):
        for (ax2, fin, base, sem2), (ax, _, sem1, semc) in zip(self.fin2, self.fin1):
            whole(fin, sem2, 3, self.other).wait_recv()
            for i in range(3):
                self.fin1_copy(ax, fin, sem1, i).start()
            self.coreg_copy(ax, fin, semc, 0).start()

    def coreg_start(self):
        for i in (0, 2, 1):
            for ax, fin, sem1, semc in self.fin1:
                self.fin1_got(ax, fin, sem1, i).wait_recv()
                self.coreg_copy(ax, fin, semc, i + 1).start()

    def coreg_wait(self):
        for ax, fin, _, semc in self.fin1:
            for o in range(4):
                self.coreg_got(ax, fin, semc, o).wait_recv()

    def drain_sums(self):
        for (ax, full, half, slots, _, sem, sem1), (_, _, slots2, sem2, _, _) in zip(
            self.first, self.second
        ):
            for o in range(4):
                self.core_copy(ax, full, half, sem, o).wait_send()
            whole(slots, sem1, 3, self.other).wait_send()
            whole(slots2, sem2, 3, self.other).wait_send()

    def drain(self):
        whole(self.z, self.zs, 7, self.other).wait_send()
        whole(self.z, self.zgs, 7, self.other).wait_send()
        if self.out:
            whole(self.zo, self.zos, 7, self.other).wait_send()
        for (_, fin, _, sem2), (ax, _, sem1, semc) in zip(self.fin2, self.fin1):
            whole(fin, sem2, 3, self.other).wait_send()
            for i in range(3):
                self.fin1_copy(ax, fin, sem1, i).wait_send()
            for o in range(4):
                self.coreg_copy(ax, fin, semc, o).wait_send()


class Late:
    def __init__(self, s, p, place, scale):
        for name in late_scratch(0, 1):
            setattr(self, name[3:], getattr(s, "l%d_%s" % (p, name[3:])))
        self.scale = scale
        x, c, z, y = place
        self.x, self.c, self.pz, self.y = x, c, z, y
        self.k = x * NY + y
        self.own = c * KXY + self.k
        self.az = Axis(NZ, z, lambda t: (x * NC + c, t * NY + y))
        self.other = (x * NC + (1 - c), z * NY + y)

    def dev(self, xx, yy):
        return (xx * NC + self.c, self.pz * NY + yy)

    def to(self, i):
        j = i + 1
        return lax.rem(self.x + j // NY, NX), lax.rem(self.y + j % NY, NY)

    def core_copy(self):
        theirs = pl.ds((1 - self.c) * KXY, KXY)
        return remote(self.all.at[theirs], self.half, self.cs.at[0], self.cs.at[1], self.other)

    def core_start(self):
        self.core_copy().start()

    def xy_copy(self, i):
        xx, yy = self.to(i)
        return remote(
            self.half.at[xx * NY + yy], self.xy.at[i], self.xys.at[0], self.xys.at[1],
            self.dev(xx, yy),
        )

    def xy_start(self):
        self.core_copy().wait_recv()
        self.half[...] = self.half[...] + self.all[pl.ds(self.c * KXY, KXY)]
        each(KXY - 1, lambda i: self.xy_copy(i).start())

    def z_copy(self, i):
        piece = self.z.at[self.pz]
        return remote(
            piece, piece, self.zs.at[0], self.zs.at[1], self.az.dev(self.az.to(i))
        )

    def z_start(self):
        whole(self.xy, self.xys, KXY - 1, self.other).wait_recv()
        part = self.half[self.k]
        for i in range(KXY - 1):
            part = part + self.xy[i]
        self.z[self.pz] = part
        each(NZ - 1, lambda i: self.z_copy(i).start())

    def g_copy(self, i):
        piece = self.fin.at[self.own]
        return remote(piece, piece, self.gs.at[0], self.gs.at[1], self.dev(*self.to(i)))

    def g_start(self):
        whole(self.z, self.zs, NZ - 1, self.other).wait_recv()
        total = self.z[0]
        for i in range(1, NZ):
            total = total + self.z[i]
        self.fin[self.own] = total * self.scale
        each(KXY - 1, lambda i: self.g_copy(i).start())

    def c_copy(self, c):
        mine = self.fin.at[pl.ds(c * KXY, KXY)]
        return remote(mine, mine, self.cgs.at[0], self.cgs.at[1], self.other)

    def c_start(self):
        whole(self.fin, self.gs, KXY - 1, self.other).wait_recv()
        self.c_copy(self.c).start()

    def wait(self):
        self.c_copy(1 - self.c).wait_recv()

    def drain_sums(self):
        self.core_copy().wait_send()
        whole(self.xy, self.xys, KXY - 1, self.other).wait_send()

    def drain(self):
        whole(self.z, self.zs, NZ - 1, self.other).wait_send()
        whole(self.fin, self.gs, KXY - 1, self.other).wait_send()
        self.c_copy(self.c).wait_send()


def kernel(scale, *refs):
    ins, rest = refs[:10], refs[10:]
    (o_upd, o_pg, o_feat, o_proj, o_slice, o_tok, o_out, o_up, o_down) = rest[:9]
    s = Names()
    for name, ref in zip(SCRATCH, rest[9:]):
        setattr(s, name, ref)

    dp, pt = lax.axis_index("dp"), lax.axis_index("point")
    x, c = dp // NC, dp % NC
    z, y = pt // NY, pt % NY
    k = x * NY + y
    own = c * KXY + k
    other = (x * NC + (1 - c), pt)

    def at_y(i):
        return lax.rem(y + i + 1, NY)

    def from_y(i):
        return lax.rem(y + NY - 1 - i, NY)

    def at_z(i):
        return lax.rem(z + i + 1, NZ)

    def from_z(i):
        return lax.rem(z + NZ - 1 - i, NZ)

    def at_xy(i):
        j = i + 1
        return lax.rem(x + j // NY, NX), lax.rem(y + j % NY, NY)

    def from_xy(i):
        j = i + 1
        return lax.rem(x + NX - j // NY, NX), lax.rem(y + NY - j % NY, NY)

    def at_x(i):
        return lax.rem(x + i + 1, NX)

    def from_x(i):
        return lax.rem(x + NX - 1 - i, NX)

    def dev_x(xx):
        return (xx * NC + c, pt)

    def dev_y(yy):
        return (dp, z * NY + yy)

    def dev_z(zz):
        return (dp, zz * NY + y)

    def dev_xy(xx, yy):
        return (xx * NC + c, z * NY + yy)

    in_dst = (s.mp, s.ls, s.wa, s.wp, s.ws, s.wt, s.wc, s.we, s.wd)
    loads = [pltpu.make_async_copy(a, b, s.in_sem.at[i]) for i, (a, b) in enumerate(zip(ins, in_dst))]
    order = (0, 2, 3, 4, 5, 1, 6, 7, 8)
    for i in order:
        loads[i].start()
    barrier = pltpu.get_barrier_semaphore()
    pl.semaphore_signal(barrier, inc=1, device_id=other, device_id_type=MESH)
    each(
        KXY - 1,
        lambda i: pl.semaphore_signal(
            barrier, inc=1, device_id=dev_xy(*at_xy(i)), device_id_type=MESH
        ),
    )
    each(
        NZ - 1,
        lambda i: pl.semaphore_signal(barrier, inc=1, device_id=dev_z(at_z(i)), device_id_type=MESH),
    )

    sharp_ref = ins[9]

    lane = lax.broadcasted_iota(jnp.int32, (1, 512), 1)
    sharp = jnp.full((1, 512), sharp_ref[0], F32)
    for h in range(1, HEADS):
        sharp = jnp.where(lane // SL == h, sharp_ref[h], sharp)
    inv_sharp = 1.0 / sharp
    rr = lax.broadcasted_iota(jnp.int32, (256, 256), 0)
    cc = lax.broadcasted_iota(jnp.int32, (256, 256), 1)
    s.ones[...] = jnp.where(rr // SL == cc // SL, 1.0, 0.0).astype(BF16)
    s.bdm[...] = jnp.zeros_like(s.bdm)
    s.bdg[...] = jnp.zeros_like(s.bdg)
    low = lax.broadcasted_iota(jnp.int32, (HD, 128), 1) < SL

    def pack_diag(t):
        return jnp.where(low, t[:HD], t[HD:])

    def spread_diag(v):
        return jnp.concatenate([jnp.where(low, v, 0.0), jnp.where(low, 0.0, v)], axis=0).astype(BF16)

    loads[4].wait()
    w1 = s.ws[...].astype(F32)
    w2 = jnp.concatenate([w1, w1], axis=1)
    s.bdw[...] = jnp.zeros_like(s.bdw)
    for j in range(PAIRS):
        s.bdw[64 * j : 64 * j + 64, 128 * j : 128 * j + 128] = spread_diag(w2)

    for i in (0, 2, 3):
        loads[i].wait()
    mass = jnp.zeros((1, 512), F32)
    for r in range(0, ROWS, CH):
        rows = slice(r, r + CH)
        normed, _ = norm_rows(s.mp[rows, :].astype(F32))
        nh = normed.astype(BF16)
        s.nh[rows, :] = nh
        s.feat[rows, :] = dot(nh, s.wa[...]).astype(BF16)
        proj = dot(nh, s.wp[...]).astype(BF16)
        s.proj[rows, :] = proj
        logits = (
            jnp.concatenate(
                [
                    dot(
                        proj[:, 128 * g : 128 * g + 128],
                        s.bdw[128 * g : 128 * g + 128, 256 * g : 256 * g + 256],
                    )
                    for g in range(2)
                ],
                axis=1,
            )
            * inv_sharp
        )
        e = jnp.exp(logits)
        a = e / seg_sum(e, s.ones[...])
        s.asg[rows, :] = a
        s.ah[rows, :] = a.astype(BF16)
        mass = mass + jnp.sum(a, axis=0, keepdims=True)

    def head_sums(values, out):
        for g in range(2):
            t = tdot(values[:, 128 * g : 128 * g + 128], s.ah[:, 256 * g : 256 * g + 256])
            for j in range(2):
                out[2 * g + j, 0:HD, :] = pack_diag(
                    t[64 * j : 64 * j + 64, 128 * j : 128 * j + 128]
                )

    head_sums(s.feat, s.a_p)
    for j in range(PAIRS):
        s.a_p[j, HD:, :] = mass[:, 128 * j : 128 * j + 128]

    def reduce_pairs(part, buf_y, buf_z, sem_y, sem_z):
        def put_y(i):
            t = at_y(i)
            return remote(part.at[t], buf_y.at[i], sem_y.at[0], sem_y.at[1], dev_y(t))

        def put_z(i):
            return remote(
                buf_z.at[z], buf_z.at[z], sem_z.at[0], sem_z.at[1], dev_z(at_z(i))
            )

        def start():
            each(NY - 1, lambda i: put_y(i).start())

        def middle():
            whole(buf_y, sem_y, NY - 1, other).wait_recv()
            buf_z[z] = part[y] + buf_y[0] + buf_y[1] + buf_y[2]
            each(NZ - 1, lambda i: put_z(i).start())

        def finish():
            whole(buf_z, sem_z, NZ - 1, other).wait_recv()
            total = buf_z[0]
            for i in range(1, NZ):
                total = total + buf_z[i]
            return total

        def drain():
            whole(buf_y, sem_y, NY - 1, other).wait_send()
            whole(buf_z, sem_z, NZ - 1, other).wait_send()

        return start, middle, finish, drain

    def gather_pairs(buf, sem):
        def put(i):
            return remote(buf.at[y], buf.at[y], sem.at[0], sem.at[1], dev_y(at_y(i)))

        def start():
            each(NY - 1, lambda i: put(i).start())

        def wait():
            whole(buf, sem, NY - 1, other).wait_recv()

        def drain():
            whole(buf, sem, NY - 1, other).wait_send()

        return start, wait, drain

    pl.semaphore_wait(barrier, 1 + (KXY - 1) + (NZ - 1))
    a_start, a_middle, a_finish, a_drain = reduce_pairs(s.a_p, s.a_y, s.a_z, s.a_ys, s.a_zs)
    am_start, am_wait, am_drain = gather_pairs(s.a_m, s.a_ms)
    a_start()
    a_middle()

    for g in range(2):
        t = tdot(s.nh[...], s.ah[:, 256 * g : 256 * g + 256])
        for j in range(2):
            s.n_all[2 * g + j] = t[:, 128 * j : 128 * j + 128]

    def n_puty(i):
        t = at_y(i)
        return remote(s.n_all.at[t], s.n_y.at[i], s.n_ys.at[0], s.n_ys.at[1], dev_y(t))

    def n_putz(i):
        t = at_z(i)
        rows = pl.ds(pl.multiple_of(32 * t, 32), 32)
        return remote(s.n_sum.at[rows], s.n_z.at[z], s.n_zs.at[0], s.n_zs.at[1], dev_z(t))

    each(NY - 1, lambda i: n_puty(i).start())
    for i in (5, 1, 6, 7, 8):
        loads[i].wait()
    total = a_finish()

    wt = s.wt[...].astype(F32)
    inv_mass = 1.0 / (total[HD : HD + 1] + EPS)
    tokens = total[:HD] * inv_mass
    qkv = hdot(wt, tokens, (0, 0))
    q, kk, v = qkv[:HD], qkv[HD : 2 * HD], qkv[2 * HD :]
    r2 = lax.broadcasted_iota(jnp.int32, (128, 128), 0) // SL
    c2 = lax.broadcasted_iota(jnp.int32, (128, 128), 1) // SL
    scores = hdot(q, kk, (0, 0)) * HD ** (-0.5)
    expo = jnp.where(r2 == c2, jnp.exp(jnp.where(r2 == c2, scores, 0.0)), 0.0)
    att = expo / jnp.sum(expo, axis=-1, keepdims=True)
    s.a_m[y] = hdot(v, att, (1, 1))
    am_start()
    am_wait()
    for j in range(PAIRS):
        s.bdm[64 * j : 64 * j + 64, 128 * j : 128 * j + 128] = spread_diag(s.a_m[j])

    whole(s.n_y, s.n_ys, NY - 1, other).wait_recv()
    s.n_sum[...] = s.n_all[y] + s.n_y[0] + s.n_y[1] + s.n_y[2]
    each(NZ - 1, lambda i: n_putz(i).start())
    s.n_z[z] = s.n_sum[pl.ds(pl.multiple_of(32 * z, 32), 32), :]

    for r in range(0, ROWS, CH):
        rows = slice(r, r + CH)
        spread = jnp.concatenate(
            [
                dot_t(
                    s.ah[rows, 256 * g : 256 * g + 256],
                    s.bdm[128 * g : 128 * g + 128, 256 * g : 256 * g + 256],
                )
                for g in range(2)
            ],
            axis=1,
        ).astype(BF16)
        s.spread[rows, :] = spread
        res = (s.mp[rows, :].astype(F32) + dot(spread, s.wc[...])).astype(BF16).astype(F32)
        n2, inv2 = norm_rows(res)
        n2h = n2.astype(BF16)
        s.n2h[rows, :] = n2h
        sens = s.ls[rows, :]
        s.res[rows, :] = res.astype(BF16)
        gn2 = jnp.zeros((CH, C), F32)
        for f in range(0, FF, 256):
            hid = dot(n2h, s.we[:, f : f + 256])
            gact = dot_t(sens, s.wd[f : f + 256, :])
            h2 = hid * hid
            u = 0.5 + 0.5 * jnp.tanh(hid * (GELU + GELU * 0.044715 * h2))
            act = hid * u
            slope = u + act * (1.0 - u) * (2.0 * GELU + 6.0 * GELU * 0.044715 * h2)
            acth = act.astype(BF16)
            gh = (gact * slope).astype(BF16)
            s.act[rows, f : f + 256] = acth
            s.gh[rows, f : f + 256] = gh
            gn2 = gn2 + dot_t(gh, s.we[:, f : f + 256])
        gres = sens.astype(F32) + norm_back(n2, inv2, gn2)
        s.gres[rows, :] = gres
        grh = gres.astype(BF16)
        s.grh[rows, :] = grh
        s.gspr[rows, :] = dot_t(grh, s.wc[...]).astype(BF16)

    head_sums(s.gspr, s.b_p)
    b_start, b_middle, b_finish, b_drain = reduce_pairs(s.b_p, s.b_y, s.b_z, s.b_ys, s.b_zs)
    bm_start, bm_wait, bm_drain = gather_pairs(s.b_m, s.b_ms)
    b_start()
    outs = []

    def write(src, dst):
        copy = pltpu.make_async_copy(src, dst, s.out_sem.at[len(outs)])
        copy.start()
        outs.append(copy)


    early = [Early(s, p, PARTS[p], (x, c, z, y), scale) for p in range(len(PARTS))]
    for p, e in enumerate(early):
        for b in range(2):
            f = 256 * (2 * p + b)
            e.u[:, 8 * b : 8 * b + 8, :] = tdot(s.n2h[...], s.gh[:, f : f + 256]).reshape(32, 8, C)
            e.v[16 * b : 16 * b + 16, 0:16, :] = tdot(s.act[:, f : f + 256], s.ls[...]).reshape(
                16, 16, C
            )
        if p == 0:
            e.v[:, 16:24, :] = tdot(s.spread[...], s.grh[...]).reshape(32, 8, C)
        e.core_start()
    early[0].st1_start()
    b_middle()

    for r in range(0, ROWS, CH):
        rows = slice(r, r + CH)
        for g in range(2):
            s.ga[rows, 256 * g : 256 * g + 256] = dot(
                s.gspr[rows, 128 * g : 128 * g + 128],
                s.bdm[128 * g : 128 * g + 128, 256 * g : 256 * g + 256],
            )

    early[1].st1_start()
    s.upd[...] = (s.res[...].astype(F32) + dot(s.act[...], s.wd[...])).astype(BF16)
    write(s.upd, o_upd)

    early[0].st2_start()
    gm = b_finish()
    dv = hdot(gm, att, (1, 0))
    datt = hdot(gm, v, (0, 0))
    dsc = att * (datt - jnp.sum(att * datt, axis=-1, keepdims=True)) * HD ** (-0.5)
    dq = hdot(kk, dsc, (1, 1))
    dk = hdot(q, dsc, (1, 0))
    dqkv = jnp.concatenate([dq, dk, dv], axis=0)
    tokenmap = hdot(tokens, dqkv, (1, 1))
    dtok = hdot(wt, dqkv, (1, 0))
    gsum = dtok * inv_mass
    s.b_m[y, 0:HD, :] = gsum
    s.b_m[y, HD:, :] = -jnp.sum(gsum * tokens, axis=0, keepdims=True)
    bm_start()

    whole(s.n_z, s.n_zs, NZ - 1, other).wait_recv()
    nsum = s.n_z[0]
    for i in range(1, NZ):
        nsum = nsum + s.n_z[i]
    nhi = nsum.astype(BF16)
    nlo = (nsum - nhi.astype(F32)).astype(BF16)
    gsd = spread_diag(gsum)
    fblock = dot_t(nhi, gsd) + dot_t(nlo, gsd)
    s.f_own[...] = jnp.concatenate([fblock[:16], fblock[16:]], axis=1)
    f_core = remote(s.f_own, s.f_core, s.f_cs.at[0], s.f_cs.at[1], other)
    f_core.start()

    def f_putx(i):
        t = lax.rem(x + i + 1, NX)
        piece = s.f_x.at[x]
        return remote(piece, piece, s.f_xs.at[0], s.f_xs.at[1], (t * NC + c, pt))

    def f_x_start():
        f_core.wait_recv()
        s.f_x[x] = s.f_own[...] + s.f_core[...]
        each(NX - 1, lambda i: f_putx(i).start())

    def f_putz(i):
        piece = s.f_all.at[c, y, z]
        return remote(piece, piece, s.f_zs.at[0], s.f_zs.at[1], dev_z(at_z(i)))

    def f_z_start():
        whole(s.f_x, s.f_xs, NX - 1, other).wait_recv()
        half = pl.ds(pl.multiple_of(8 * c, 8), 8)
        total = s.f_x[0, half, :] + s.f_x[1, half, :] + s.f_x[2, half, :] + s.f_x[3, half, :]
        s.f_all[c, y, z] = total * scale
        each(NZ - 1, lambda i: f_putz(i).start())

    def f_puty(i):
        piece = s.f_all.at[c, y]
        return remote(piece, piece, s.f_ys.at[0], s.f_ys.at[1], dev_y(at_y(i)))

    def f_y_start():
        whole(s.f_all.at[0, 0], s.f_zs, NZ - 1, other).wait_recv()
        each(NY - 1, lambda i: f_puty(i).start())

    def f_give(core):
        piece = s.f_all.at[core]
        return remote(piece, piece, s.f_gs.at[0], s.f_gs.at[1], other)

    def f_give_start():
        whole(s.f_all.at[0], s.f_ys, NY - 1, other).wait_recv()
        f_give(c).start()

    def f_finish():
        f_give(1 - c).wait_recv()
        left = lax.broadcasted_iota(jnp.int32, (64, 128), 1) < 64
        for core in range(NC):
            for j in range(2):
                a0 = s.f_all[core, 2 * j].reshape(64, 128)
                a1 = s.f_all[core, 2 * j + 1].reshape(64, 128)
                lo = jnp.where(left, a0, pltpu.roll(a1, 64, 1))
                hi = jnp.where(left, pltpu.roll(a0, 64, 1), a1)
                lanes = slice(128 * j, 128 * j + 128)
                s.f_out[:, core, :, lanes] = lo.reshape(NZ, 8, 128)
                s.f_out[:, 2 + core, :, lanes] = hi.reshape(NZ, 8, 128)

    def f_drain():
        whole(s.n_y, s.n_ys, NY - 1, other).wait_send()
        whole(s.n_z, s.n_zs, NZ - 1, other).wait_send()
        f_core.wait_send()
        whole(s.f_x, s.f_xs, NX - 1, other).wait_send()
        whole(s.f_all.at[0, 0], s.f_zs, NZ - 1, other).wait_send()
        whole(s.f_all.at[0], s.f_ys, NY - 1, other).wait_send()
        f_give(c).wait_send()

    f_x_start()
    bm_wait()
    for j in range(PAIRS):
        s.bdg[64 * j : 64 * j + 64, 128 * j : 128 * j + 128] = spread_diag(s.b_m[j, 0:HD, :])
    gmass = jnp.concatenate([s.b_m[j, HD : HD + 1, :] for j in range(PAIRS)], axis=1)

    late = [Late(s, p, (x, c, z, y), scale) for p in range(len(LATE))]
    second = late[0]
    early[0].z_start()
    ga = s.ga[...] + gmass
    ga = ga + jnp.concatenate(
        [
            dot(
                s.feat[:, 128 * g : 128 * g + 128],
                s.bdg[128 * g : 128 * g + 128, 256 * g : 256 * g + 256],
            )
            for g in range(2)
        ],
        axis=1,
    )
    a = s.asg[...]
    gl = (a * (ga - seg_sum(a * ga, s.ones[...])) * inv_sharp).astype(BF16)
    s.gl[...] = gl
    s.gp[...] = jnp.concatenate(
        [
            dot_t(
                gl[:, 256 * g : 256 * g + 256],
                s.bdw[128 * g : 128 * g + 128, 256 * g : 256 * g + 256],
            )
            for g in range(2)
        ],
        axis=1,
    ).astype(BF16)
    second.all[:, 0:8, :] = tdot(s.nh[...], s.gp[...]).reshape(32, 8, C)
    slices = jnp.zeros((HD, 128), F32)
    for g in range(2):
        t = tdot(s.proj[:, 128 * g : 128 * g + 128], s.gl[:, 256 * g : 256 * g + 256])
        for j in range(2):
            slices = slices + pack_diag(t[64 * j : 64 * j + 64, 128 * j : 128 * j + 128])
    tokenmap = jnp.where(z == 0, tokenmap, jnp.zeros_like(tokenmap))
    small = jnp.concatenate([slices, tokenmap, jnp.zeros((HD, 32), F32)], axis=1)
    for i in range(32):
        second.all[i, 8:9, :] = small[i : i + 1, :]
    second.core_start()
    early[1].st2_start()
    second.xy_start()
    early[1].z_start()
    f_z_start()
    s.gf[...] = jnp.concatenate(
        [
            dot_t(
                s.ah[:, 256 * g : 256 * g + 256],
                s.bdg[128 * g : 128 * g + 128, 256 * g : 256 * g + 256],
            )
            for g in range(2)
        ],
        axis=1,
    ).astype(BF16)

    for r in range(0, ROWS, CH):
        rows = slice(r, r + CH)
        normed, inv = norm_rows(s.mp[rows, :].astype(F32))
        gn = dot_t(s.gf[rows, :], s.wa[...]) + dot_t(s.gp[rows, :], s.wp[...])
        s.pgr[rows, :] = (s.gres[rows, :] + norm_back(normed, inv, gn)).astype(BF16)
    write(s.pgr, o_pg)
    a_drain()
    am_drain()
    b_drain()
    bm_drain()
    for e in early:
        e.drain_sums()

    early[0].zg_start()
    early[1].zg_start()
    f_y_start()
    early[0].st2g_start()
    second.z_start()
    early[1].st2g_start()
    early[0].st1g_start()
    f_give_start()
    second.g_start()
    early[1].st1g_start()
    f_finish()
    write(s.f_out, o_feat)
    f_drain()
    for part in late:
        part.drain_sums()
    early[0].coreg_start()
    second.c_start()
    early[1].coreg_start()
    for part in late:
        part.wait()
    write(second.fin.at[:, pl.ds(0, 8), :], o_proj)
    rows = [second.fin[i, 8:9, :] for i in range(32)]
    small = jnp.concatenate(rows, axis=0)
    s.slc[...] = small[:, 0:SL] + small[:, SL : 2 * SL]
    s.tok[...] = small[:, 128 : 128 + 3 * HD]
    write(s.slc, o_slice)
    write(s.tok, o_tok)
    for p, e in enumerate(early):
        e.coreg_wait()
        for b in range(2):
            write(
                e.uf.at[:, pl.ds(8 * b, 8), :], o_up.at[:, :, pl.ds(256 * (2 * p + b), 256)]
            )
        write(e.vf.at[:, pl.ds(0, 16), :], o_down.at[pl.ds(32 * p, 32)])
        if p == 0:
            write(e.vf.at[:, pl.ds(16, 8), :], o_out)
    for part in late:
        part.drain()
    for e in early:
        e.drain()
    for copy in outs:
        copy.wait()


def store(*refs):
    held, outs, stage, sem = refs[:9], refs[9:18], refs[18:27], refs[27]
    parts = [(7, pl.ds(8 * q, 8)) for q in range(4)]
    parts += [(8, pl.ds(16 * q, 16)) for q in range(4)]
    parts += [(i, pl.ds(0, held[i].shape[0])) for i in (0, 1, 2, 3, 6, 4, 5)]
    loads, stores = [], []
    for n, (i, rows) in enumerate(parts):
        piece = stage[i].at[rows]
        loads.append(pltpu.make_async_copy(held[i].at[rows], piece, sem.at[0, n]))
        stores.append(pltpu.make_async_copy(piece, outs[i].at[rows], sem.at[1, n]))
    for copy in loads:
        copy.start()
    for n in range(len(parts)):
        loads[n].wait()
        stores[n].start()
    for copy in stores:
        copy.wait()


def body(mp, ls, wa, wp, ws, wt, wc, we, wd, sharp):
    scale = (lax.axis_size("dp") * lax.axis_size("point") * ROWS) ** (-0.5)
    hbm = pl.BlockSpec(memory_space=pltpu.HBM)
    results = (
        jax.ShapeDtypeStruct((ROWS, C), BF16),
        jax.ShapeDtypeStruct((ROWS, C), BF16),
        jax.ShapeDtypeStruct((NZ, 4, 8, C), F32),
        jax.ShapeDtypeStruct((32, 8, C), F32),
        jax.ShapeDtypeStruct((HD, SL), F32),
        jax.ShapeDtypeStruct((HD, 3 * HD), F32),
        jax.ShapeDtypeStruct((32, 8, C), F32),
        jax.ShapeDtypeStruct((32, 8, FF), F32),
        jax.ShapeDtypeStruct((64, 16, C), F32),
    )
    held = pl.pallas_call(
        functools.partial(kernel, scale),
        out_shape=results,
        in_specs=[hbm] * 9 + [pl.BlockSpec(memory_space=pltpu.SMEM)],
        out_specs=(hbm,) * 9,
        scratch_shapes=list(SCRATCH.values()),
        compiler_params=pltpu.CompilerParams(
            collective_id=0, has_side_effects=True, vmem_limit_bytes=58 << 20
        ),
        name="layer",
    )(mp[0], ls[0], wa, wp, ws, wt, wc, we, wd, sharp)
    outs = pl.pallas_call(
        store,
        out_shape=results,
        in_specs=[hbm] * 9,
        out_specs=(hbm,) * 9,
        scratch_shapes=[pltpu.VMEM(r.shape, r.dtype) for r in results]
        + [pltpu.SemaphoreType.DMA((2, 15))],
        compiler_params=pltpu.CompilerParams(vmem_limit_bytes=58 << 20),
        name="store",
    )(*held)
    upd, pg, feat, proj, sl, tok, out, up, down = outs
    return (
        upd[None],
        pg[None],
        feat.reshape(C, C),
        proj.reshape(C, C),
        sl,
        tok,
        out.reshape(C, C),
        up.reshape(C, FF),
        down.reshape(FF, C),
    )


def solution(mesh):
    split = P("dp", "point", None)
    return jax.shard_map(
        body,
        mesh=mesh,
        in_specs=(split, split) + (P(),) * 8,
        out_specs=(split, split) + (P(),) * 7,
        check_vma=False,
    )
```
